256 devices in a mesh: gx: 4 (over x), gy: 8 (over y, core), gz: 8 (over z).
Axes of the slice: x: 4, y: 4, z: 8, core: 2. Of those that a mesh axis runs over, the one named last changes fastest.
Arguments:
- coarse_old: float32 [5, 64, 128, 4096], P(None, 'gx', 'gy', 'gz'), as said below
- fine_old: float32 [4096, 5, 4096], P(('gx', 'gy', 'gz'))
- slot_owner: int32 [4, 8, 256], P('gx', 'gy', 'gz'), may hold values from -1 to 31, as said below
- box_corner: int32 [4096, 3], P(('gx', 'gy', 'gz')), may hold values from 0 to 255, as said below
Outputs:
- coarse_new: float32 [5, 64, 128, 4096], P(None, 'gx', 'gy', 'gz')
- fine_new: float32 [4096, 5, 4096], P(('gx', 'gy', 'gz'))
The draws below stay inside these ranges and needn't reach their ends.
Inputs may be any that keep to these rules, and one draw needn't show every extreme that they name: coarse_old and fine_old: density at least 1 and pressure at least 1 in every cell. `slot_owner`: an owner lies in the same gy index as the candidate. At most 2 refined candidates of one device have the same owner, and some device sends exactly 2 to one owner; every device owns exactly 16 fine boxes. `box_corner`: rows of one device are the 16 boxes it owns, each a candidate whose slot_owner names this device, ordered by the device that holds the candidate (gx slowest, then gz) and then by the candidate's coordinates (x slowest).
All inputs are finite; a program needn't handle non-finite values.
Results may differ from the reference program's by a relative error of at most 0.0003.
Values sent between devices are 32-bit elements; how exact they have to be, the bound alone decides.
A program may use at most 256 MiB of HBM per device.

```python
import jax
import jax.numpy as jnp
from jax import lax

BOX = 16
FB_DEV = 16
SX = 1
SY = 1
SZ = 32
SLOTS = 32
PEERS = 32
CAP = 2
NX = 64
NY = 128
NZ = 4096
FINE_BOXES = 4096
N_GX = 4
N_GY = 8
N_GZ = 8
DEVICES = 256


def owner_tables(key):
    slab_keys = jax.random.split(key, N_GY)
    cycle_length = PEERS * CAP

    def one_slab(slab_key):
        key_source, key_owner, key_pick = jax.random.split(slab_key, 3)
        source_order = jax.random.permutation(key_source, PEERS).astype(jnp.int32)
        owner_order = jax.random.permutation(key_owner, PEERS).astype(jnp.int32)
        position = jnp.arange(PEERS, dtype=jnp.int32)
        counts_by_pos = jnp.where(position < PEERS // 4, 2 * FB_DEV, jnp.where(position < PEERS // 2, FB_DEV, FB_DEV // 2)).astype(jnp.int32)
        starts_by_pos = ((jnp.cumsum(counts_by_pos) - counts_by_pos) % cycle_length).astype(jnp.int32)
        counts = jnp.zeros((PEERS,), jnp.int32).at[source_order].set(counts_by_pos)
        starts = jnp.zeros((PEERS,), jnp.int32).at[source_order].set(starts_by_pos)
        shuffles = jax.vmap(lambda sub_key: jax.random.permutation(sub_key, SLOTS))(jax.random.split(key_pick, PEERS))
        places = jnp.argsort(shuffles, axis=1).astype(jnp.int32)
        chosen = places < counts[:, None]
        chosen_int = chosen.astype(jnp.int32)
        within = jnp.cumsum(chosen_int, axis=1).astype(jnp.int32) - chosen_int
        cycle = (starts[:, None] + within) % cycle_length
        owner = jnp.where(chosen, owner_order[cycle // CAP], -1).astype(jnp.int32)
        source_ids = jnp.arange(PEERS, dtype=jnp.int32)[:, None]
        slot_ids = jnp.arange(SLOTS, dtype=jnp.int32)[None, :]
        sort_keys = jnp.where(chosen, owner * (PEERS * SLOTS) + source_ids * SLOTS + slot_ids, PEERS * PEERS * SLOTS).astype(jnp.int32)
        listed = jnp.sort(sort_keys.reshape(-1))[:PEERS * FB_DEV]
        return (owner, listed // SLOTS % PEERS, listed % SLOTS)
    owners, sources, slot_ids = jax.vmap(one_slab)(slab_keys)
    table = owners.reshape(N_GY, N_GX, N_GZ, SX, SY, SZ).transpose(1, 3, 0, 4, 2, 5)
    table = table.reshape(N_GX * SX, N_GY * SY, N_GZ * SZ).astype(jnp.int32)
    slab_index = jnp.arange(N_GY, dtype=jnp.int32)[:, None]
    coord_x = sources // N_GZ * SX + slot_ids // (SY * SZ)
    coord_y = slab_index * SY + slot_ids // SZ % SY
    coord_z = sources % N_GZ * SZ + slot_ids % SZ
    corners = jnp.stack([coord_x, coord_y, coord_z], axis=-1).reshape(N_GY, N_GX, N_GZ, FB_DEV, 3)
    corners = corners.transpose(1, 0, 2, 3, 4).reshape(FINE_BOXES, 3).astype(jnp.int32)
    return (table, corners)


def conserved(density, pressure, velocity, axis_at):
    kinetic = 0.5 * density * (velocity[0] * velocity[0] + velocity[1] * velocity[1] + velocity[2] * velocity[2])
    energy = pressure / 0.4 + kinetic
    pieces = [density, density * velocity[0], density * velocity[1], density * velocity[2], energy]
    return jnp.stack(pieces, axis=axis_at).astype(jnp.float32)


def draw_slot_owner(key, part):
    return owner_tables(key)[0]


def draw_box_corner(key, part):
    return owner_tables(key)[1]


def draw_coarse_old(key, part):
    key = jax.random.fold_in(key, 7)
    keys = jax.random.split(key, 5)
    shape = (NX, NY, NZ)
    position = (jnp.arange(NX, dtype=jnp.float32) / NX)[:, None, None]
    density = 1.0 + jax.random.uniform(keys[0], shape, jnp.float32)
    pressure = (1.0 + jax.random.uniform(keys[1], shape, jnp.float32)) * (1.0 + 8.0 * position)
    velocity = [jax.random.uniform(keys[2 + member], shape, jnp.float32, -0.5, 0.5) for member in range(3)]
    return conserved(density, pressure, velocity, 0)


def draw_fine_old(key, part):
    key = jax.random.fold_in(key, 19)
    keys = jax.random.split(key, 6)
    shape = (FINE_BOXES, BOX * BOX * BOX)
    factor = jnp.exp(jax.random.uniform(keys[5], (FINE_BOXES, 1), jnp.float32, 0.0, 2.1972246))
    density = 1.0 + jax.random.uniform(keys[0], shape, jnp.float32)
    pressure = (1.0 + jax.random.uniform(keys[1], shape, jnp.float32)) * factor
    velocity = [jax.random.uniform(keys[2 + member], shape, jnp.float32, -0.5, 0.5) for member in range(3)]
    return conserved(density, pressure, velocity, 1)


def setup_inputs(seed: int = 0) -> dict:
    key_list = jax.random.split(jax.random.key(seed), 5)
    coarse_old = draw_coarse_old(jax.random.fold_in(key_list[4], 71), 0)
    fine_old = draw_fine_old(jax.random.fold_in(key_list[4], 71), 0)
    slot_owner = draw_slot_owner(jax.random.fold_in(key_list[4], 71), 0)
    box_corner = draw_box_corner(jax.random.fold_in(key_list[4], 71), 0)
    return {"coarse_old": coarse_old, "fine_old": fine_old, "slot_owner": slot_owner, "box_corner": box_corner}


HEAT_RATIO = 1.4
COURANT_NUMBER = 0.15

def flux_speed(fields, direction):
    density = fields[0]
    momenta = [fields[1], fields[2], fields[3]]
    energy = fields[4]
    inverse = 1.0 / density
    velocity = [momenta[0] * inverse, momenta[1] * inverse, momenta[2] * inverse]
    kinetic = 0.5 * (momenta[0] * velocity[0] + momenta[1] * velocity[1] + momenta[2] * velocity[2])
    pressure = (HEAT_RATIO - 1.0) * (energy - kinetic)
    sound_speed = jnp.sqrt(HEAT_RATIO * pressure * inverse)
    normal_vel = velocity[direction]
    pieces = [momenta[direction]]
    for member in range(3):
        moment_flux = momenta[member] * normal_vel
        if member == direction:
            moment_flux = moment_flux + pressure
        pieces.append(moment_flux)
    pieces.append((energy + pressure) * normal_vel)
    return (jnp.stack(pieces), jnp.abs(normal_vel) + sound_speed)

def rusanov(lower_cells, upper_cells, direction):
    flux_lower, speed_lower = flux_speed(lower_cells, direction)
    flux_upper, speed_upper = flux_speed(upper_cells, direction)
    signal = jnp.maximum(speed_lower, speed_upper)
    return 0.5 * (flux_lower + flux_upper) - 0.5 * signal[None] * (upper_cells - lower_cells)

def wave_speed(fields):
    density = fields[0]
    inverse = 1.0 / density
    speed_x = fields[1] * inverse
    speed_y = fields[2] * inverse
    speed_z = fields[3] * inverse
    kinetic = 0.5 * (fields[1] * speed_x + fields[2] * speed_y + fields[3] * speed_z)
    pressure = (HEAT_RATIO - 1.0) * (fields[4] - kinetic)
    sound_speed = jnp.sqrt(HEAT_RATIO * pressure * inverse)
    return jnp.maximum(jnp.maximum(jnp.abs(speed_x), jnp.abs(speed_y)), jnp.abs(speed_z)) + sound_speed

def advance(padded, courant):
    interior = padded[..., 1:-1, 1:-1, 1:-1]
    flux_x = rusanov(padded[..., :-1, 1:-1, 1:-1], padded[..., 1:, 1:-1, 1:-1], 0)
    flux_y = rusanov(padded[..., 1:-1, :-1, 1:-1], padded[..., 1:-1, 1:, 1:-1], 1)
    flux_z = rusanov(padded[..., 1:-1, 1:-1, :-1], padded[..., 1:-1, 1:-1, 1:], 2)
    change = flux_x[..., 1:, :, :] - flux_x[..., :-1, :, :] + (flux_y[..., :, 1:, :] - flux_y[..., :, :-1, :]) + (flux_z[..., 1:] - flux_z[..., :-1])
    return (interior - courant * change, (flux_x, flux_y, flux_z))

def zcut(piece, start_cut, stop_cut):
    length = piece.shape[-1]
    return piece.reshape(piece.shape[:-1] + (length // BOX, BOX))[..., start_cut:stop_cut]

def expand_z(piece, offset, extent_z):
    widths = [(0, 0)] * (piece.ndim - 1) + [(offset, BOX - offset - extent_z)]
    spread = jnp.pad(piece, widths)
    return spread.reshape(spread.shape[:-2] + (spread.shape[-2] * BOX,))

def coarse_faces(coarse):
    core = BOX // 2
    shift = BOX // 4
    size_x, size_y, size_z = (coarse.shape[1], coarse.shape[2], coarse.shape[3])
    blocked = coarse.reshape(5, size_x // BOX, BOX, size_y // BOX, BOX, size_z)
    boundary = []
    for first_cell in (shift - 1, shift + core - 1):
        lower_cells = zcut(blocked[:, :, first_cell, :, shift:shift + core, :], shift, shift + core)
        upper_cells = zcut(blocked[:, :, first_cell + 1, :, shift:shift + core, :], shift, shift + core)
        boundary.append(rusanov(lower_cells, upper_cells, 0).transpose(1, 2, 4, 0, 3, 5))
    for first_cell in (shift - 1, shift + core - 1):
        lower_cells = zcut(blocked[:, :, shift:shift + core, :, first_cell, :], shift, shift + core)
        upper_cells = zcut(blocked[:, :, shift:shift + core, :, first_cell + 1, :], shift, shift + core)
        boundary.append(rusanov(lower_cells, upper_cells, 1).transpose(1, 3, 4, 0, 2, 5))
    for first_cell in (shift - 1, shift + core - 1):
        inner = blocked[:, :, shift:shift + core, :, shift:shift + core, :]
        lower_cells = zcut(inner, first_cell, first_cell + 1)[..., 0]
        upper_cells = zcut(inner, first_cell + 1, first_cell + 2)[..., 0]
        boundary.append(rusanov(lower_cells, upper_cells, 2).transpose(1, 3, 5, 0, 2, 4))
    stacked = jnp.stack(boundary, axis=4)
    return stacked.reshape(stacked.shape[:4] + (6 * core * core,))

def apply_fine(advanced, coarse_flux, register, average, refined, courant):
    core = BOX // 2
    shift = BOX // 4
    size_x, size_y, size_z = (advanced.shape[1], advanced.shape[2], advanced.shape[3])
    blocks_x, blocks_y, blocks_z = (size_x // BOX, size_y // BOX, size_z // BOX)
    blocked = advanced.reshape(5, blocks_x, BOX, blocks_y, BOX, size_z)
    mismatch = jnp.where(refined[:, :, :, None, None], courant * (coarse_flux - register), 0.0)
    mismatch = mismatch.reshape(blocks_x, blocks_y, blocks_z, 5, 6, core, core)
    lower_x = expand_z(mismatch[:, :, :, :, 0].transpose(3, 0, 1, 4, 2, 5), shift, core)
    upper_x = expand_z(mismatch[:, :, :, :, 1].transpose(3, 0, 1, 4, 2, 5), shift, core)
    blocked = blocked.at[:, :, shift - 1, :, shift:shift + core, :].add(lower_x)
    blocked = blocked.at[:, :, shift + core, :, shift:shift + core, :].add(-upper_x)
    lower_y = expand_z(mismatch[:, :, :, :, 2].transpose(3, 0, 4, 1, 2, 5), shift, core)
    upper_y = expand_z(mismatch[:, :, :, :, 3].transpose(3, 0, 4, 1, 2, 5), shift, core)
    blocked = blocked.at[:, :, shift:shift + core, :, shift - 1, :].add(lower_y)
    blocked = blocked.at[:, :, shift:shift + core, :, shift + core, :].add(-upper_y)
    lower_z = expand_z(mismatch[:, :, :, :, 4].transpose(3, 0, 4, 1, 5, 2)[..., None], shift - 1, 1)
    upper_z = expand_z(mismatch[:, :, :, :, 5].transpose(3, 0, 4, 1, 5, 2)[..., None], shift + core, 1)
    region = blocked[:, :, shift:shift + core, :, shift:shift + core, :]
    region = region + lower_z - upper_z
    marks = jnp.broadcast_to(refined.astype(jnp.float32)[None, :, None, :, None, :, None], (1, blocks_x, core, blocks_y, core, blocks_z, core))
    inside = expand_z(marks, shift, core) > 0.5
    filling = expand_z(average.reshape(blocks_x, blocks_y, blocks_z, 5, core, core, core).transpose(3, 0, 4, 1, 5, 2, 6), shift, core)
    region = jnp.where(inside, filling, region)
    blocked = blocked.at[:, :, shift:shift + core, :, shift:shift + core, :].set(region)
    return blocked.reshape(5, size_x, size_y, size_z)

def fine_step(fine_fields, patch_old, patch_new, courant):
    core = BOX // 2
    count = fine_fields.shape[1]
    summed = None
    for substep in range(2):
        if substep == 0:
            coarse_now = patch_old
        else:
            coarse_now = 0.5 * (patch_old + patch_new)
        upsampled = jnp.repeat(jnp.repeat(jnp.repeat(coarse_now, 2, axis=2), 2, axis=3), 2, axis=4)[:, :, 1:BOX + 3, 1:BOX + 3, 1:BOX + 3]
        padded = upsampled.at[:, :, 1:BOX + 1, 1:BOX + 1, 1:BOX + 1].set(fine_fields)
        fine_fields, (flux_x, flux_y, flux_z) = advance(padded, courant)
        boundary = jnp.stack([flux_x[:, :, 0], flux_x[:, :, BOX], flux_y[:, :, :, 0], flux_y[:, :, :, BOX], flux_z[..., 0], flux_z[..., BOX]], axis=2)
        coarse_face = boundary.reshape(5, count, 6, core, 2, core, 2).sum(axis=(4, 6)) * 0.25
        summed = coarse_face if summed is None else summed + coarse_face
    register = 0.5 * summed
    average = fine_fields.reshape(5, count, core, 2, core, 2, core, 2).sum(axis=(3, 5, 7)) * 0.125
    return (fine_fields, register, average)

def pack_results(register, average):
    core = BOX // 2
    count = register.shape[1]
    joined = jnp.concatenate([average.reshape(5, count, core ** 3), register.reshape(5, count, 6 * core * core)], axis=2)
    return joined.transpose(1, 0, 2)

def reference(coarse_old, fine_old, slot_owner, box_corner):
    core = BOX // 2
    shift = BOX // 4
    volume = core ** 3
    packed_len = volume + 6 * core * core
    fine_first = fine_old.reshape(FINE_BOXES, 5, BOX, BOX, BOX).transpose(1, 0, 2, 3, 4)
    fastest = jnp.maximum(jnp.max(wave_speed(coarse_old)), jnp.max(wave_speed(fine_first)))
    courant = COURANT_NUMBER / fastest
    padded = jnp.pad(coarse_old, ((0, 0), (1, 1), (1, 1), (1, 1)), mode='wrap')

    def slab_step(start):
        planes = lax.dynamic_slice(padded, (jnp.int32(0), start, jnp.int32(0), jnp.int32(0)), (5, 10, NY + 2, NZ + 2))
        return advance(planes, courant)[0]
    starts = jnp.arange(NX // 8, dtype=jnp.int32) * 8
    advanced = lax.map(slab_step, starts).transpose(1, 0, 2, 3, 4).reshape(5, NX, NY, NZ)

    def cut_patch(source, corner):
        anchor = (corner * BOX + shift - 1).astype(jnp.int32)
        return lax.dynamic_slice(source, (jnp.int32(0), anchor[0], anchor[1], anchor[2]), (5, core + 2, core + 2, core + 2))

    def box_group(inputs):
        corners, fine_rows = inputs
        patch_old = jax.vmap(lambda corner: cut_patch(coarse_old, corner), out_axes=1)(corners)
        patch_new = jax.vmap(lambda corner: cut_patch(advanced, corner), out_axes=1)(corners)
        fine_now = fine_rows.reshape(FB_DEV, 5, BOX, BOX, BOX).transpose(1, 0, 2, 3, 4)
        fine_next, register, average = fine_step(fine_now, patch_old, patch_new, courant)
        packed = pack_results(register, average)
        return (fine_next.transpose(1, 0, 2, 3, 4).reshape(FB_DEV, 5, BOX ** 3), packed)
    fine_new, packed = lax.map(box_group, (box_corner.reshape(DEVICES, FB_DEV, 3), fine_old.reshape(DEVICES, FB_DEV, 5, BOX ** 3)))
    fine_new = fine_new.reshape(FINE_BOXES, 5, BOX ** 3)
    packed = packed.reshape(FINE_BOXES, 5, packed_len)
    slot_table = jnp.zeros((NX // BOX, NY // BOX, NZ // BOX, 5, packed_len), jnp.float32)
    slot_table = slot_table.at[box_corner[:, 0], box_corner[:, 1], box_corner[:, 2]].set(packed)
    coarse_flux = coarse_faces(coarse_old)
    coarse_new = apply_fine(advanced, coarse_flux, slot_table[..., volume:], slot_table[..., :volume], slot_owner >= 0, courant)
    return (coarse_new, fine_new)
```

```python
import functools

import jax
import jax.numpy as jnp
import numpy as np
from jax import lax
from jax.experimental import pallas as pl
from jax.experimental.pallas import tpu as pltpu
from jax.sharding import PartitionSpec as P

BOX = 16
CORE = 8
SHIFT = 4
HEAT_RATIO = 1.4
COURANT_NUMBER = 0.15
OUT_ROWS = 32
BACK_ROWS = 40
MESH = pl.DeviceIdType.MESH
F32 = jnp.float32
BF16 = jnp.bfloat16
VMEM_LIMIT = 56 * 1024 * 1024


def speeds(u):
    inverse = 1.0 / u[0]
    velocity = [u[1] * inverse, u[2] * inverse, u[3] * inverse]
    kinetic = 0.5 * (u[1] * velocity[0] + u[2] * velocity[1] + u[3] * velocity[2])
    pressure = (HEAT_RATIO - 1.0) * (u[4] - kinetic)
    sound = jnp.sqrt(HEAT_RATIO * pressure * inverse)
    return velocity, pressure, sound


def dirflux(u, prims, d):
    velocity, pressure, sound = prims
    normal = velocity[d]
    flux = [u[1 + d]]
    for m in range(3):
        piece = u[1 + m] * normal
        flux.append(piece + pressure if m == d else piece)
    flux.append((u[4] + pressure) * normal)
    return flux, jnp.abs(normal) + sound


def face(ul, fl, sl, ur, fr, sr):
    half = 0.5 * jnp.maximum(sl, sr)
    return [0.5 * (a + b) - half * (d - c) for a, b, c, d in zip(fl, fr, ul, ur)]


def fastest_of(prims):
    velocity, _, sound = prims
    top = jnp.maximum(jnp.abs(velocity[0]), jnp.abs(velocity[1]))
    return jnp.maximum(top, jnp.abs(velocity[2])) + sound


def fold(top):
    best = None
    for row in range(0, top.shape[0], 8):
        for lane in range(0, top.shape[1], 128):
            tile = top[row : row + 8, lane : lane + 128]
            best = tile if best is None else jnp.maximum(best, tile)
    return best


def split3(x):
    high = x.astype(BF16)
    rest = x - high.astype(F32)
    middle = rest.astype(BF16)
    low = (rest - middle.astype(F32)).astype(BF16)
    return high, middle, low


def put_split(ref, row, count, x):
    for part, piece in enumerate(split3(x)):
        ref[pl.ds(part * count + row, x.shape[0]), :] = piece


def sum_split(product):
    count = product.shape[0] // 3
    return product[:count] + product[count : 2 * count] + product[2 * count :]


def dot_nt(a, b):
    return lax.dot_general(a, b, (((1,), (1,)), ((), ())), preferred_element_type=F32)


def dot_nn(a, b):
    return lax.dot_general(a, b, (((1,), (0,)), ((), ())), preferred_element_type=F32)


def onehot(key_row, rows):
    index = lax.broadcasted_iota(jnp.int32, (rows, key_row.shape[1]), 0)
    return jnp.where(index == key_row, 1.0, 0.0).astype(BF16)


def coarse_kernel(coarse, keys, fine, pay, chgl, hy, hz, finet, top, chgf, pflux, pspeed, cxy, cz, rxy):
    nx, ny, nz = coarse.shape[1:]
    row = lax.broadcasted_iota(jnp.int32, (ny, nz), 0)
    lane = lax.broadcasted_iota(jnp.int32, (ny, nz), 1)
    spot = lane % BOX
    refined = jnp.broadcast_to(keys[2:3, :], (ny, nz)) >= 0
    row_in = (row >= SHIFT) & (row < SHIFT + CORE)
    lane_in = refined & (spot >= SHIFT) & (spot < SHIFT + CORE)

    def mark(mask):
        return jnp.where(mask, 1.0, 0.0)

    at_x = mark(row_in & lane_in)
    at_y_lo = mark(lane_in & ((row == SHIFT) | (row == SHIFT + CORE)))
    at_y_hi = mark(lane_in & ((row == SHIFT - 1) | (row == SHIFT + CORE - 1)))
    at_z_lo = mark(refined & row_in & ((spot == SHIFT) | (spot == SHIFT + CORE)))
    at_z_hi = mark(refined & row_in & ((spot == SHIFT - 1) | (spot == SHIFT + CORE - 1)))
    keep_row = mark(row > 0)
    keep_lane = mark(lane > 0)
    lane_tile = lax.broadcasted_iota(jnp.int32, (ny, 128), 1)

    def plane(x, best):
        before = jnp.maximum(x - 1, 0)
        u = [coarse[f, x] for f in range(5)]
        prims = speeds(u)
        best = jnp.maximum(best, fastest_of(prims))
        for side, edge in ((0, 0), (1, ny - 1)):
            for f in range(5):
                hy[side, f, pl.ds(x, 1), :] = coarse[f, x, edge : edge + 1, :]
        for side, edge in ((0, 0), (1, nz - 1)):
            for f in range(5):
                column = jnp.broadcast_to(u[f][:, edge : edge + 1], (ny, 128))
                hz[side, f] = jnp.where(lane_tile == x, column, hz[side, f])
        x_inside = jnp.where((x >= SHIFT) & (x < SHIFT + CORE), 1.0, 0.0)
        x_face = jnp.where((x == SHIFT) | (x == SHIFT + CORE), 1.0, 0.0)
        flux, speed = dirflux(u, prims, 0)
        lower = face(
            [coarse[f, before] for f in range(5)], [pflux[f] for f in range(5)], pspeed[...], u, flux, speed
        )
        lower = [jnp.where(x > 0, piece, 0.0) for piece in lower]
        for f in range(5):
            pflux[f] = flux[f]
        pspeed[...] = speed
        keep = 1.0 - x_face * at_x
        lower_l = [piece * keep for piece in lower]
        change = [-piece for piece in lower]
        change_l = [-piece for piece in lower_l]
        for d, axis, size, first, at_lo, at_hi in (
            (1, 0, ny, keep_row, at_y_lo, at_y_hi),
            (2, 1, nz, keep_lane, at_z_lo, at_z_hi),
        ):
            flux, speed = dirflux(u, prims, d)
            ru = [pltpu.roll(piece, 1, axis) for piece in u]
            rf = [ru[1 + d]] + [pltpu.roll(piece, 1, axis) for piece in flux[1:]]
            lo = face(ru, rf, pltpu.roll(speed, 1, axis), u, flux, speed)
            keep_lo = 1.0 - x_inside * at_lo
            keep_hi = 1.0 - x_inside * at_hi
            for f in range(5):
                low = lo[f] * first
                high = pltpu.roll(low, size - 1, axis)
                change[f] = change[f] + (high - low)
                change_l[f] = change_l[f] + (high * keep_hi - low * keep_lo)
        for f in range(5):
            chgf[f, x] = change[f]
            chgl[f, x] = change_l[f]
            chgf[f, before] = chgf[f, before] + lower[f]
            chgl[f, before] = chgl[f, before] + lower_l[f]
        return best

    hz[...] = jnp.zeros_like(hz)
    best = fold(lax.fori_loop(0, nx, plane, jnp.zeros((ny, nz), F32)))

    count = 10 * 32
    for g in range(10):
        src, f = (coarse, g) if g < 5 else (chgf, g - 5)
        outer = (SHIFT - 1, SHIFT + CORE)
        inner = range(SHIFT, SHIFT + CORE)
        on_x = [src[f, x, SHIFT : SHIFT + CORE, :] for x in outer]
        on_y = [src[f, x, y : y + 1, :] for y in outer for x in inner]
        put_split(cxy, g * 32, count, jnp.concatenate(on_x + on_y, axis=0))
        on_z = [src[f, x, SHIFT : SHIFT + CORE, :] for x in inner]
        put_split(cz, g * 64, 640, jnp.concatenate(on_z, axis=0))
    rxy[...] = sum_split(dot_nt(cxy[...], onehot(keys[0:1, :], 512)))
    rz = sum_split(dot_nt(cz[...], onehot(keys[1:2, :], 128)))
    left = lax.broadcasted_iota(jnp.int32, (8, 128), 1) < 64
    left64 = lax.broadcasted_iota(jnp.int32, (64, 128), 1) < 64

    def put(line, tile):
        for part in range(8):
            pay[pl.ds(part * 8 * OUT_ROWS + line, 8, stride=OUT_ROWS), :] = tile[part * 8 : part * 8 + 8]

    for g in range(10):
        pieces = []
        for side in range(2):
            for j in range(CORE):
                lanes = slice(j // 2 * 128, j // 2 * 128 + 128)
                a = rxy[g * 32 + side * 8 : g * 32 + side * 8 + 8, lanes]
                b = rxy[g * 32 + 16 + side * 8 : g * 32 + 24 + side * 8, lanes]
                if j % 2 == 0:
                    pieces.append(jnp.where(left, a, pltpu.roll(b, 64, 1)))
                else:
                    pieces.append(jnp.where(left, pltpu.roll(a, 64, 1), b))
        turned = jnp.concatenate(pieces, axis=0).T
        put(g * 3, turned[:64])
        put(g * 3 + 1, turned[64:])
    for pair in range(5):
        turned = rz[pair * 128 : pair * 128 + 128].T
        a, b = turned[:64], turned[64:]
        put(pair * 6 + 2, jnp.where(left64, a, pltpu.roll(b, 64, 1)))
        put(pair * 6 + 5, jnp.where(left64, pltpu.roll(a, 64, 1), b))
    for line in (30, 31):
        put(line, jnp.zeros((64, 128), F32))

    def fine_plane(p, best):
        at = pl.multiple_of(p * 256, 256)
        u = [fine[:, f, pl.ds(at, 256)] for f in range(5)]
        for f in range(5):
            finet[f, :, pl.ds(at, 256)] = u[f]
        return jnp.maximum(best, fastest_of(speeds(u)))

    fine_best = lax.fori_loop(0, BOX, fine_plane, jnp.zeros((16, 256), F32))
    top[...] = jnp.maximum(best, fold(fine_best))


def plane_peer(s, sign):
    count_x, count_z = lax.axis_size("gx"), lax.axis_size("gz")
    x = lax.rem(lax.axis_index("gx") + sign * (s // count_z) + count_x, count_x)
    z = lax.rem(lax.axis_index("gz") + sign * lax.rem(s, count_z) + count_z, count_z)
    return x, z


def exchange_kernel(halos, *refs):
    if halos:
        (pay, coarse, hy, hz, top, arr, gx, gy, gz, gmax, tops, tops2, mine, send, recv, here, hs, hr, ts, tr, us, ur) = refs
    else:
        pay, arr, send, recv, here = refs
    ix, iy, iz = (lax.axis_index(a) for a in ("gx", "gy", "gz"))
    nx, ny, nz = (lax.axis_size(a) for a in ("gx", "gy", "gz"))
    me = ix * nz + iz
    peers = nx * nz
    barrier = pltpu.get_barrier_semaphore()

    @pl.loop(1, peers)
    def _(s):
        x, z = plane_peer(s, 1)
        pl.semaphore_signal(barrier, inc=1, device_id=(x, iy, z), device_id_type=MESH)

    if halos:

        @pl.loop(1, ny)
        def _(s):
            pl.semaphore_signal(
                barrier, inc=1, device_id=(ix, lax.rem(iy + s, ny), iz), device_id_type=MESH
            )

    pl.semaphore_wait(barrier, peers - 1 + (ny - 1 if halos else 0))

    def remote(src, dst, a, b, device):
        return pltpu.make_async_remote_copy(
            src_ref=src, dst_ref=dst, send_sem=a, recv_sem=b, device_id=device, device_id_type=MESH
        )

    def patch(s):
        x, z = plane_peer(s, 1)
        return remote(pay.at[x * nz + z], arr.at[me], send.at[s], recv.at[s], (x, iy, z))

    if halos:

        def first(s):
            return remote(mine.at[0], tops.at[s], ts.at[s], tr.at[s], (ix, lax.rem(iy + s, ny), iz))

        def second(s):
            x, z = plane_peer(s, 1)
            return remote(mine.at[1], tops2.at[s], us.at[s], ur.at[s], (x, iy, z))

        mine[0] = top[...]

        @pl.loop(1, ny)
        def _(s):
            first(s).start()

        up_x, down_x = lax.rem(ix + 1, nx), lax.rem(ix + nx - 1, nx)
        up_y, down_y = lax.rem(iy + 1, ny), lax.rem(iy + ny - 1, ny)
        up_z, down_z = lax.rem(iz + 1, nz), lax.rem(iz + nz - 1, nz)
        sides = [
            remote(coarse.at[:, coarse.shape[1] - 1], gx.at[0], hs.at[0], hr.at[0], (up_x, iy, iz)),
            remote(coarse.at[:, 0], gx.at[1], hs.at[1], hr.at[1], (down_x, iy, iz)),
            remote(hy.at[1], gy.at[0], hs.at[2], hr.at[2], (ix, up_y, iz)),
            remote(hy.at[0], gy.at[1], hs.at[3], hr.at[3], (ix, down_y, iz)),
            remote(hz.at[1], gz.at[0], hs.at[4], hr.at[4], (ix, iy, up_z)),
            remote(hz.at[0], gz.at[1], hs.at[5], hr.at[5], (ix, iy, down_z)),
        ]
        for side in sides:
            side.start()

    @pl.loop(1, peers)
    def _(s):
        patch(s).start()

    own = pltpu.make_async_copy(pay.at[me], arr.at[me], here.at[0])
    own.start()
    if halos:

        @pl.loop(1, ny)
        def _(s):
            first(s).wait()

        best = mine[0]
        for s in range(1, ny):
            best = jnp.maximum(best, tops[s])
        mine[1] = best

        @pl.loop(1, peers)
        def _(s):
            second(s).start()

        @pl.loop(1, peers)
        def _(s):
            second(s).wait()

        for s in range(1, peers):
            best = jnp.maximum(best, tops2[s])
        gmax[...] = best
        for side in sides:
            side.wait()
    own.wait()

    @pl.loop(1, peers)
    def _(s):
        patch(s).wait()


def fine_tables():
    c = np.arange(128)
    side, high, low = c // 64, c // 8 % 8, c % 8
    q, r = np.arange(256) // 16, np.arange(256) % 16
    half_q, half_r = q // 2, r // 2
    edge_q = np.where(q == 0, 0, np.where(q == 15, 1, -1))
    edge_r = np.where(r == 0, 0, np.where(r == 15, 1, -1))

    def both(*conditions):
        return np.logical_and.reduce(np.broadcast_arrays(*conditions))

    up_x = np.concatenate(
        [
            both(side[:, None] == s, low[:, None] == half_q[None], high[:, None] == half_r[None])
            for s in range(2)
        ],
        axis=1,
    )
    up_y = np.concatenate(
        [
            both(low[:, None] == x, side[:, None] == edge_q[None], high[:, None] == half_r[None])
            for x in range(8)
        ],
        axis=1,
    )
    up_z = np.concatenate(
        [
            both(high[:, None] == x, side[:, None] == edge_r[None], low[:, None] == half_q[None])
            for x in range(8)
        ],
        axis=1,
    )
    pool_a = both(half_q[:, None] == low[None], half_r[:, None] == high[None]) * 0.125
    pool_y = both(edge_q[:, None] == side[None], half_r[:, None] == high[None]) * 0.125
    pool_z = both(edge_r[:, None] == side[None], half_q[:, None] == low[None]) * 0.125
    return [jnp.asarray(t.astype(np.float32), BF16) for t in (up_x, up_y, up_z, pool_a, pool_y, pool_z)]


def fine_kernel(
    box_lane, arr, gmax, finet, ux, uy, uz, pa, py, pz, ret, out,
    fu, g, lhs, gy, gz, rx, ry, rz, big, stage, sems,
):
    copies = [
        pltpu.make_async_copy(finet.at[f], fu.at[f, :, pl.ds(256, 4096)], sems.at[f]) for f in range(5)
    ]
    for copy in copies:
        copy.start()
    courant = COURANT_NUMBER / jnp.max(gmax[...])
    for b in range(16):
        at = pl.multiple_of(box_lane[b] * OUT_ROWS, OUT_ROWS)
        g[pl.ds(b, OUT_ROWS, stride=16), :] = arr[pl.ds(at, OUT_ROWS), :]
    rx[...] = jnp.zeros_like(rx)
    ry[...] = jnp.zeros_like(ry)
    rz[...] = jnp.zeros_like(rz)

    def ghost(part, table):
        for f in range(5):
            old = g[pl.ds((f * 3 + part) * 16, 16), :]
            change = g[pl.ds(((5 + f) * 3 + part) * 16, 16), :]
            put_split(lhs, f * 16, 160, old)
            put_split(lhs, 80 + f * 16, 160, 0.5 * (old + (old - courant * change)))
        return sum_split(dot_nn(lhs[...], table[...]))

    gy[...] = ghost(1, uy)
    gz[...] = ghost(2, uz)
    gx = ghost(0, ux)
    lane = lax.broadcasted_iota(jnp.int32, (8, 256), 1)
    q, r = lane // 16, lane % 16
    for copy in copies:
        copy.wait()
    for sub in range(2):
        for f in range(5):
            fu[f, :, 0:256] = gx[sub * 80 + f * 16 : sub * 80 + f * 16 + 16, :256]
            fu[f, :, 17 * 256 :] = gx[sub * 80 + f * 16 : sub * 80 + f * 16 + 16, 256:]

        @pl.loop(0, 2)
        def _(half):
            rows = pl.ds(pl.multiple_of(half * 8, 8), 8)

            def load(p):
                return [fu[f, rows, pl.ds(pl.multiple_of(p * 256, 256), 256)] for f in range(5)]

            ghost_u = load(0)
            gp = speeds(ghost_u)
            gf, gs = dirflux(ghost_u, gp, 0)
            u0 = load(1)
            p0 = speeds(u0)
            f0, s0 = dirflux(u0, p0, 0)
            start = face(ghost_u, gf, gs, u0, f0, s0)
            for f in range(5):
                rx[f, rows, 0:256] = rx[f, rows, 0:256] + start[f]

            def plane(p, carry):
                u, vel, pressure, sound, lower = carry
                prims = (vel, pressure, sound)
                nxt = load(p + 2)
                nprims = speeds(nxt)
                fx, sx = dirflux(u, prims, 0)
                nf, ns = dirflux(nxt, nprims, 0)
                upper = face(u, fx, sx, nxt, nf, ns)
                change = [a - b for a, b in zip(upper, lower)]
                pair = pl.multiple_of(p // 2 * 256, 256)
                for d, ghosts, regs, coordinate, shift in ((1, gy, ry, q, 16), (2, gz, rz, r, 1)):
                    gu = [
                        ghosts[pl.ds(pl.multiple_of(sub * 80 + f * 16 + half * 8, 8), 8), pl.ds(pair, 256)]
                        for f in range(5)
                    ]
                    fc, sc = dirflux(u, prims, d)
                    first, last = coordinate == 0, coordinate == 15
                    ul = [jnp.where(first, a, pltpu.roll(b, shift, 1)) for a, b in zip(gu, u)]
                    fl, sl = dirflux(ul, speeds(ul), d)
                    lo = face(ul, fl, sl, u, fc, sc)
                    uh = [jnp.where(last, a, b) for a, b in zip(gu, u)]
                    fh, sh = dirflux(uh, speeds(uh), d)
                    top = face(u, fc, sc, uh, fh, sh)
                    for f in range(5):
                        hi = jnp.where(last, top[f], pltpu.roll(lo[f], 256 - shift, 1))
                        change[f] = change[f] + (hi - lo[f])
                        edge = jnp.where(first, lo[f], jnp.where(last, hi, 0.0))
                        regs[f, rows, pl.ds(pair, 256)] = regs[f, rows, pl.ds(pair, 256)] + edge
                for f in range(5):
                    fu[f, rows, pl.ds(pl.multiple_of((p + 1) * 256, 256), 256)] = u[f] - courant * change[f]
                return nxt, nprims[0], nprims[1], nprims[2], upper

            final = lax.fori_loop(0, BOX, plane, (u0, p0[0], p0[1], p0[2], start))
            for f in range(5):
                rx[f, rows, 256:512] = rx[f, rows, 256:512] + final[4][f]

    for f in range(5):
        for p in range(16):
            out[:, f, p * 256 : p * 256 + 256] = fu[f, :, (p + 1) * 256 : (p + 2) * 256]
    ret[...] = jnp.zeros_like(ret)
    tile_lane = lax.broadcasted_iota(jnp.int32, (16, 128), 1)
    left = tile_lane < 64

    def put(line, tile):
        for half in range(2):
            stage[pl.ds(half * 8 * BACK_ROWS + line, 8, stride=BACK_ROWS), :] = tile[half * 8 : half * 8 + 8]

    def pooled(pieces, table):
        count = 16 * len(pieces)
        for i, piece in enumerate(pieces):
            put_split(big, i * 16, count, piece)
        return sum_split(dot_nn(big[pl.ds(0, 3 * count), :], table[...]))

    cells = [
        fu[f, :, (2 * x + 1) * 256 : (2 * x + 2) * 256] + fu[f, :, (2 * x + 2) * 256 : (2 * x + 3) * 256]
        for f in range(5)
        for x in range(8)
    ]
    cells += [rx[f, :, s * 256 : s * 256 + 256] for f in range(5) for s in range(2)]
    done = pooled(cells, pa)
    for f in range(5):
        for i in range(4):
            at = (f * 8 + 2 * i) * 16
            put(f * 7 + i, jnp.where(left, done[at : at + 16], done[at + 16 : at + 32]))
        at = (40 + 2 * f) * 16
        put(f * 7 + 4, jnp.where(left, done[at : at + 16], done[at + 16 : at + 32]))
    for line, regs, table, owner in ((5, ry, py, tile_lane % 8), (6, rz, pz, tile_lane // 8 % 8)):
        done = pooled([regs[f, :, x * 256 : x * 256 + 256] for f in range(5) for x in range(8)], table)
        for f in range(5):
            total = done[f * 128 : f * 128 + 16]
            for x in range(1, 8):
                at = (f * 8 + x) * 16
                total = jnp.where(owner == x, done[at : at + 16], total)
            put(f * 7 + line, total)
    for line in range(35, BACK_ROWS):
        put(line, jnp.zeros((16, 128), F32))
    for b in range(16):
        at = pl.multiple_of(box_lane[b] * BACK_ROWS, BACK_ROWS)
        ret[pl.ds(at, BACK_ROWS), :] = stage[b * BACK_ROWS : (b + 1) * BACK_ROWS, :]


def apply_kernel(coarse, chgl, keys, arr, gmax, gx, gy, gz, hy, hz, out, lxy, lz, dxy, dz):
    nx, ny, nz = coarse.shape[1:]
    courant = COURANT_NUMBER / jnp.max(gmax[...])
    left = lax.broadcasted_iota(jnp.int32, (16, 128), 1) < 64
    left64 = lax.broadcasted_iota(jnp.int32, (64, 128), 1) < 64

    def lanes_of(line):
        return jnp.concatenate(
            [arr[pl.ds(part * 8 * BACK_ROWS + line, 8, stride=BACK_ROWS), :] for part in range(8)], axis=0
        )

    flat = [(f, i) for f in range(5) for i in range(6)]
    for first in range(0, 30, 2):
        pair = flat[first : first + 2]
        turned = jnp.concatenate([lanes_of(f * 7 + i) for f, i in pair], axis=0).T
        for second in range(2):
            pieces = []
            for couple in range(4):
                even = jnp.concatenate(
                    [turned[a * 64 + couple * 16 : a * 64 + couple * 16 + 8] for a in range(2)], axis=0
                )
                odd = jnp.concatenate(
                    [turned[a * 64 + couple * 16 + 8 : a * 64 + couple * 16 + 16] for a in range(2)], axis=0
                )
                if second == 0:
                    pieces.append(jnp.where(left, even, pltpu.roll(odd, 64, 1)))
                else:
                    pieces.append(jnp.where(left, pltpu.roll(even, 64, 1), odd))
            put_split(lxy, (first + second) * 16, 480, jnp.concatenate(pieces, axis=1))
    for f in range(5):
        both = jnp.concatenate([lanes_of(f * 7 + 6), lanes_of(f * 7 + 6)], axis=0).T
        put_split(lz, f * 64, 320, jnp.where(left64, both[:64], both[64:]))
    dxy[...] = sum_split(dot_nn(lxy[...], onehot(keys[0:1, :], 512)))
    dz[...] = sum_split(dot_nn(lz[...], onehot(keys[1:2, :], 128)))

    def edge(lower, upper, d):
        fl, sl = dirflux(lower, speeds(lower), d)
        fu, su = dirflux(upper, speeds(upper), d)
        return face(lower, fl, sl, upper, fu, su)

    def take(ref, *index):
        return [ref[index[:1] + (f,) + index[1:]] for f in range(5)]

    spot = lax.broadcasted_iota(jnp.int32, (CORE, nz), 1) % BOX
    refined = jnp.broadcast_to(keys[2:3, :], (CORE, nz)) >= 0
    inside = refined & (spot >= SHIFT) & (spot < SHIFT + CORE)
    z_sign = courant * jnp.where(spot == SHIFT - 1, -1.0, jnp.where(spot == SHIFT + CORE, 1.0, 0.0))
    mid = slice(SHIFT, SHIFT + CORE)
    for f in range(5):
        for x in range(nx):
            out[f, x] = coarse[f, x] - courant * chgl[f, x]
        for side, x, sign in ((0, SHIFT - 1, -1.0), (1, SHIFT + CORE, 1.0)):
            at = (f * 6 + 4) * 16 + side * 8
            out[f, x, mid, :] = out[f, x, mid, :] + (sign * courant) * dxy[at : at + 8, :]
            at = (f * 6 + 5) * 16 + side * 8
            for i in range(CORE):
                y = x
                out[f, SHIFT + i, y : y + 1, :] = (
                    out[f, SHIFT + i, y : y + 1, :] + (sign * courant) * dxy[at + i : at + i + 1, :]
                )
        for i in range(CORE):
            fixed = out[f, SHIFT + i, mid, :] + z_sign * dz[f * 64 + i * 8 : f * 64 + i * 8 + 8, :]
            average = dxy[f * 96 + i * 8 : f * 96 + i * 8 + 8, :]
            out[f, SHIFT + i, mid, :] = jnp.where(inside, average, fixed)

    low = edge([gx[0, f] for f in range(5)], [coarse[f, 0] for f in range(5)], 0)
    high = edge([coarse[f, nx - 1] for f in range(5)], [gx[1, f] for f in range(5)], 0)
    for f in range(5):
        out[f, 0] = out[f, 0] + courant * low[f]
        out[f, nx - 1] = out[f, nx - 1] - courant * high[f]
    low = edge(take(gy, 0), take(hy, 0), 1)
    high = edge(take(hy, 1), take(gy, 1), 1)
    for f in range(5):
        for x in range(nx):
            out[f, x, 0:1, :] = out[f, x, 0:1, :] + courant * low[f][x : x + 1]
            out[f, x, ny - 1 : ny, :] = out[f, x, ny - 1 : ny, :] - courant * high[f][x : x + 1]
    tile = lax.broadcasted_iota(jnp.int32, (ny, 128), 1)
    real = tile < nx

    def cells(ref, side):
        return [jnp.where(real, ref[side, f], 1.0) for f in range(5)]

    low = edge(cells(gz, 0), cells(hz, 0), 2)
    high = edge(cells(hz, 1), cells(gz, 1), 2)
    for f in range(5):
        for x in range(nx):
            add = jnp.broadcast_to(courant * low[f][:, x : x + 1], (ny, 128))
            out[f, x, :, 0:128] = out[f, x, :, 0:128] + jnp.where(tile == 0, add, 0.0)
            add = jnp.broadcast_to(courant * high[f][:, x : x + 1], (ny, 128))
            out[f, x, :, nz - 128 :] = out[f, x, :, nz - 128 :] - jnp.where(tile == 127, add, 0.0)


VMEM = pl.BlockSpec(memory_space=pltpu.VMEM)
SMEM = pl.BlockSpec(memory_space=pltpu.SMEM)
ANY = pl.BlockSpec(memory_space=pl.ANY)


def shape(*dims):
    return jax.ShapeDtypeStruct(dims, F32)


def coarse_call(coarse, keys, fine):
    _, nx, ny, nz = coarse.shape
    return pl.pallas_call(
        coarse_kernel,
        out_shape=[
            shape(64 * OUT_ROWS, 128),
            shape(5, nx, ny, nz),
            shape(2, 5, nx, nz),
            shape(2, 5, ny, 128),
            shape(5, 16, 4096),
            shape(8, 128),
        ],
        in_specs=[VMEM, VMEM, VMEM],
        out_specs=[VMEM] * 6,
        scratch_shapes=[
            pltpu.VMEM((5, nx, ny, nz), F32),
            pltpu.VMEM((5, ny, nz), F32),
            pltpu.VMEM((ny, nz), F32),
            pltpu.VMEM((960, nz), BF16),
            pltpu.VMEM((1920, nz), BF16),
            pltpu.VMEM((320, 512), F32),
        ],
        compiler_params=pltpu.CompilerParams(vmem_limit_bytes=VMEM_LIMIT),
        name="coarse_flux_pack",
    )(coarse, keys, fine)


def exchange_call(pay, halos):
    peers = lax.axis_size("gx") * lax.axis_size("gz")
    count_y = lax.axis_size("gy")
    dma = pltpu.SemaphoreType.DMA
    own = [dma((peers,)), dma((peers,)), dma((1,))]
    if halos is None:
        return pl.pallas_call(
            functools.partial(exchange_kernel, False),
            out_shape=shape(*pay.shape),
            in_specs=[ANY],
            out_specs=ANY,
            scratch_shapes=own,
            compiler_params=pltpu.CompilerParams(
                collective_id=1, has_side_effects=True, vmem_limit_bytes=VMEM_LIMIT
            ),
            name="return_exchange",
        )(pay)
    coarse, hy, hz, top = halos
    return pl.pallas_call(
        functools.partial(exchange_kernel, True),
        out_shape=[
            shape(*pay.shape),
            shape(2, 5, coarse.shape[2], coarse.shape[3]),
            shape(*hy.shape),
            shape(*hz.shape),
            shape(8, 128),
        ],
        in_specs=[ANY, ANY, ANY, ANY, VMEM],
        out_specs=[ANY, ANY, ANY, ANY, VMEM],
        scratch_shapes=[
            pltpu.VMEM((count_y, 8, 128), F32),
            pltpu.VMEM((peers, 8, 128), F32),
            pltpu.VMEM((2, 8, 128), F32),
            *own,
            dma((6,)),
            dma((6,)),
            dma((count_y,)),
            dma((count_y,)),
            dma((peers,)),
            dma((peers,)),
        ],
        compiler_params=pltpu.CompilerParams(
            collective_id=0, has_side_effects=True, vmem_limit_bytes=VMEM_LIMIT
        ),
        name="patch_exchange",
    )(pay, coarse, hy, hz, top)


def fine_call(box_lane, arr, gmax, finet):
    tables = fine_tables()
    return pl.pallas_call(
        fine_kernel,
        out_shape=[shape(64 * BACK_ROWS, 128), shape(16, 5, 4096)],
        in_specs=[SMEM, VMEM, VMEM, ANY] + [VMEM] * 6,
        out_specs=[VMEM, VMEM],
        scratch_shapes=[
            pltpu.VMEM((5, 16, 18 * 256), F32),
            pltpu.VMEM((16 * OUT_ROWS, 128), F32),
            pltpu.VMEM((480, 128), BF16),
            pltpu.VMEM((160, 2048), F32),
            pltpu.VMEM((160, 2048), F32),
            pltpu.VMEM((5, 16, 512), F32),
            pltpu.VMEM((5, 16, 2048), F32),
            pltpu.VMEM((5, 16, 2048), F32),
            pltpu.VMEM((2400, 256), BF16),
            pltpu.VMEM((16 * BACK_ROWS, 128), F32),
            pltpu.SemaphoreType.DMA((5,)),
        ],
        compiler_params=pltpu.CompilerParams(vmem_limit_bytes=VMEM_LIMIT),
        name="fine_boxes",
    )(box_lane, arr, gmax, finet, *tables)


def apply_call(coarse, chgl, keys, arr, gmax, gx, gy, gz, hy, hz):
    nz = coarse.shape[3]
    return pl.pallas_call(
        apply_kernel,
        out_shape=shape(*coarse.shape),
        in_specs=[VMEM] * 10,
        out_specs=VMEM,
        scratch_shapes=[
            pltpu.VMEM((1440, 512), BF16),
            pltpu.VMEM((960, 128), BF16),
            pltpu.VMEM((480, nz), F32),
            pltpu.VMEM((320, nz), F32),
        ],
        compiler_params=pltpu.CompilerParams(vmem_limit_bytes=VMEM_LIMIT),
        name="reflux_apply",
    )(coarse, chgl, keys, arr, gmax, gx, gy, gz, hy, hz)


def tables_of(slot_owner, box_corner, count_gz):
    owners = slot_owner.reshape(-1)
    slots = owners.shape[0]
    index = jnp.arange(slots, dtype=jnp.int32)
    rank = jnp.sum(
        (owners[:, None] == owners[None, :]) & (index[None, :] < index[:, None]), axis=1, dtype=jnp.int32
    )
    slot_lane = jnp.where(owners >= 0, owners * 2 + rank, -1)
    lane_z = jnp.repeat(slot_lane, BOX)
    spot = jnp.arange(slots * BOX, dtype=jnp.int32) % BOX
    on = lane_z >= 0
    inner = on & (spot >= SHIFT) & (spot < SHIFT + CORE)
    outer = on & ((spot == SHIFT - 1) | (spot == SHIFT + CORE))
    key_xy = jnp.where(inner, (spot - SHIFT) * 64 + lane_z, -1)
    key_z = jnp.where(outer, jnp.where(spot < SHIFT, 0, 64) + lane_z, -1)
    keys = jnp.stack([key_xy, key_z, lane_z] + [lane_z] * 5)
    source = box_corner[:, 0] * count_gz + box_corner[:, 2] // slots
    number = jnp.arange(source.shape[0], dtype=jnp.int32)
    place = jnp.sum(
        (source[:, None] == source[None, :]) & (number[None, :] < number[:, None]), axis=1, dtype=jnp.int32
    )
    return keys, source * 2 + place


def local(coarse_old, fine_old, slot_owner, box_corner):
    peers = lax.axis_size("gx") * lax.axis_size("gz")
    keys, box_lane = tables_of(slot_owner, box_corner, lax.axis_size("gz"))
    pay, chgl, hy, hz, finet, top = coarse_call(coarse_old, keys, fine_old)
    arr, gx, gy, gz, gmax = exchange_call(pay.reshape(peers, -1, 128), (coarse_old, hy, hz, top))
    ret, fine_new = fine_call(box_lane, arr.reshape(-1, 128), gmax, finet)
    back = exchange_call(ret.reshape(peers, -1, 128), None)
    coarse_new = apply_call(
        coarse_old, chgl, keys, back.reshape(-1, 128), gmax, gx, gy, gz, hy, hz
    )
    return (coarse_new, fine_new)


def solution(mesh):
    in_specs = (
        P(None, "gx", "gy", "gz"),
        P(("gx", "gy", "gz"), None, None),
        P("gx", "gy", "gz"),
        P(("gx", "gy", "gz"), None),
    )
    out_specs = (P(None, "gx", "gy", "gz"), P(("gx", "gy", "gz"), None, None))
    return jax.shard_map(local, mesh=mesh, in_specs=in_specs, out_specs=out_specs, check_vma=False)
```

```python
import functools

import jax
import jax.numpy as jnp
import numpy as np
from jax import lax
from jax.experimental import pallas as pl
from jax.experimental.pallas import tpu as pltpu
from jax.sharding import PartitionSpec as P

BOX = 16
CORE = 8
SHIFT = 4
HEAT_RATIO = 1.4
COURANT_NUMBER = 0.15
OUT_ROWS = 16
BACK_ROWS = 36
STAGE_ROWS = 40
MESH = pl.DeviceIdType.MESH
F32 = jnp.float32
BF16 = jnp.bfloat16
VMEM_LIMIT = 56 * 1024 * 1024


def speeds(u):
    inverse = 1.0 / u[0]
    velocity = [u[1] * inverse, u[2] * inverse, u[3] * inverse]
    kinetic = 0.5 * (u[1] * velocity[0] + u[2] * velocity[1] + u[3] * velocity[2])
    pressure = (HEAT_RATIO - 1.0) * (u[4] - kinetic)
    sound = jnp.sqrt(HEAT_RATIO * pressure * inverse)
    return velocity, pressure, sound


def dirflux(u, prims, d):
    velocity, pressure, sound = prims
    normal = velocity[d]
    flux = [u[1 + d]]
    for m in range(3):
        piece = u[1 + m] * normal
        flux.append(piece + pressure if m == d else piece)
    flux.append((u[4] + pressure) * normal)
    return flux, jnp.abs(normal) + sound


def face(ul, fl, sl, ur, fr, sr):
    half = 0.5 * jnp.maximum(sl, sr)
    return [0.5 * (a + b) - half * (d - c) for a, b, c, d in zip(fl, fr, ul, ur)]


def fastest_of(prims):
    velocity, _, sound = prims
    top = jnp.maximum(jnp.abs(velocity[0]), jnp.abs(velocity[1]))
    return jnp.maximum(top, jnp.abs(velocity[2])) + sound


def fold(top):
    best = None
    for row in range(0, top.shape[0], 8):
        for lane in range(0, top.shape[1], 128):
            tile = top[row : row + 8, lane : lane + 128]
            best = tile if best is None else jnp.maximum(best, tile)
    return best


def split3(x):
    high = x.astype(BF16)
    rest = x - high.astype(F32)
    middle = rest.astype(BF16)
    low = (rest - middle.astype(F32)).astype(BF16)
    return high, middle, low


def put_split(ref, row, count, x):
    for part, piece in enumerate(split3(x)):
        ref[pl.ds(part * count + row, x.shape[0]), :] = piece


def sum_split(product):
    count = product.shape[0] // 3
    return product[:count] + product[count : 2 * count] + product[2 * count :]


def dot_nt(a, b):
    return lax.dot_general(a, b, (((1,), (1,)), ((), ())), preferred_element_type=F32)


def dot_nn(a, b):
    return lax.dot_general(a, b, (((1,), (0,)), ((), ())), preferred_element_type=F32)


def onehot(key_row, rows):
    index = lax.broadcasted_iota(jnp.int32, (rows, key_row.shape[1]), 0)
    return jnp.where(index == key_row, 1.0, 0.0).astype(BF16)


def fine_tables():
    c = np.arange(128)
    side, high, low = c // 64, c // 8 % 8, c % 8
    q, r = np.arange(256) // 16, np.arange(256) % 16
    half_q, half_r = q // 2, r // 2
    edge_q = np.where(q == 0, 0, np.where(q == 15, 1, -1))
    edge_r = np.where(r == 0, 0, np.where(r == 15, 1, -1))

    def both(*conditions):
        return np.logical_and.reduce(np.broadcast_arrays(*conditions))

    up_x = np.concatenate(
        [
            both(side[:, None] == s, low[:, None] == half_q[None], high[:, None] == half_r[None])
            for s in range(2)
        ],
        axis=1,
    )
    up_y = np.concatenate(
        [
            both(low[:, None] == x, side[:, None] == edge_q[None], high[:, None] == half_r[None])
            for x in range(8)
        ],
        axis=1,
    )
    up_z = np.concatenate(
        [
            both(high[:, None] == x, side[:, None] == edge_r[None], low[:, None] == half_q[None])
            for x in range(8)
        ],
        axis=1,
    )
    pool_a = both(half_q[:, None] == low[None], half_r[:, None] == high[None]) * 0.125
    pool_y = both(edge_q[:, None] == side[None], half_r[:, None] == high[None]) * 0.125
    pool_z = both(edge_r[:, None] == side[None], half_q[:, None] == low[None]) * 0.125
    return [jnp.asarray(t.astype(np.float32), BF16) for t in (up_x, up_y, up_z, pool_a, pool_y, pool_z)]


def plane_peer(s, sign):
    count_x, count_z = lax.axis_size("gx"), lax.axis_size("gz")
    x = lax.rem(lax.axis_index("gx") + sign * (s // count_z) + count_x, count_x)
    z = lax.rem(lax.axis_index("gz") + sign * lax.rem(s, count_z) + count_z, count_z)
    return x, z


def remote(src, dst, send, recv, device):
    return pltpu.make_async_remote_copy(
        src_ref=src, dst_ref=dst, send_sem=send, recv_sem=recv, device_id=device, device_id_type=MESH
    )


def lanes_of_peer(peer, rows):
    return pl.ds(pl.multiple_of(peer * 2 * rows, 8), 2 * rows)


def start_patches(pay, arr, rows, send, recv):
    iy = lax.axis_index("gy")
    me = lax.axis_index("gx") * lax.axis_size("gz") + lax.axis_index("gz")

    def patch(s):
        x, z = plane_peer(s, 1)
        peer = x * lax.axis_size("gz") + z
        return remote(
            pay.at[lanes_of_peer(peer, rows), :], arr.at[lanes_of_peer(me, rows), :], send.at[s], recv.at[s], (x, iy, z)
        )

    @pl.loop(1, lax.axis_size("gx") * lax.axis_size("gz"))
    def _(s):
        patch(s).start()

    return patch


def pack(fields, keys_z, exy, pay, cxy, cz, rxy):
    outer = (SHIFT - 1, SHIFT + CORE)
    inner = range(SHIFT, SHIFT + CORE)
    for f in range(5):
        on_x = [fields[f, x, SHIFT : SHIFT + CORE, :] for x in outer]
        on_y = [fields[f, x, y : y + 1, :] for y in outer for x in inner]
        put_split(cxy, f * 32, 160, jnp.concatenate(on_x + on_y, axis=0))
        on_z = [fields[f, x, SHIFT : SHIFT + CORE, :] for x in inner]
        put_split(cz, f * 64, 320, jnp.concatenate(on_z, axis=0))
    rxy[...] = sum_split(dot_nt(cxy[...], exy[...]))
    rz = sum_split(dot_nt(cz[...], onehot(keys_z, 128)))
    left = lax.broadcasted_iota(jnp.int32, (8, 128), 1) < 64
    left64 = lax.broadcasted_iota(jnp.int32, (64, 128), 1) < 64

    def put(line, tile):
        for part in range(8):
            pay[pl.ds(part * 8 * OUT_ROWS + line, 8, stride=OUT_ROWS), :] = tile[part * 8 : part * 8 + 8]

    for f in range(5):
        pieces = []
        for side in range(2):
            for j in range(CORE):
                lanes = slice(j // 2 * 128, j // 2 * 128 + 128)
                a = rxy[f * 32 + side * 8 : f * 32 + side * 8 + 8, lanes]
                b = rxy[f * 32 + 16 + side * 8 : f * 32 + 24 + side * 8, lanes]
                if j % 2 == 0:
                    pieces.append(jnp.where(left, a, pltpu.roll(b, 64, 1)))
                else:
                    pieces.append(jnp.where(left, pltpu.roll(a, 64, 1), b))
        turned = jnp.concatenate(pieces, axis=0).T
        put(f * 3, turned[:64])
        put(f * 3 + 1, turned[64:])
        turned = rz[f * 64 : f * 64 + 64]
        turned = jnp.concatenate([turned, turned], axis=0).T
        put(f * 3 + 2, jnp.where(left64, turned[:64], turned[64:]))


def coarse_changes(coarse, refined_row, chgf, chgl, pflux, pspeed, hy, hz):
    nx, ny, nz = coarse.shape[1:]
    row = lax.broadcasted_iota(jnp.int32, (ny, nz), 0)
    lane = lax.broadcasted_iota(jnp.int32, (ny, nz), 1)
    spot = lane % BOX
    refined = jnp.broadcast_to(refined_row, (ny, nz)) >= 0
    row_in = (row >= SHIFT) & (row < SHIFT + CORE)
    lane_in = refined & (spot >= SHIFT) & (spot < SHIFT + CORE)

    def mark(mask):
        return jnp.where(mask, 1.0, 0.0)

    at_x = mark(row_in & lane_in)
    at_y_lo = mark(lane_in & ((row == SHIFT) | (row == SHIFT + CORE)))
    at_y_hi = mark(lane_in & ((row == SHIFT - 1) | (row == SHIFT + CORE - 1)))
    at_z_lo = mark(refined & row_in & ((spot == SHIFT) | (spot == SHIFT + CORE)))
    at_z_hi = mark(refined & row_in & ((spot == SHIFT - 1) | (spot == SHIFT + CORE - 1)))
    keep_row = mark(row > 0)
    keep_lane = mark(lane > 0)
    lane_tile = lax.broadcasted_iota(jnp.int32, (ny, 128), 1)

    def plane(x, best):
        before = jnp.maximum(x - 1, 0)
        u = [coarse[f, x] for f in range(5)]
        prims = speeds(u)
        best = jnp.maximum(best, fastest_of(prims))
        for side, edge in ((0, 0), (1, ny - 1)):
            for f in range(5):
                hy[side, f, pl.ds(x, 1), :] = coarse[f, x, edge : edge + 1, :]
        for side, edge in ((0, 0), (1, nz - 1)):
            for f in range(5):
                column = jnp.broadcast_to(u[f][:, edge : edge + 1], (ny, 128))
                hz[side, f] = jnp.where(lane_tile == x, column, hz[side, f])
        x_inside = jnp.where((x >= SHIFT) & (x < SHIFT + CORE), 1.0, 0.0)
        x_face = jnp.where((x == SHIFT) | (x == SHIFT + CORE), 1.0, 0.0)
        flux, speed = dirflux(u, prims, 0)
        lower = face(
            [coarse[f, before] for f in range(5)], [pflux[f] for f in range(5)], pspeed[...], u, flux, speed
        )
        lower = [jnp.where(x > 0, piece, 0.0) for piece in lower]
        for f in range(5):
            pflux[f] = flux[f]
        pspeed[...] = speed
        keep = 1.0 - x_face * at_x
        lower_l = [piece * keep for piece in lower]
        change = [-piece for piece in lower]
        change_l = [-piece for piece in lower_l]
        for d, axis, size, first, at_lo, at_hi in (
            (1, 0, ny, keep_row, at_y_lo, at_y_hi),
            (2, 1, nz, keep_lane, at_z_lo, at_z_hi),
        ):
            flux, speed = dirflux(u, prims, d)
            ru = [pltpu.roll(piece, 1, axis) for piece in u]
            rf = [ru[1 + d]] + [pltpu.roll(piece, 1, axis) for piece in flux[1:]]
            lo = face(ru, rf, pltpu.roll(speed, 1, axis), u, flux, speed)
            keep_lo = 1.0 - x_inside * at_lo
            keep_hi = 1.0 - x_inside * at_hi
            for f in range(5):
                low = lo[f] * first
                high = pltpu.roll(low, size - 1, axis)
                change[f] = change[f] + (high - low)
                change_l[f] = change_l[f] + (high * keep_hi - low * keep_lo)
        for f in range(5):
            chgf[f, x] = change[f]
            chgl[f, x] = change_l[f]
            chgf[f, before] = chgf[f, before] + lower[f]
            chgl[f, before] = chgl[f, before] + lower_l[f]
        return best

    hz[...] = jnp.zeros_like(hz)
    pflux[...] = jnp.zeros_like(pflux)
    pspeed[...] = jnp.zeros_like(pspeed)
    return fold(lax.fori_loop(0, nx, plane, jnp.zeros((ny, nz), F32)))


def coarse_base(coarse, chgl, courant, gx, gy, gz, hy, hz):
    nx, ny, nz = coarse.shape[1:]

    @pl.loop(0, nx)
    def _(x):
        for f in range(5):
            chgl[f, x] = coarse[f, x] - courant * chgl[f, x]

    def edge(lower, upper, d):
        fl, sl = dirflux(lower, speeds(lower), d)
        fu, su = dirflux(upper, speeds(upper), d)
        return face(lower, fl, sl, upper, fu, su)

    def take(ref, side):
        return [ref[side, f] for f in range(5)]

    low = edge(take(gx, 0), [coarse[f, 0] for f in range(5)], 0)
    high = edge([coarse[f, nx - 1] for f in range(5)], take(gx, 1), 0)
    for f in range(5):
        chgl[f, 0] = chgl[f, 0] + courant * low[f]
        chgl[f, nx - 1] = chgl[f, nx - 1] - courant * high[f]
    low = edge(take(gy, 0), take(hy, 0), 1)
    high = edge(take(hy, 1), take(gy, 1), 1)
    for f in range(5):
        for x in range(nx):
            chgl[f, x, 0:1, :] = chgl[f, x, 0:1, :] + courant * low[f][x : x + 1]
            chgl[f, x, ny - 1 : ny, :] = chgl[f, x, ny - 1 : ny, :] - courant * high[f][x : x + 1]
    tile = lax.broadcasted_iota(jnp.int32, (ny, 128), 1)

    def cells(ref, side):
        return [jnp.where(tile < nx, ref[side, f], 1.0) for f in range(5)]

    low = edge(cells(gz, 0), cells(hz, 0), 2)
    high = edge(cells(hz, 1), cells(gz, 1), 2)
    for f in range(5):
        for x in range(nx):
            add = jnp.broadcast_to(courant * low[f][:, x : x + 1], (ny, 128))
            chgl[f, x, :, 0:128] = chgl[f, x, :, 0:128] + jnp.where(tile == 0, add, 0.0)
            add = jnp.broadcast_to(courant * high[f][:, x : x + 1], (ny, 128))
            chgl[f, x, :, nz - 128 :] = chgl[f, x, :, nz - 128 :] - jnp.where(tile == 127, add, 0.0)


def fine_steps(courant, g_o, g_c, ux, uy, uz, fu, lhs, ghost_y, ghost_z, rx, ry, rz):
    rx[...] = jnp.zeros_like(rx)
    ry[...] = jnp.zeros_like(ry)
    rz[...] = jnp.zeros_like(rz)

    def ghost(part, table):
        for f in range(5):
            old = g_o[pl.ds((f * 3 + part) * 16, 16), :]
            change = g_c[pl.ds((f * 3 + part) * 16, 16), :]
            put_split(lhs, f * 16, 160, old)
            put_split(lhs, 80 + f * 16, 160, 0.5 * (old + (old - courant * change)))
        return sum_split(dot_nn(lhs[...], table[...]))

    ghost_y[...] = ghost(1, uy)
    ghost_z[...] = ghost(2, uz)
    ghost_x = ghost(0, ux)
    lane = lax.broadcasted_iota(jnp.int32, (8, 256), 1)
    q, r = lane // 16, lane % 16
    for sub in range(2):
        for f in range(5):
            fu[f, :, 0:256] = ghost_x[sub * 80 + f * 16 : sub * 80 + f * 16 + 16, :256]
            fu[f, :, 17 * 256 :] = ghost_x[sub * 80 + f * 16 : sub * 80 + f * 16 + 16, 256:]

        @pl.loop(0, 2)
        def _(half):
            rows = pl.ds(pl.multiple_of(half * 8, 8), 8)

            def load(p):
                return [fu[f, rows, pl.ds(pl.multiple_of(p * 256, 256), 256)] for f in range(5)]

            ghost_u = load(0)
            gp = speeds(ghost_u)
            gf, gs = dirflux(ghost_u, gp, 0)
            u0 = load(1)
            p0 = speeds(u0)
            f0, s0 = dirflux(u0, p0, 0)
            start = face(ghost_u, gf, gs, u0, f0, s0)
            for f in range(5):
                rx[f, rows, 0:256] = rx[f, rows, 0:256] + start[f]

            def plane(p, carry):
                u, vel, pressure, sound, lower = carry
                prims = (vel, pressure, sound)
                nxt = load(p + 2)
                nprims = speeds(nxt)
                fx, sx = dirflux(u, prims, 0)
                nf, ns = dirflux(nxt, nprims, 0)
                upper = face(u, fx, sx, nxt, nf, ns)
                change = [a - b for a, b in zip(upper, lower)]
                pair = pl.multiple_of(p // 2 * 256, 256)
                for d, ghosts, regs, coordinate, shift in ((1, ghost_y, ry, q, 16), (2, ghost_z, rz, r, 1)):
                    gu = [
                        ghosts[pl.ds(pl.multiple_of(sub * 80 + f * 16 + half * 8, 8), 8), pl.ds(pair, 256)]
                        for f in range(5)
                    ]
                    fc, sc = dirflux(u, prims, d)
                    first, last = coordinate == 0, coordinate == 15
                    ul = [jnp.where(first, a, pltpu.roll(b, shift, 1)) for a, b in zip(gu, u)]
                    fl, sl = dirflux(ul, speeds(ul), d)
                    lo = face(ul, fl, sl, u, fc, sc)
                    uh = [jnp.where(last, a, b) for a, b in zip(gu, u)]
                    fh, sh = dirflux(uh, speeds(uh), d)
                    top = face(u, fc, sc, uh, fh, sh)
                    for f in range(5):
                        hi = jnp.where(last, top[f], pltpu.roll(lo[f], 256 - shift, 1))
                        change[f] = change[f] + (hi - lo[f])
                        edge = jnp.where(first, lo[f], jnp.where(last, hi, 0.0))
                        regs[f, rows, pl.ds(pair, 256)] = regs[f, rows, pl.ds(pair, 256)] + edge
                for f in range(5):
                    fu[f, rows, pl.ds(pl.multiple_of((p + 1) * 256, 256), 256)] = u[f] - courant * change[f]
                return nxt, nprims[0], nprims[1], nprims[2], upper

            final = lax.fori_loop(0, BOX, plane, (u0, p0[0], p0[1], p0[2], start))
            for f in range(5):
                rx[f, rows, 256:512] = rx[f, rows, 256:512] + final[4][f]


def fine_results(fu, rx, ry, rz, pa, py, pz, big, stage):
    stage[16 * STAGE_ROWS :, :] = jnp.zeros((STAGE_ROWS, 128), F32)
    tile_lane = lax.broadcasted_iota(jnp.int32, (16, 128), 1)
    left = tile_lane < 64

    def put(line, tile):
        for half in range(2):
            stage[pl.ds(half * 8 * STAGE_ROWS + line, 8, stride=STAGE_ROWS), :] = tile[half * 8 : half * 8 + 8]

    def pooled(pieces, table):
        count = 16 * len(pieces)
        for i, piece in enumerate(pieces):
            put_split(big, i * 16, count, piece)
        return sum_split(dot_nn(big[pl.ds(0, 3 * count), :], table[...]))

    cells = [
        fu[f, :, (2 * x + 1) * 256 : (2 * x + 2) * 256] + fu[f, :, (2 * x + 2) * 256 : (2 * x + 3) * 256]
        for f in range(5)
        for x in range(8)
    ]
    cells += [rx[f, :, s * 256 : s * 256 + 256] for f in range(5) for s in range(2)]
    done = pooled(cells, pa)
    for f in range(5):
        for i in range(4):
            at = (f * 8 + 2 * i) * 16
            put(f * 7 + i, jnp.where(left, done[at : at + 16], done[at + 16 : at + 32]))
        at = (40 + 2 * f) * 16
        put(f * 7 + 4, jnp.where(left, done[at : at + 16], done[at + 16 : at + 32]))
    for line, regs, table, owner in ((5, ry, py, tile_lane % 8), (6, rz, pz, tile_lane // 8 % 8)):
        done = pooled([regs[f, :, x * 256 : x * 256 + 256] for f in range(5) for x in range(8)], table)
        for f in range(5):
            total = done[f * 128 : f * 128 + 16]
            for x in range(1, 8):
                at = (f * 8 + x) * 16
                total = jnp.where(owner == x, done[at : at + 16], total)
            put(f * 7 + line, total)
    for line in range(35, STAGE_ROWS):
        put(line, jnp.zeros((16, 128), F32))


def step_kernel(
    box_lane, lane_box, coarse, keys, fine, ux, uy, uz, pa, py, pz,
    base, fine_new, back, gmax,
    fv, fu, chgf, chgl, pflux, pspeed, exy, cxy, cz, rxy, pay_o, pay_c, arr_o, arr_c,
    hy, hz, gx, gy, gz, tops, mine, g_o, g_c, lhs, ghost_y, ghost_z, rx, ry, rz, big, stage, ret, by_lane, by_box,
    in_sem, out_sem, so, ro, sc, rc, sr, rr, hs, hr, ts, tr,
):
    ix, iy, iz = (lax.axis_index(a) for a in ("gx", "gy", "gz"))
    nx, ny, nz = (lax.axis_size(a) for a in ("gx", "gy", "gz"))
    me = ix * nz + iz
    peers = nx * nz
    load_fine = pltpu.make_async_copy(fine, fv, in_sem.at[0])
    load_fine.start()
    barrier = pltpu.get_barrier_semaphore()

    @pl.loop(1, peers)
    def _(s):
        x, z = plane_peer(s, 1)
        pl.semaphore_signal(barrier, inc=1, device_id=(x, iy, z), device_id_type=MESH)

    @pl.loop(1, ny)
    def _(s):
        pl.semaphore_signal(barrier, inc=1, device_id=(ix, lax.rem(iy + s, ny), iz), device_id_type=MESH)

    exy[...] = onehot(keys[0:1, :], 512)
    pack(coarse, keys[1:2, :], exy, pay_o, cxy, cz, rxy)
    for part in range(8):
        pay_o[pl.ds(part * 8 * OUT_ROWS + 15, 8, stride=OUT_ROWS), :] = jnp.zeros((8, 128), F32)
    pl.semaphore_wait(barrier, peers - 1 + ny - 1)
    old_patch = start_patches(pay_o, arr_o, OUT_ROWS, so, ro)
    arr_o[lanes_of_peer(me, OUT_ROWS), :] = pay_o[lanes_of_peer(me, OUT_ROWS), :]

    best = coarse_changes(coarse, keys[2:3, :], chgf, chgl, pflux, pspeed, hy, hz)
    load_fine.wait()

    def fine_plane(p, best):
        at = pl.multiple_of(p * 256, 256)
        u = [fv[:, f, pl.ds(at, 256)] for f in range(5)]
        for f in range(5):
            fu[f, :, pl.ds(pl.multiple_of(p * 256 + 256, 256), 256)] = u[f]
        return jnp.maximum(best, fastest_of(speeds(u)))

    fine_best = lax.fori_loop(0, BOX, fine_plane, jnp.zeros((16, 256), F32))
    mine[...] = jnp.maximum(best, fold(fine_best))

    def top(s):
        return remote(mine, tops.at[s], ts.at[s], tr.at[s], (ix, lax.rem(iy + s, ny), iz))

    @pl.loop(1, ny)
    def _(s):
        top(s).start()

    pack(chgf, keys[1:2, :], exy, pay_c, cxy, cz, rxy)

    @pl.loop(1, ny)
    def _(s):
        top(s).wait()

    best = mine[...]
    for s in range(1, ny):
        best = jnp.maximum(best, tops[s])
    best = jnp.full((8, 128), jnp.max(best), F32)
    for part in range(8):
        pay_c[pl.ds(part * 8 * OUT_ROWS + 15, 8, stride=OUT_ROWS), :] = best
    new_patch = start_patches(pay_c, arr_c, OUT_ROWS, sc, rc)
    arr_c[lanes_of_peer(me, OUT_ROWS), :] = pay_c[lanes_of_peer(me, OUT_ROWS), :]
    up_x, down_x = lax.rem(ix + 1, nx), lax.rem(ix + nx - 1, nx)
    up_y, down_y = lax.rem(iy + 1, ny), lax.rem(iy + ny - 1, ny)
    up_z, down_z = lax.rem(iz + 1, nz), lax.rem(iz + nz - 1, nz)
    sides = [
        remote(coarse.at[:, coarse.shape[1] - 1], gx.at[0], hs.at[0], hr.at[0], (up_x, iy, iz)),
        remote(coarse.at[:, 0], gx.at[1], hs.at[1], hr.at[1], (down_x, iy, iz)),
        remote(hy.at[1], gy.at[0], hs.at[2], hr.at[2], (ix, up_y, iz)),
        remote(hy.at[0], gy.at[1], hs.at[3], hr.at[3], (ix, down_y, iz)),
        remote(hz.at[1], gz.at[0], hs.at[4], hr.at[4], (ix, iy, up_z)),
        remote(hz.at[0], gz.at[1], hs.at[5], hr.at[5], (ix, iy, down_z)),
    ]
    for side in sides:
        side.start()

    @pl.loop(1, peers)
    def _(s):
        old_patch(s).wait()

    @pl.loop(1, peers)
    def _(s):
        new_patch(s).wait()

    for part in range(8):
        best = jnp.maximum(best, arr_c[pl.ds(part * 8 * OUT_ROWS + 15, 8, stride=OUT_ROWS), :])
    gmax[...] = best
    courant = COURANT_NUMBER / jnp.max(best)
    for arr, g in ((arr_o, g_o), (arr_c, g_c)):
        for lane in range(64):
            by_lane[lane] = arr[lane * OUT_ROWS : (lane + 1) * OUT_ROWS, :]
        for b in range(16):
            g[pl.ds(b, OUT_ROWS, stride=16), :] = by_lane[box_lane[b]]
    fine_steps(courant, g_o, g_c, ux, uy, uz, fu, lhs, ghost_y, ghost_z, rx, ry, rz)
    fine_results(fu, rx, ry, rz, pa, py, pz, big, stage)
    for b in range(17):
        by_box[b] = stage[b * STAGE_ROWS : (b + 1) * STAGE_ROWS, :]
    for lane in range(64):
        ret[lane * BACK_ROWS : (lane + 1) * BACK_ROWS, :] = by_box[lane_box[lane]][:BACK_ROWS]
    back_patch = start_patches(ret, back, BACK_ROWS, sr, rr)
    own = pltpu.make_async_copy(
        ret.at[lanes_of_peer(me, BACK_ROWS), :], back.at[lanes_of_peer(me, BACK_ROWS), :], out_sem.at[0]
    )
    own.start()
    for f in range(5):
        for p in range(16):
            fv[:, f, p * 256 : p * 256 + 256] = fu[f, :, (p + 1) * 256 : (p + 2) * 256]
    store_fine = pltpu.make_async_copy(fv, fine_new, out_sem.at[1])
    store_fine.start()
    for side in sides:
        side.wait()
    coarse_base(coarse, chgl, courant, gx, gy, gz, hy, hz)
    store_base = pltpu.make_async_copy(chgl, base, out_sem.at[2])
    store_base.start()
    own.wait()
    store_fine.wait()
    store_base.wait()

    @pl.loop(1, peers)
    def _(s):
        back_patch(s).wait()


def apply_kernel(base, keys, arr, gmax, out, lxy, lz, dxy, dz):
    nx, _, nz = base.shape[1:]
    courant = COURANT_NUMBER / jnp.max(gmax[...])
    left = lax.broadcasted_iota(jnp.int32, (16, 128), 1) < 64
    left64 = lax.broadcasted_iota(jnp.int32, (64, 128), 1) < 64

    def lanes_of(line):
        return jnp.concatenate(
            [arr[pl.ds(part * 8 * BACK_ROWS + line, 8, stride=BACK_ROWS), :] for part in range(8)], axis=0
        )

    flat = [(f, i) for f in range(5) for i in range(6)]
    for first in range(0, 30, 2):
        pair = flat[first : first + 2]
        turned = jnp.concatenate([lanes_of(f * 7 + i) for f, i in pair], axis=0).T
        for second in range(2):
            pieces = []
            for couple in range(4):
                even = jnp.concatenate(
                    [turned[a * 64 + couple * 16 : a * 64 + couple * 16 + 8] for a in range(2)], axis=0
                )
                odd = jnp.concatenate(
                    [turned[a * 64 + couple * 16 + 8 : a * 64 + couple * 16 + 16] for a in range(2)], axis=0
                )
                if second == 0:
                    pieces.append(jnp.where(left, even, pltpu.roll(odd, 64, 1)))
                else:
                    pieces.append(jnp.where(left, pltpu.roll(even, 64, 1), odd))
            put_split(lxy, (first + second) * 16, 480, jnp.concatenate(pieces, axis=1))
    for f in range(5):
        both = jnp.concatenate([lanes_of(f * 7 + 6), lanes_of(f * 7 + 6)], axis=0).T
        put_split(lz, f * 64, 320, jnp.where(left64, both[:64], both[64:]))
    dxy[...] = sum_split(dot_nn(lxy[...], onehot(keys[0:1, :], 512)))
    dz[...] = sum_split(dot_nn(lz[...], onehot(keys[1:2, :], 128)))

    spot = lax.broadcasted_iota(jnp.int32, (CORE, nz), 1) % BOX
    refined = jnp.broadcast_to(keys[2:3, :], (CORE, nz)) >= 0
    inside = refined & (spot >= SHIFT) & (spot < SHIFT + CORE)
    z_sign = courant * jnp.where(spot == SHIFT - 1, -1.0, jnp.where(spot == SHIFT + CORE, 1.0, 0.0))
    mid = slice(SHIFT, SHIFT + CORE)
    for f in range(5):
        for x in range(nx):
            out[f, x] = base[f, x]
        for side, x, sign in ((0, SHIFT - 1, -1.0), (1, SHIFT + CORE, 1.0)):
            at = (f * 6 + 4) * 16 + side * 8
            out[f, x, mid, :] = out[f, x, mid, :] + (sign * courant) * dxy[at : at + 8, :]
            at = (f * 6 + 5) * 16 + side * 8
            for i in range(CORE):
                y = x
                out[f, SHIFT + i, y : y + 1, :] = (
                    out[f, SHIFT + i, y : y + 1, :] + (sign * courant) * dxy[at + i : at + i + 1, :]
                )
        for i in range(CORE):
            fixed = out[f, SHIFT + i, mid, :] + z_sign * dz[f * 64 + i * 8 : f * 64 + i * 8 + 8, :]
            average = dxy[f * 96 + i * 8 : f * 96 + i * 8 + 8, :]
            out[f, SHIFT + i, mid, :] = jnp.where(inside, average, fixed)


VMEM = pl.BlockSpec(memory_space=pltpu.VMEM)
SMEM = pl.BlockSpec(memory_space=pltpu.SMEM)
ANY = pl.BlockSpec(memory_space=pl.ANY)


def shape(*dims):
    return jax.ShapeDtypeStruct(dims, F32)


def step_call(box_lane, lane_box, coarse, keys, fine):
    peers = lax.axis_size("gx") * lax.axis_size("gz")
    count_y = lax.axis_size("gy")
    _, nx, ny, nz = coarse.shape
    dma = pltpu.SemaphoreType.DMA
    tables = fine_tables()

    def vmem(*dims, dtype=F32):
        return pltpu.VMEM(dims, dtype)

    return pl.pallas_call(
        step_kernel,
        out_shape=[shape(*coarse.shape), shape(*fine.shape), shape(64 * BACK_ROWS, 128), shape(8, 128)],
        in_specs=[SMEM, SMEM, VMEM, VMEM, ANY] + [VMEM] * 6,
        out_specs=[ANY, ANY, ANY, VMEM],
        scratch_shapes=[
            vmem(*fine.shape),
            vmem(5, 16, 18 * 256),
            vmem(5, nx, ny, nz),
            vmem(5, nx, ny, nz),
            vmem(5, ny, nz),
            vmem(ny, nz),
            vmem(512, nz, dtype=BF16),
            vmem(480, nz, dtype=BF16),
            vmem(960, nz, dtype=BF16),
            vmem(160, 512),
            *[vmem(64 * OUT_ROWS, 128)] * 4,
            vmem(2, 5, nx, nz),
            vmem(2, 5, ny, 128),
            vmem(2, 5, ny, nz),
            vmem(2, 5, nx, nz),
            vmem(2, 5, ny, 128),
            vmem(count_y, 8, 128),
            vmem(8, 128),
            vmem(16 * OUT_ROWS, 128),
            vmem(16 * OUT_ROWS, 128),
            vmem(480, 128, dtype=BF16),
            vmem(160, 2048),
            vmem(160, 2048),
            vmem(5, 16, 512),
            vmem(5, 16, 2048),
            vmem(5, 16, 2048),
            vmem(2400, 256, dtype=BF16),
            vmem(17 * STAGE_ROWS, 128),
            vmem(64 * BACK_ROWS, 128),
            vmem(64, OUT_ROWS, 128),
            vmem(17, STAGE_ROWS, 128),
            dma((1,)),
            dma((3,)),
            *[dma((peers,))] * 6,
            dma((6,)),
            dma((6,)),
            dma((count_y,)),
            dma((count_y,)),
        ],
        compiler_params=pltpu.CompilerParams(
            collective_id=0, has_side_effects=True, vmem_limit_bytes=VMEM_LIMIT
        ),
        name="step",
    )(box_lane, lane_box, coarse, keys, fine, *tables)


def apply_call(base, keys, arr, gmax):
    nz = base.shape[3]
    return pl.pallas_call(
        apply_kernel,
        out_shape=shape(*base.shape),
        in_specs=[VMEM] * 4,
        out_specs=VMEM,
        scratch_shapes=[
            pltpu.VMEM((1440, 512), BF16),
            pltpu.VMEM((960, 128), BF16),
            pltpu.VMEM((480, nz), F32),
            pltpu.VMEM((320, nz), F32),
        ],
        compiler_params=pltpu.CompilerParams(vmem_limit_bytes=VMEM_LIMIT),
        name="reflux_apply",
    )(base, keys, arr, gmax)


def tables_of(slot_owner, box_corner, count_gz):
    owners = slot_owner.reshape(-1)
    slots = owners.shape[0]
    index = jnp.arange(slots, dtype=jnp.int32)
    rank = jnp.sum(
        (owners[:, None] == owners[None, :]) & (index[None, :] < index[:, None]), axis=1, dtype=jnp.int32
    )
    slot_lane = jnp.where(owners >= 0, owners * 2 + rank, -1)
    lane_z = jnp.repeat(slot_lane, BOX)
    spot = jnp.arange(slots * BOX, dtype=jnp.int32) % BOX
    on = lane_z >= 0
    inner = on & (spot >= SHIFT) & (spot < SHIFT + CORE)
    outer = on & ((spot == SHIFT - 1) | (spot == SHIFT + CORE))
    key_xy = jnp.where(inner, (spot - SHIFT) * 64 + lane_z, -1)
    key_z = jnp.where(outer, jnp.where(spot < SHIFT, 0, 64) + lane_z, -1)
    keys = jnp.stack([key_xy, key_z, lane_z] + [lane_z] * 5)
    source = box_corner[:, 0] * count_gz + box_corner[:, 2] // slots
    number = jnp.arange(source.shape[0], dtype=jnp.int32)
    place = jnp.sum(
        (source[:, None] == source[None, :]) & (number[None, :] < number[:, None]), axis=1, dtype=jnp.int32
    )
    box_lane = source * 2 + place
    lanes = jnp.arange(64, dtype=jnp.int32)
    lane_box = jnp.min(jnp.where(box_lane[None, :] == lanes[:, None], number[None, :], 16), axis=1)
    return keys, box_lane, lane_box


def local(coarse_old, fine_old, slot_owner, box_corner):
    keys, box_lane, lane_box = tables_of(slot_owner, box_corner, lax.axis_size("gz"))
    base, fine_new, back, gmax = step_call(box_lane, lane_box, coarse_old, keys, fine_old)
    coarse_new = apply_call(base, keys, back, gmax)
    return (coarse_new, fine_new)


def solution(mesh):
    in_specs = (
        P(None, "gx", "gy", "gz"),
        P(("gx", "gy", "gz"), None, None),
        P("gx", "gy", "gz"),
        P(("gx", "gy", "gz"), None),
    )
    out_specs = (P(None, "gx", "gy", "gz"), P(("gx", "gy", "gz"), None, None))
    return jax.shard_map(local, mesh=mesh, in_specs=in_specs, out_specs=out_specs, check_vma=False)
```

```python
import jax
import jax.numpy as jnp
from jax import lax
from jax.experimental import pallas as pl
from jax.experimental.pallas import tpu as pltpu
from jax.sharding import PartitionSpec as P

BOX = 16
CORE = 8
SHIFT = 4
HEAT_RATIO = 1.4
COURANT_NUMBER = 0.15
OUT_ROWS = 16
BACK_ROWS = 36
STAGE_ROWS = 40
MESH = pl.DeviceIdType.MESH
F32 = jnp.float32
BF16 = jnp.bfloat16
VMEM_LIMIT = 56 * 1024 * 1024


def speeds(u):
    inverse = 1.0 / u[0]
    velocity = [u[1] * inverse, u[2] * inverse, u[3] * inverse]
    kinetic = 0.5 * (u[1] * velocity[0] + u[2] * velocity[1] + u[3] * velocity[2])
    pressure = (HEAT_RATIO - 1.0) * (u[4] - kinetic)
    sound = jnp.sqrt(HEAT_RATIO * pressure * inverse)
    return velocity, pressure, sound


def dirflux(u, prims, d):
    velocity, pressure, sound = prims
    normal = velocity[d]
    flux = [u[1 + d]]
    for m in range(3):
        piece = u[1 + m] * normal
        flux.append(piece + pressure if m == d else piece)
    flux.append((u[4] + pressure) * normal)
    return flux, jnp.abs(normal) + sound


def face(ul, fl, sl, ur, fr, sr):
    half = 0.5 * jnp.maximum(sl, sr)
    return [0.5 * (a + b) - half * (d - c) for a, b, c, d in zip(fl, fr, ul, ur)]


def fastest_of(prims):
    velocity, _, sound = prims
    top = jnp.maximum(jnp.abs(velocity[0]), jnp.abs(velocity[1]))
    return jnp.maximum(top, jnp.abs(velocity[2])) + sound


def fold(top):
    best = None
    for row in range(0, top.shape[0], 8):
        for lane in range(0, top.shape[1], 128):
            tile = top[row : row + 8, lane : lane + 128]
            best = tile if best is None else jnp.maximum(best, tile)
    return best


def split3(x):
    high = x.astype(BF16)
    rest = x - high.astype(F32)
    middle = rest.astype(BF16)
    low = (rest - middle.astype(F32)).astype(BF16)
    return high, middle, low


def put_split(ref, row, count, x):
    for part, piece in enumerate(split3(x)):
        ref[pl.ds(part * count + row, x.shape[0]), :] = piece


def sum_split(product):
    count = product.shape[0] // 3
    return product[:count] + product[count : 2 * count] + product[2 * count :]


def dot_nt(a, b):
    return lax.dot_general(a, b, (((1,), (1,)), ((), ())), preferred_element_type=F32)


def dot_nn(a, b):
    return lax.dot_general(a, b, (((1,), (0,)), ((), ())), preferred_element_type=F32)


def onehot(key_row, rows):
    index = lax.broadcasted_iota(jnp.int32, (rows, key_row.shape[1]), 0)
    return jnp.where(index == key_row, 1.0, 0.0).astype(BF16)


def plane_peer(s, sign):
    count_x, count_z = lax.axis_size("gx"), lax.axis_size("gz")
    x = lax.rem(lax.axis_index("gx") + sign * (s // count_z) + count_x, count_x)
    z = lax.rem(lax.axis_index("gz") + sign * lax.rem(s, count_z) + count_z, count_z)
    return x, z


def remote(src, dst, send, recv, device):
    return pltpu.make_async_remote_copy(
        src_ref=src, dst_ref=dst, send_sem=send, recv_sem=recv, device_id=device, device_id_type=MESH
    )


def lanes_of_peer(peer, rows):
    return pl.ds(pl.multiple_of(peer * 2 * rows, 8), 2 * rows)


def start_patches(pay, arr, rows, send, recv):
    iy = lax.axis_index("gy")
    me = lax.axis_index("gx") * lax.axis_size("gz") + lax.axis_index("gz")

    def patch(s):
        x, z = plane_peer(s, 1)
        peer = x * lax.axis_size("gz") + z
        return remote(
            pay.at[lanes_of_peer(peer, rows), :], arr.at[lanes_of_peer(me, rows), :], send.at[s], recv.at[s], (x, iy, z)
        )

    @pl.loop(1, lax.axis_size("gx") * lax.axis_size("gz"))
    def _(s):
        patch(s).start()

    return patch


def pack(fields, keys_z, exy, pay, cxy, cz, rxy):
    outer = (SHIFT - 1, SHIFT + CORE)
    inner = range(SHIFT, SHIFT + CORE)
    for f in range(5):
        on_x = [fields[f, x, SHIFT : SHIFT + CORE, :] for x in outer]
        on_y = [fields[f, x, y : y + 1, :] for y in outer for x in inner]
        put_split(cxy, f * 32, 160, jnp.concatenate(on_x + on_y, axis=0))
        on_z = [fields[f, x, SHIFT : SHIFT + CORE, :] for x in inner]
        put_split(cz, f * 64, 320, jnp.concatenate(on_z, axis=0))
    rxy[...] = sum_split(dot_nt(cxy[...], exy[...]))
    rz = sum_split(dot_nt(cz[...], onehot(keys_z, 128)))
    left = lax.broadcasted_iota(jnp.int32, (8, 128), 1) < 64
    left64 = lax.broadcasted_iota(jnp.int32, (64, 128), 1) < 64

    def put(line, tile):
        for part in range(8):
            pay[pl.ds(part * 8 * OUT_ROWS + line, 8, stride=OUT_ROWS), :] = tile[part * 8 : part * 8 + 8]

    for f in range(5):
        pieces = []
        for side in range(2):
            for j in range(CORE):
                lanes = slice(j // 2 * 128, j // 2 * 128 + 128)
                a = rxy[f * 32 + side * 8 : f * 32 + side * 8 + 8, lanes]
                b = rxy[f * 32 + 16 + side * 8 : f * 32 + 24 + side * 8, lanes]
                if j % 2 == 0:
                    pieces.append(jnp.where(left, a, pltpu.roll(b, 64, 1)))
                else:
                    pieces.append(jnp.where(left, pltpu.roll(a, 64, 1), b))
        turned = jnp.concatenate(pieces, axis=0).T
        put(f * 3, turned[:64])
        put(f * 3 + 1, turned[64:])
        turned = rz[f * 64 : f * 64 + 64]
        turned = jnp.concatenate([turned, turned], axis=0).T
        put(f * 3 + 2, jnp.where(left64, turned[:64], turned[64:]))


def coarse_changes(coarse, refined_row, chgf, chgl, pflux, pspeed, hy, hz):
    nx, ny, nz = coarse.shape[1:]
    row = lax.broadcasted_iota(jnp.int32, (ny, nz), 0)
    lane = lax.broadcasted_iota(jnp.int32, (ny, nz), 1)
    spot = lane % BOX
    refined = jnp.broadcast_to(refined_row, (ny, nz)) >= 0
    row_in = (row >= SHIFT) & (row < SHIFT + CORE)
    lane_in = refined & (spot >= SHIFT) & (spot < SHIFT + CORE)

    def mark(mask):
        return jnp.where(mask, 1.0, 0.0)

    at_x = mark(row_in & lane_in)
    at_y_lo = mark(lane_in & ((row == SHIFT) | (row == SHIFT + CORE)))
    at_y_hi = mark(lane_in & ((row == SHIFT - 1) | (row == SHIFT + CORE - 1)))
    at_z_lo = mark(refined & row_in & ((spot == SHIFT) | (spot == SHIFT + CORE)))
    at_z_hi = mark(refined & row_in & ((spot == SHIFT - 1) | (spot == SHIFT + CORE - 1)))
    keep_row = mark(row > 0)
    keep_lane = mark(lane > 0)
    lane_tile = lax.broadcasted_iota(jnp.int32, (ny, 128), 1)

    def plane(x, best):
        before = jnp.maximum(x - 1, 0)
        u = [coarse[f, x] for f in range(5)]
        prims = speeds(u)
        best = jnp.maximum(best, fastest_of(prims))
        for side, edge in ((0, 0), (1, ny - 1)):
            for f in range(5):
                hy[side, f, pl.ds(x, 1), :] = coarse[f, x, edge : edge + 1, :]
        for side, edge in ((0, 0), (1, nz - 1)):
            for f in range(5):
                column = jnp.broadcast_to(u[f][:, edge : edge + 1], (ny, 128))
                hz[side, f] = jnp.where(lane_tile == x, column, hz[side, f])
        x_inside = jnp.where((x >= SHIFT) & (x < SHIFT + CORE), 1.0, 0.0)
        x_face = jnp.where((x == SHIFT) | (x == SHIFT + CORE), 1.0, 0.0)
        flux, speed = dirflux(u, prims, 0)
        lower = face(
            [coarse[f, before] for f in range(5)], [pflux[f] for f in range(5)], pspeed[...], u, flux, speed
        )
        lower = [jnp.where(x > 0, piece, 0.0) for piece in lower]
        for f in range(5):
            pflux[f] = flux[f]
        pspeed[...] = speed
        keep = 1.0 - x_face * at_x
        lower_l = [piece * keep for piece in lower]
        change = [-piece for piece in lower]
        change_l = [-piece for piece in lower_l]
        for d, axis, size, first, at_lo, at_hi in (
            (1, 0, ny, keep_row, at_y_lo, at_y_hi),
            (2, 1, nz, keep_lane, at_z_lo, at_z_hi),
        ):
            flux, speed = dirflux(u, prims, d)
            ru = [pltpu.roll(piece, 1, axis) for piece in u]
            rf = [ru[1 + d]] + [pltpu.roll(piece, 1, axis) for piece in flux[1:]]
            lo = face(ru, rf, pltpu.roll(speed, 1, axis), u, flux, speed)
            keep_lo = 1.0 - x_inside * at_lo
            keep_hi = 1.0 - x_inside * at_hi
            for f in range(5):
                low = lo[f] * first
                high = pltpu.roll(low, size - 1, axis)
                change[f] = change[f] + (high - low)
                change_l[f] = change_l[f] + (high * keep_hi - low * keep_lo)
        for f in range(5):
            chgf[f, x] = change[f]
            chgl[f, x] = change_l[f]
            chgf[f, before] = chgf[f, before] + lower[f]
            chgl[f, before] = chgl[f, before] + lower_l[f]
        return best

    hz[...] = jnp.zeros_like(hz)
    pflux[...] = jnp.zeros_like(pflux)
    pspeed[...] = jnp.zeros_like(pspeed)
    return fold(lax.fori_loop(0, nx, plane, jnp.zeros((ny, nz), F32)))


def coarse_base(coarse, chgl, courant, gx, gy, gz, hy, hz):
    nx, ny, nz = coarse.shape[1:]

    @pl.loop(0, nx)
    def _(x):
        for f in range(5):
            chgl[f, x] = coarse[f, x] - courant * chgl[f, x]

    def edge(lower, upper, d):
        fl, sl = dirflux(lower, speeds(lower), d)
        fu, su = dirflux(upper, speeds(upper), d)
        return face(lower, fl, sl, upper, fu, su)

    def take(ref, side):
        return [ref[side, f] for f in range(5)]

    low = edge(take(gx, 0), [coarse[f, 0] for f in range(5)], 0)
    high = edge([coarse[f, nx - 1] for f in range(5)], take(gx, 1), 0)
    for f in range(5):
        chgl[f, 0] = chgl[f, 0] + courant * low[f]
        chgl[f, nx - 1] = chgl[f, nx - 1] - courant * high[f]
    low = edge(take(gy, 0), take(hy, 0), 1)
    high = edge(take(hy, 1), take(gy, 1), 1)
    for f in range(5):
        for x in range(nx):
            chgl[f, x, 0:1, :] = chgl[f, x, 0:1, :] + courant * low[f][x : x + 1]
            chgl[f, x, ny - 1 : ny, :] = chgl[f, x, ny - 1 : ny, :] - courant * high[f][x : x + 1]
    tile = lax.broadcasted_iota(jnp.int32, (ny, 128), 1)

    def cells(ref, side):
        return [jnp.where(tile < nx, ref[side, f], 1.0) for f in range(5)]

    low = edge(cells(gz, 0), cells(hz, 0), 2)
    high = edge(cells(hz, 1), cells(gz, 1), 2)
    for f in range(5):
        for x in range(nx):
            add = jnp.broadcast_to(courant * low[f][:, x : x + 1], (ny, 128))
            chgl[f, x, :, 0:128] = chgl[f, x, :, 0:128] + jnp.where(tile == 0, add, 0.0)
            add = jnp.broadcast_to(courant * high[f][:, x : x + 1], (ny, 128))
            chgl[f, x, :, nz - 128 :] = chgl[f, x, :, nz - 128 :] - jnp.where(tile == 127, add, 0.0)


def spread_table():
    cell = lax.broadcasted_iota(jnp.int32, (128, 512), 0)
    lane = lax.broadcasted_iota(jnp.int32, (128, 512), 1)
    wanted = (lane >> 8) * 64 + ((lane & 15) >> 1) * 8 + ((lane >> 5) & 7)
    return jnp.where(cell == wanted, 1.0, 0.0).astype(BF16)


def pool_table():
    lane = lax.broadcasted_iota(jnp.int32, (256, 128), 0)
    cell = lax.broadcasted_iota(jnp.int32, (256, 128), 1) & 63
    wanted = ((lane & 15) >> 1) * 8 + ((lane >> 5) & 7)
    return jnp.where(cell == wanted, 0.125, 0.0).astype(BF16)


def plane_lanes(p):
    return pl.ds(pl.multiple_of(p * 256, 256), 256)


def fine_inner(fu, chg, edge_y, edge_z):
    lane = lax.broadcasted_iota(jnp.int32, (8, 256), 1)
    inner_y = jnp.where(lane >= 16, 1.0, 0.0)
    inner_z = jnp.where(lane & 15 != 0, 1.0, 0.0)
    tile = lax.broadcasted_iota(jnp.int32, (8, 128), 1)

    @pl.loop(0, 2)
    def _(half):
        rows = pl.ds(pl.multiple_of(half * 8, 8), 8)

        def load(p):
            return [fu[f, rows, plane_lanes(p)] for f in range(5)]

        def plane(p, carry):
            u, velocity, pressure, sound, lower = carry
            prims = (velocity, pressure, sound)
            after = load(jnp.minimum(p + 1, BOX - 1))
            next_prims = speeds(after)
            flux, speed = dirflux(u, prims, 0)
            next_flux, next_speed = dirflux(after, next_prims, 0)
            more = jnp.where(p < BOX - 1, 1.0, 0.0)
            upper = [piece * more for piece in face(u, flux, speed, after, next_flux, next_speed)]
            change = [a - b for a, b in zip(upper, lower)]
            for d, shift, keep in ((1, 16, inner_y), (2, 1, inner_z)):
                flux, speed = dirflux(u, prims, d)
                ru = [pltpu.roll(piece, shift, 1) for piece in u]
                rf = [ru[1 + d]] + [pltpu.roll(piece, shift, 1) for piece in flux[1:]]
                low = face(ru, rf, pltpu.roll(speed, shift, 1), u, flux, speed)
                low = [piece * keep for piece in low]
                change = [c + (pltpu.roll(b, 256 - shift, 1) - b) for c, b in zip(change, low)]
            seat = lax.rem(p, 8)
            at = pl.multiple_of(p // 8 * 128, 128)
            here_y = tile >> 4 == seat
            here_z = tile & 15 == p
            for f in range(5):
                chg[f, rows, plane_lanes(p)] = change[f]
                for side, shift in ((0, seat * 16), (1, lax.rem(seat * 16 + 16, 128))):
                    moved = pltpu.roll(u[f][:, side * 128 : side * 128 + 128], shift, 1)
                    place = pl.ds(side * 256 + at, 128)
                    edge_y[f, rows, place] = jnp.where(here_y, moved, edge_y[f, rows, place])
                for side, shift in ((0, p), (1, lax.rem(p + 113, 128))):
                    for t in range(2):
                        moved = pltpu.roll(u[f][:, t * 128 : t * 128 + 128], shift, 1)
                        place = slice(side * 256 + t * 128, side * 256 + t * 128 + 128)
                        edge_z[f, rows, place] = jnp.where(here_z, moved, edge_z[f, rows, place])
            return after, next_prims[0], next_prims[1], next_prims[2], upper

        first = load(0)
        prims = speeds(first)
        nothing = [jnp.zeros((8, 256), F32)] * 5
        lax.fori_loop(0, BOX, plane, (first, prims[0], prims[1], prims[2], nothing))


def fine_outer(sub, fu, chg, edge_y, edge_z, ghosts, regs):
    last = (BOX - 1) * 256
    for part in range(3):
        for side in range(2):
            lanes = slice(side * 256, side * 256 + 256)
            if part == 0:
                inside = [fu[f, :, side * last : side * last + 256] for f in range(5)]
            else:
                inside = [(edge_y, edge_z)[part - 1][f, :, lanes] for f in range(5)]
            at = part * 160 + sub * 80
            outside = [ghosts[at + f * 16 : at + f * 16 + 16, lanes] for f in range(5)]
            lower, upper = (outside, inside) if side == 0 else (inside, outside)
            fl, sl = dirflux(lower, speeds(lower), part)
            fh, sh = dirflux(upper, speeds(upper), part)
            through = face(lower, fl, sl, upper, fh, sh)
            for f in range(5):
                line = (part * 5 + f) * 16
                if sub == 0:
                    regs[line : line + 16, lanes] = through[f]
                else:
                    regs[line : line + 16, lanes] = regs[line : line + 16, lanes] + through[f]
                if part == 0:
                    place = slice(side * last, side * last + 256)
                    chg[f, :, place] = chg[f, :, place] + (through[f] if side else -through[f])
                else:
                    (edge_y, edge_z)[part - 1][f, :, lanes] = through[f] if side else -through[f]


def fine_update(courant, fu, chg, edge_y, edge_z):
    tile = lax.broadcasted_iota(jnp.int32, (16, 128), 1)
    y_side = (tile < 16, tile >= 112)
    z_side = (tile & 15 == 0, tile & 15 == 15)

    @pl.loop(0, BOX)
    def _(p):
        seat = lax.rem(p, 8)
        at = pl.multiple_of(p // 8 * 128, 128)
        y_shift = (lax.rem(128 - seat * 16, 128), 112 - seat * 16)
        z_shift = (lax.rem(128 - p, 128), 15 - p)
        for f in range(5):
            for t in range(2):
                place = pl.ds(pl.multiple_of(p * 256 + t * 128, 128), 128)
                change = chg[f, :, place]
                moved = pltpu.roll(edge_y[f, :, pl.ds(t * 256 + at, 128)], y_shift[t], 1)
                change = change + jnp.where(y_side[t], moved, 0.0)
                for side in range(2):
                    piece = edge_z[f, :, side * 256 + t * 128 : side * 256 + t * 128 + 128]
                    change = change + jnp.where(z_side[side], pltpu.roll(piece, z_shift[side], 1), 0.0)
                fu[f, :, place] = fu[f, :, place] - courant * change


def fine_ghosts(courant, g_o, g_c, spread, lhs):
    for part in range(3):
        for f in range(5):
            old = g_o[(f * 3 + part) * 16 : (f * 3 + part) * 16 + 16, :]
            change = g_c[(f * 3 + part) * 16 : (f * 3 + part) * 16 + 16, :]
            put_split(lhs, part * 160 + f * 16, 480, old)
            put_split(lhs, part * 160 + 80 + f * 16, 480, 0.5 * (old + (old - courant * change)))
    return sum_split(dot_nn(lhs[...], spread[...]))


def fine_results(fu, regs, pool, big, stage):
    stage[16 * STAGE_ROWS :, :] = jnp.zeros((STAGE_ROWS, 128), F32)
    left = lax.broadcasted_iota(jnp.int32, (16, 128), 1) < 64
    count = 16 * 70
    for f in range(5):
        for x in range(8):
            at = x * 512
            put_split(big, (f * 8 + x) * 16, count, fu[f, :, at : at + 256] + fu[f, :, at + 256 : at + 512])
    for line in range(15):
        for side in range(2):
            piece = regs[line * 16 : line * 16 + 16, side * 256 : side * 256 + 256]
            put_split(big, (40 + line * 2 + side) * 16, count, piece)
    done = sum_split(dot_nn(big[...], pool[...]))

    def put(line, group):
        tile = jnp.where(left, done[group * 16 : group * 16 + 16], done[group * 16 + 16 : group * 16 + 32])
        for half in range(2):
            stage[pl.ds(half * 8 * STAGE_ROWS + line, 8, stride=STAGE_ROWS), :] = tile[half * 8 : half * 8 + 8]

    for f in range(5):
        for i in range(4):
            put(f * 7 + i, f * 8 + 2 * i)
        for part in range(3):
            put(f * 7 + 4 + part, 40 + (part * 5 + f) * 2)
    for line in range(35, STAGE_ROWS):
        for half in range(2):
            stage[pl.ds(half * 8 * STAGE_ROWS + line, 8, stride=STAGE_ROWS), :] = jnp.zeros((8, 128), F32)


def candidate_keys(owner, keys):
    slots = owner.shape[0]
    lane = lax.broadcasted_iota(jnp.int32, (8, slots * BOX), 1)
    slot = lane >> 4
    spot = lane & 15
    owners = jnp.full(lane.shape, -1, jnp.int32)
    for k in range(slots):
        owners = jnp.where(slot == k, owner[k], owners)
    rank = jnp.zeros(lane.shape, jnp.int32)
    for k in range(slots - 1):
        rank = rank + jnp.where((owners == owner[k]) & (slot > k), 1, 0)
    seat = jnp.where(owners >= 0, owners * 2 + rank, -1)
    on = seat >= 0
    inner = on & (spot >= SHIFT) & (spot < SHIFT + CORE)
    keys[0:1, :] = jnp.where(inner, (spot - SHIFT) * 64 + seat, -1)[0:1]
    outer = jnp.where(spot == SHIFT - 1, seat, jnp.where(spot == SHIFT + CORE, seat + 64, -1))
    keys[1:2, :] = jnp.where(on, outer, -1)[0:1]
    keys[2:8, :] = seat[0:6]


def box_tables(corner, slots, count_z, box_lane, lane_box):
    count = corner.shape[1]
    sources = [corner[0, b] * count_z + lax.div(corner[2, b], slots) for b in range(count)]
    lanes = []
    for b in range(count):
        place = jnp.int32(0)
        for i in range(b):
            place = place + jnp.where(sources[i] == sources[b], 1, 0)
        lanes.append(sources[b] * 2 + place)
        box_lane[b] = lanes[b]

    @pl.loop(0, 64)
    def _(lane):
        box = jnp.int32(count)
        for b in range(count):
            box = jnp.where(box_lane[b] == lane, b, box)
        lane_box[lane] = box


def step_kernel(
    owner, corner, coarse, fine,
    base, fine_new, back, gmax, keys,
    fu, chg, chgf, chgl, pflux, pspeed, exy, cxy, cz, rxy, pay_o, pay_c, arr_o, arr_c,
    hy, hz, gx, gy, gz, tops, mine, g_o, g_c, spread, pool, lhs, ghosts, edge_y, edge_z, regs, big, stage,
    ret, by_lane, by_box, box_lane, lane_box,
    in_sem, out_sem, so, ro, sc, rc, sr, rr, hs, hr, ts, tr,
):
    ix, iy, iz = (lax.axis_index(a) for a in ("gx", "gy", "gz"))
    nx, ny, nz = (lax.axis_size(a) for a in ("gx", "gy", "gz"))
    me = ix * nz + iz
    peers = nx * nz
    load_fine = pltpu.make_async_copy(fine, fu, in_sem.at[0])
    load_fine.start()
    barrier = pltpu.get_barrier_semaphore()

    @pl.loop(1, peers)
    def _(s):
        x, z = plane_peer(s, 1)
        pl.semaphore_signal(barrier, inc=1, device_id=(x, iy, z), device_id_type=MESH)

    @pl.loop(1, ny)
    def _(s):
        pl.semaphore_signal(barrier, inc=1, device_id=(ix, lax.rem(iy + s, ny), iz), device_id_type=MESH)

    candidate_keys(owner, keys)
    exy[...] = onehot(keys[0:1, :], 512)
    pack(coarse, keys[1:2, :], exy, pay_o, cxy, cz, rxy)
    for part in range(8):
        pay_o[pl.ds(part * 8 * OUT_ROWS + 15, 8, stride=OUT_ROWS), :] = jnp.zeros((8, 128), F32)
    pl.semaphore_wait(barrier, peers - 1 + ny - 1)
    old_patch = start_patches(pay_o, arr_o, OUT_ROWS, so, ro)
    arr_o[lanes_of_peer(me, OUT_ROWS), :] = pay_o[lanes_of_peer(me, OUT_ROWS), :]

    best = coarse_changes(coarse, keys[2:3, :], chgf, chgl, pflux, pspeed, hy, hz)
    load_fine.wait()

    def fine_plane(p, best):
        u = [fu[f, :, plane_lanes(p)] for f in range(5)]
        return jnp.maximum(best, fastest_of(speeds(u)))

    fine_best = lax.fori_loop(0, BOX, fine_plane, jnp.zeros((16, 256), F32))
    mine[...] = jnp.maximum(best, fold(fine_best))

    def top(s):
        return remote(mine, tops.at[s], ts.at[s], tr.at[s], (ix, lax.rem(iy + s, ny), iz))

    @pl.loop(1, ny)
    def _(s):
        top(s).start()

    pack(chgf, keys[1:2, :], exy, pay_c, cxy, cz, rxy)

    @pl.loop(1, ny)
    def _(s):
        top(s).wait()

    best = mine[...]
    for s in range(1, ny):
        best = jnp.maximum(best, tops[s])
    best = jnp.full((8, 128), jnp.max(best), F32)
    for part in range(8):
        pay_c[pl.ds(part * 8 * OUT_ROWS + 15, 8, stride=OUT_ROWS), :] = best
    new_patch = start_patches(pay_c, arr_c, OUT_ROWS, sc, rc)
    arr_c[lanes_of_peer(me, OUT_ROWS), :] = pay_c[lanes_of_peer(me, OUT_ROWS), :]
    up_x, down_x = lax.rem(ix + 1, nx), lax.rem(ix + nx - 1, nx)
    up_y, down_y = lax.rem(iy + 1, ny), lax.rem(iy + ny - 1, ny)
    up_z, down_z = lax.rem(iz + 1, nz), lax.rem(iz + nz - 1, nz)
    sides = [
        remote(coarse.at[:, coarse.shape[1] - 1], gx.at[0], hs.at[0], hr.at[0], (up_x, iy, iz)),
        remote(coarse.at[:, 0], gx.at[1], hs.at[1], hr.at[1], (down_x, iy, iz)),
        remote(hy.at[1], gy.at[0], hs.at[2], hr.at[2], (ix, up_y, iz)),
        remote(hy.at[0], gy.at[1], hs.at[3], hr.at[3], (ix, down_y, iz)),
        remote(hz.at[1], gz.at[0], hs.at[4], hr.at[4], (ix, iy, up_z)),
        remote(hz.at[0], gz.at[1], hs.at[5], hr.at[5], (ix, iy, down_z)),
    ]
    for side in sides:
        side.start()

    fine_inner(fu, chg, edge_y, edge_z)
    box_tables(corner, owner.shape[0], nz, box_lane, lane_box)
    spread[...] = spread_table()
    pool[...] = pool_table()

    @pl.loop(1, peers)
    def _(s):
        old_patch(s).wait()

    @pl.loop(1, peers)
    def _(s):
        new_patch(s).wait()

    for part in range(8):
        best = jnp.maximum(best, arr_c[pl.ds(part * 8 * OUT_ROWS + 15, 8, stride=OUT_ROWS), :])
    gmax[...] = best
    courant = COURANT_NUMBER / jnp.max(best)
    for arr, g in ((arr_o, g_o), (arr_c, g_c)):
        for lane in range(64):
            by_lane[lane] = arr[lane * OUT_ROWS : (lane + 1) * OUT_ROWS, :]
        for b in range(16):
            g[pl.ds(b, OUT_ROWS, stride=16), :] = by_lane[box_lane[b]]
    ghosts[...] = fine_ghosts(courant, g_o, g_c, spread, lhs)
    fine_outer(0, fu, chg, edge_y, edge_z, ghosts, regs)
    fine_update(courant, fu, chg, edge_y, edge_z)
    fine_inner(fu, chg, edge_y, edge_z)
    fine_outer(1, fu, chg, edge_y, edge_z, ghosts, regs)
    fine_update(courant, fu, chg, edge_y, edge_z)
    fine_results(fu, regs, pool, big, stage)
    for b in range(17):
        by_box[b] = stage[b * STAGE_ROWS : (b + 1) * STAGE_ROWS, :]
    for lane in range(64):
        ret[lane * BACK_ROWS : (lane + 1) * BACK_ROWS, :] = by_box[lane_box[lane]][:BACK_ROWS]
    back_patch = start_patches(ret, back, BACK_ROWS, sr, rr)
    own = pltpu.make_async_copy(
        ret.at[lanes_of_peer(me, BACK_ROWS), :], back.at[lanes_of_peer(me, BACK_ROWS), :], out_sem.at[0]
    )
    own.start()
    store_fine = pltpu.make_async_copy(fu, fine_new, out_sem.at[1])
    store_fine.start()
    for side in sides:
        side.wait()
    coarse_base(coarse, chgl, courant, gx, gy, gz, hy, hz)
    store_base = pltpu.make_async_copy(chgl, base, out_sem.at[2])
    store_base.start()
    own.wait()
    store_fine.wait()
    store_base.wait()

    @pl.loop(1, peers)
    def _(s):
        back_patch(s).wait()


def apply_kernel(base, keys, arr, gmax, out, lxy, lz, dxy, dz):
    nx, _, nz = base.shape[1:]
    courant = COURANT_NUMBER / jnp.max(gmax[...])
    left = lax.broadcasted_iota(jnp.int32, (16, 128), 1) < 64
    left64 = lax.broadcasted_iota(jnp.int32, (64, 128), 1) < 64

    def lanes_of(line):
        return jnp.concatenate(
            [arr[pl.ds(part * 8 * BACK_ROWS + line, 8, stride=BACK_ROWS), :] for part in range(8)], axis=0
        )

    flat = [(f, i) for f in range(5) for i in range(6)]
    for first in range(0, 30, 2):
        pair = flat[first : first + 2]
        turned = jnp.concatenate([lanes_of(f * 7 + i) for f, i in pair], axis=0).T
        for second in range(2):
            pieces = []
            for couple in range(4):
                even = jnp.concatenate(
                    [turned[a * 64 + couple * 16 : a * 64 + couple * 16 + 8] for a in range(2)], axis=0
                )
                odd = jnp.concatenate(
                    [turned[a * 64 + couple * 16 + 8 : a * 64 + couple * 16 + 16] for a in range(2)], axis=0
                )
                if second == 0:
                    pieces.append(jnp.where(left, even, pltpu.roll(odd, 64, 1)))
                else:
                    pieces.append(jnp.where(left, pltpu.roll(even, 64, 1), odd))
            put_split(lxy, (first + second) * 16, 480, jnp.concatenate(pieces, axis=1))
    for f in range(5):
        both = jnp.concatenate([lanes_of(f * 7 + 6), lanes_of(f * 7 + 6)], axis=0).T
        put_split(lz, f * 64, 320, jnp.where(left64, both[:64], both[64:]))
    dxy[...] = sum_split(dot_nn(lxy[...], onehot(keys[0:1, :], 512)))
    dz[...] = sum_split(dot_nn(lz[...], onehot(keys[1:2, :], 128)))

    spot = lax.broadcasted_iota(jnp.int32, (CORE, nz), 1) % BOX
    refined = jnp.broadcast_to(keys[2:3, :], (CORE, nz)) >= 0
    inside = refined & (spot >= SHIFT) & (spot < SHIFT + CORE)
    z_sign = courant * jnp.where(spot == SHIFT - 1, -1.0, jnp.where(spot == SHIFT + CORE, 1.0, 0.0))
    mid = slice(SHIFT, SHIFT + CORE)
    for f in range(5):
        for x in range(nx):
            out[f, x] = base[f, x]
        for side, x, sign in ((0, SHIFT - 1, -1.0), (1, SHIFT + CORE, 1.0)):
            at = (f * 6 + 4) * 16 + side * 8
            out[f, x, mid, :] = out[f, x, mid, :] + (sign * courant) * dxy[at : at + 8, :]
            at = (f * 6 + 5) * 16 + side * 8
            for i in range(CORE):
                y = x
                out[f, SHIFT + i, y : y + 1, :] = (
                    out[f, SHIFT + i, y : y + 1, :] + (sign * courant) * dxy[at + i : at + i + 1, :]
                )
        for i in range(CORE):
            fixed = out[f, SHIFT + i, mid, :] + z_sign * dz[f * 64 + i * 8 : f * 64 + i * 8 + 8, :]
            average = dxy[f * 96 + i * 8 : f * 96 + i * 8 + 8, :]
            out[f, SHIFT + i, mid, :] = jnp.where(inside, average, fixed)


VMEM = pl.BlockSpec(memory_space=pltpu.VMEM)
SMEM = pl.BlockSpec(memory_space=pltpu.SMEM)
ANY = pl.BlockSpec(memory_space=pl.ANY)


def shape(*dims):
    return jax.ShapeDtypeStruct(dims, F32)


def step_call(owner, corner, coarse, fine):
    peers = lax.axis_size("gx") * lax.axis_size("gz")
    count_y = lax.axis_size("gy")
    _, nx, ny, nz = coarse.shape
    dma = pltpu.SemaphoreType.DMA

    def vmem(*dims, dtype=F32):
        return pltpu.VMEM(dims, dtype)

    return pl.pallas_call(
        step_kernel,
        out_shape=[
            shape(*coarse.shape),
            shape(*fine.shape),
            shape(64 * BACK_ROWS, 128),
            shape(8, 128),
            jax.ShapeDtypeStruct((8, nz), jnp.int32),
        ],
        in_specs=[SMEM, SMEM, VMEM, ANY],
        out_specs=[ANY, ANY, ANY, VMEM, VMEM],
        scratch_shapes=[
            vmem(*fine.shape),
            vmem(*fine.shape),
            vmem(5, nx, ny, nz),
            vmem(5, nx, ny, nz),
            vmem(5, ny, nz),
            vmem(ny, nz),
            vmem(512, nz, dtype=BF16),
            vmem(480, nz, dtype=BF16),
            vmem(960, nz, dtype=BF16),
            vmem(160, 512),
            *[vmem(64 * OUT_ROWS, 128)] * 4,
            vmem(2, 5, nx, nz),
            vmem(2, 5, ny, 128),
            vmem(2, 5, ny, nz),
            vmem(2, 5, nx, nz),
            vmem(2, 5, ny, 128),
            vmem(count_y, 8, 128),
            vmem(8, 128),
            vmem(16 * OUT_ROWS, 128),
            vmem(16 * OUT_ROWS, 128),
            vmem(128, 512, dtype=BF16),
            vmem(256, 128, dtype=BF16),
            vmem(1440, 128, dtype=BF16),
            vmem(480, 512),
            vmem(5, 16, 512),
            vmem(5, 16, 512),
            vmem(240, 512),
            vmem(3360, 256, dtype=BF16),
            vmem(17 * STAGE_ROWS, 128),
            vmem(64 * BACK_ROWS, 128),
            vmem(64, OUT_ROWS, 128),
            vmem(17, STAGE_ROWS, 128),
            pltpu.SMEM((16,), jnp.int32),
            pltpu.SMEM((64,), jnp.int32),
            dma((1,)),
            dma((3,)),
            *[dma((peers,))] * 6,
            dma((6,)),
            dma((6,)),
            dma((count_y,)),
            dma((count_y,)),
        ],
        compiler_params=pltpu.CompilerParams(
            collective_id=0, has_side_effects=True, vmem_limit_bytes=VMEM_LIMIT
        ),
        name="step",
    )(owner, corner, coarse, fine)


def apply_call(base, keys, arr, gmax):
    nz = base.shape[3]
    return pl.pallas_call(
        apply_kernel,
        out_shape=shape(*base.shape),
        in_specs=[VMEM] * 4,
        out_specs=VMEM,
        scratch_shapes=[
            pltpu.VMEM((1440, 512), BF16),
            pltpu.VMEM((960, 128), BF16),
            pltpu.VMEM((480, nz), F32),
            pltpu.VMEM((320, nz), F32),
        ],
        compiler_params=pltpu.CompilerParams(vmem_limit_bytes=VMEM_LIMIT),
        name="reflux_apply",
    )(base, keys, arr, gmax)


def local(coarse_old, fine_old, slot_owner, box_corner):
    base, fine_new, back, gmax, keys = step_call(
        slot_owner.reshape(-1), box_corner.T, coarse_old, fine_old.transpose(1, 0, 2)
    )
    coarse_new = apply_call(base, keys, back, gmax)
    return (coarse_new, fine_new.transpose(1, 0, 2))


def solution(mesh):
    in_specs = (
        P(None, "gx", "gy", "gz"),
        P(("gx", "gy", "gz"), None, None),
        P("gx", "gy", "gz"),
        P(("gx", "gy", "gz"), None),
    )
    out_specs = (P(None, "gx", "gy", "gz"), P(("gx", "gy", "gz"), None, None))
    return jax.shard_map(local, mesh=mesh, in_specs=in_specs, out_specs=out_specs, check_vma=False)
```

```python
import jax
import jax.numpy as jnp
from jax import lax
from jax.experimental import pallas as pl
from jax.experimental.pallas import tpu as pltpu
from jax.sharding import PartitionSpec as P

BOX = 16
CORE = 8
SHIFT = 4
HEAT_RATIO = 1.4
COURANT_NUMBER = 0.15
OUT_ROWS = 15
OUT_BLOCK = 32
BACK_ROWS = 35
BACK_BLOCK = 72
STAGE_ROWS = 40
MESH = pl.DeviceIdType.MESH
F32 = jnp.float32
BF16 = jnp.bfloat16
VMEM_LIMIT = 56 * 1024 * 1024


def speeds(u):
    inverse = 1.0 / u[0]
    velocity = [u[1] * inverse, u[2] * inverse, u[3] * inverse]
    kinetic = 0.5 * (u[1] * velocity[0] + u[2] * velocity[1] + u[3] * velocity[2])
    pressure = (HEAT_RATIO - 1.0) * (u[4] - kinetic)
    sound = jnp.sqrt(HEAT_RATIO * pressure * inverse)
    return velocity, pressure, sound


def dirflux(u, prims, d):
    velocity, pressure, sound = prims
    normal = velocity[d]
    flux = [u[1 + d]]
    for m in range(3):
        piece = u[1 + m] * normal
        flux.append(piece + pressure if m == d else piece)
    flux.append((u[4] + pressure) * normal)
    return flux, jnp.abs(normal) + sound


def face(ul, fl, sl, ur, fr, sr):
    half = 0.5 * jnp.maximum(sl, sr)
    return [0.5 * (a + b) - half * (d - c) for a, b, c, d in zip(fl, fr, ul, ur)]


def fastest_of(prims):
    velocity, _, sound = prims
    top = jnp.maximum(jnp.abs(velocity[0]), jnp.abs(velocity[1]))
    return jnp.maximum(top, jnp.abs(velocity[2])) + sound


def fold(top):
    best = None
    for row in range(0, top.shape[0], 8):
        for lane in range(0, top.shape[1], 128):
            tile = top[row : row + 8, lane : lane + 128]
            best = tile if best is None else jnp.maximum(best, tile)
    return best


def split3(x):
    high = x.astype(BF16)
    rest = x - high.astype(F32)
    middle = rest.astype(BF16)
    low = (rest - middle.astype(F32)).astype(BF16)
    return high, middle, low


def put_split(ref, row, count, x):
    for part, piece in enumerate(split3(x)):
        ref[pl.ds(part * count + row, x.shape[0]), :] = piece


def sum_split(product):
    count = product.shape[0] // 3
    return product[:count] + product[count : 2 * count] + product[2 * count :]


def dot_nt(a, b):
    return lax.dot_general(a, b, (((1,), (1,)), ((), ())), preferred_element_type=F32)


def dot_nn(a, b):
    return lax.dot_general(a, b, (((1,), (0,)), ((), ())), preferred_element_type=F32)


def onehot(key_row, rows):
    index = lax.broadcasted_iota(jnp.int32, (rows, key_row.shape[1]), 0)
    return jnp.where(index == key_row, 1.0, 0.0).astype(BF16)


def plane_peer(s, sign):
    count_x, count_z = lax.axis_size("gx"), lax.axis_size("gz")
    x = lax.rem(lax.axis_index("gx") + sign * (s // count_z) + count_x, count_x)
    z = lax.rem(lax.axis_index("gz") + sign * lax.rem(s, count_z) + count_z, count_z)
    return x, z


def remote(src, dst, send, recv, device):
    return pltpu.make_async_remote_copy(
        src_ref=src, dst_ref=dst, send_sem=send, recv_sem=recv, device_id=device, device_id_type=MESH
    )


def rows_of_lanes(part, block, rows, line):
    return pl.ds(part % 4 * 8 * block + part // 4 * rows + line, 8, stride=block)


def block_of(peer, block, rows):
    return pl.ds(pl.multiple_of(peer * block, 8), rows)


def start_patches(pay, arr, block, rows, send, recv):
    iy = lax.axis_index("gy")
    me = lax.axis_index("gx") * lax.axis_size("gz") + lax.axis_index("gz")

    def patch(s):
        x, z = plane_peer(s, 1)
        peer = x * lax.axis_size("gz") + z
        return remote(
            pay.at[block_of(peer, block, rows), :], arr.at[block_of(me, block, rows), :], send.at[s], recv.at[s], (x, iy, z)
        )

    @pl.loop(1, lax.axis_size("gx") * lax.axis_size("gz"))
    def _(s):
        patch(s).start()

    return patch


def pack(fields, keys_z, exy, pay, cxy, cz, rxy):
    outer = (SHIFT - 1, SHIFT + CORE)
    inner = range(SHIFT, SHIFT + CORE)
    for f in range(5):
        on_x = [fields[f, x, SHIFT : SHIFT + CORE, :] for x in outer]
        on_y = [fields[f, x, y : y + 1, :] for y in outer for x in inner]
        put_split(cxy, f * 32, 160, jnp.concatenate(on_x + on_y, axis=0))
        on_z = [fields[f, x, SHIFT : SHIFT + CORE, :] for x in inner]
        put_split(cz, f * 64, 320, jnp.concatenate(on_z, axis=0))
    rxy[...] = sum_split(dot_nt(cxy[...], exy[...]))
    rz = sum_split(dot_nt(cz[...], onehot(keys_z, 128)))
    left = lax.broadcasted_iota(jnp.int32, (8, 128), 1) < 64
    left64 = lax.broadcasted_iota(jnp.int32, (64, 128), 1) < 64

    def put(line, tile):
        for part in range(8):
            pay[rows_of_lanes(part, OUT_BLOCK, OUT_ROWS, line), :] = tile[part * 8 : part * 8 + 8]

    for f in range(5):
        pieces = []
        for side in range(2):
            for j in range(CORE):
                lanes = slice(j // 2 * 128, j // 2 * 128 + 128)
                a = rxy[f * 32 + side * 8 : f * 32 + side * 8 + 8, lanes]
                b = rxy[f * 32 + 16 + side * 8 : f * 32 + 24 + side * 8, lanes]
                if j % 2 == 0:
                    pieces.append(jnp.where(left, a, pltpu.roll(b, 64, 1)))
                else:
                    pieces.append(jnp.where(left, pltpu.roll(a, 64, 1), b))
        turned = jnp.concatenate(pieces, axis=0).T
        put(f * 3, turned[:64])
        put(f * 3 + 1, turned[64:])
        turned = rz[f * 64 : f * 64 + 64]
        turned = jnp.concatenate([turned, turned], axis=0).T
        put(f * 3 + 2, jnp.where(left64, turned[:64], turned[64:]))


def coarse_changes(coarse, refined_row, chgf, chgl, pflux, pspeed, hy, hz):
    nx, ny, nz = coarse.shape[1:]
    row = lax.broadcasted_iota(jnp.int32, (ny, nz), 0)
    lane = lax.broadcasted_iota(jnp.int32, (ny, nz), 1)
    spot = lane % BOX
    refined = jnp.broadcast_to(refined_row, (ny, nz)) >= 0
    row_in = (row >= SHIFT) & (row < SHIFT + CORE)
    lane_in = refined & (spot >= SHIFT) & (spot < SHIFT + CORE)

    def mark(mask):
        return jnp.where(mask, 1.0, 0.0)

    at_x = mark(row_in & lane_in)
    at_y_lo = mark(lane_in & ((row == SHIFT) | (row == SHIFT + CORE)))
    at_y_hi = mark(lane_in & ((row == SHIFT - 1) | (row == SHIFT + CORE - 1)))
    at_z_lo = mark(refined & row_in & ((spot == SHIFT) | (spot == SHIFT + CORE)))
    at_z_hi = mark(refined & row_in & ((spot == SHIFT - 1) | (spot == SHIFT + CORE - 1)))
    keep_row = mark(row > 0)
    keep_lane = mark(lane > 0)
    lane_tile = lax.broadcasted_iota(jnp.int32, (ny, 128), 1)

    def plane(x, best):
        before = jnp.maximum(x - 1, 0)
        u = [coarse[f, x] for f in range(5)]
        prims = speeds(u)
        best = jnp.maximum(best, fastest_of(prims))
        for side, edge in ((0, 0), (1, ny - 1)):
            for f in range(5):
                hy[side, f, pl.ds(x, 1), :] = coarse[f, x, edge : edge + 1, :]
        for side, edge in ((0, 0), (1, nz - 1)):
            for f in range(5):
                column = jnp.broadcast_to(u[f][:, edge : edge + 1], (ny, 128))
                hz[side, f] = jnp.where(lane_tile == x, column, hz[side, f])
        x_inside = jnp.where((x >= SHIFT) & (x < SHIFT + CORE), 1.0, 0.0)
        x_face = jnp.where((x == SHIFT) | (x == SHIFT + CORE), 1.0, 0.0)
        flux, speed = dirflux(u, prims, 0)
        lower = face(
            [coarse[f, before] for f in range(5)], [pflux[f] for f in range(5)], pspeed[...], u, flux, speed
        )
        lower = [jnp.where(x > 0, piece, 0.0) for piece in lower]
        for f in range(5):
            pflux[f] = flux[f]
        pspeed[...] = speed
        keep = 1.0 - x_face * at_x
        lower_l = [piece * keep for piece in lower]
        change = [-piece for piece in lower]
        change_l = [-piece for piece in lower_l]
        for d, axis, size, first, at_lo, at_hi in (
            (1, 0, ny, keep_row, at_y_lo, at_y_hi),
            (2, 1, nz, keep_lane, at_z_lo, at_z_hi),
        ):
            flux, speed = dirflux(u, prims, d)
            ru = [pltpu.roll(piece, 1, axis) for piece in u]
            rf = [ru[1 + d]] + [pltpu.roll(piece, 1, axis) for piece in flux[1:]]
            lo = face(ru, rf, pltpu.roll(speed, 1, axis), u, flux, speed)
            keep_lo = 1.0 - x_inside * at_lo
            keep_hi = 1.0 - x_inside * at_hi
            for f in range(5):
                low = lo[f] * first
                high = pltpu.roll(low, size - 1, axis)
                change[f] = change[f] + (high - low)
                change_l[f] = change_l[f] + (high * keep_hi - low * keep_lo)
        for f in range(5):
            chgf[f, x] = change[f]
            chgl[f, x] = change_l[f]
            chgf[f, before] = chgf[f, before] + lower[f]
            chgl[f, before] = chgl[f, before] + lower_l[f]
        return best

    hz[...] = jnp.zeros_like(hz)
    pflux[...] = jnp.zeros_like(pflux)
    pspeed[...] = jnp.zeros_like(pspeed)
    return fold(lax.fori_loop(0, nx, plane, jnp.zeros((ny, nz), F32)))


def coarse_base(coarse, chgl, courant, gx, gy, gz, hy, hz):
    nx, ny, nz = coarse.shape[1:]

    @pl.loop(0, nx)
    def _(x):
        for f in range(5):
            chgl[f, x] = coarse[f, x] - courant * chgl[f, x]

    def edge(lower, upper, d):
        fl, sl = dirflux(lower, speeds(lower), d)
        fu, su = dirflux(upper, speeds(upper), d)
        return face(lower, fl, sl, upper, fu, su)

    def take(ref, side):
        return [ref[side, f] for f in range(5)]

    low = edge(take(gx, 0), [coarse[f, 0] for f in range(5)], 0)
    high = edge([coarse[f, nx - 1] for f in range(5)], take(gx, 1), 0)
    for f in range(5):
        chgl[f, 0] = chgl[f, 0] + courant * low[f]
        chgl[f, nx - 1] = chgl[f, nx - 1] - courant * high[f]
    low = edge(take(gy, 0), take(hy, 0), 1)
    high = edge(take(hy, 1), take(gy, 1), 1)
    for f in range(5):
        for x in range(nx):
            chgl[f, x, 0:1, :] = chgl[f, x, 0:1, :] + courant * low[f][x : x + 1]
            chgl[f, x, ny - 1 : ny, :] = chgl[f, x, ny - 1 : ny, :] - courant * high[f][x : x + 1]
    tile = lax.broadcasted_iota(jnp.int32, (ny, 128), 1)

    def cells(ref, side):
        return [jnp.where(tile < nx, ref[side, f], 1.0) for f in range(5)]

    low = edge(cells(gz, 0), cells(hz, 0), 2)
    high = edge(cells(hz, 1), cells(gz, 1), 2)
    for f in range(5):
        for x in range(nx):
            add = jnp.broadcast_to(courant * low[f][:, x : x + 1], (ny, 128))
            chgl[f, x, :, 0:128] = chgl[f, x, :, 0:128] + jnp.where(tile == 0, add, 0.0)
            add = jnp.broadcast_to(courant * high[f][:, x : x + 1], (ny, 128))
            chgl[f, x, :, nz - 128 :] = chgl[f, x, :, nz - 128 :] - jnp.where(tile == 127, add, 0.0)


def spread_table():
    cell = lax.broadcasted_iota(jnp.int32, (128, 512), 0)
    lane = lax.broadcasted_iota(jnp.int32, (128, 512), 1)
    wanted = (lane >> 8) * 64 + ((lane & 15) >> 1) * 8 + ((lane >> 5) & 7)
    return jnp.where(cell == wanted, 1.0, 0.0).astype(BF16)


def pool_table():
    lane = lax.broadcasted_iota(jnp.int32, (256, 128), 0)
    cell = lax.broadcasted_iota(jnp.int32, (256, 128), 1) & 63
    wanted = ((lane & 15) >> 1) * 8 + ((lane >> 5) & 7)
    return jnp.where(cell == wanted, 0.125, 0.0).astype(BF16)


def roll_tiles(x, shift):
    return jnp.concatenate([pltpu.roll(x[:, at : at + 128], shift, 1) for at in range(0, x.shape[1], 128)], axis=1)


def plane_lanes(p):
    return pl.ds(pl.multiple_of(p * 256, 256), 256)


def fine_inner(fu, chg, pflux, pspeed):
    lane = lax.broadcasted_iota(jnp.int32, (16, 512), 1)
    inner_y = jnp.where(lane & 255 >= 16, 1.0, 0.0)
    inner_z = jnp.where(lane & 15 != 0, 1.0, 0.0)
    for f in range(5):
        pflux[f, :, 0:256] = jnp.zeros((16, 256), F32)
    pspeed[:, 0:256] = jnp.zeros((16, 256), F32)

    def pair(t, _):
        first = t * 2
        before = jnp.maximum(first - 1, 0)
        both = pl.ds(pl.multiple_of(t * 512, 512), 512)
        u = [fu[f, :, both] for f in range(5)]
        prims = speeds(u)
        flux, speed = dirflux(u, prims, 0)
        lu = [jnp.concatenate([fu[f, :, plane_lanes(before)], u[f][:, :256]], axis=1) for f in range(5)]
        lf = [jnp.concatenate([pflux[f, :, 0:256], flux[f][:, :256]], axis=1) for f in range(5)]
        ls = jnp.concatenate([pspeed[:, 0:256], speed[:, :256]], axis=1)
        lower = face(lu, lf, ls, u, flux, speed)
        one = [jnp.where(t > 0, piece[:, :256], 0.0) for piece in lower]
        two = [piece[:, 256:] for piece in lower]
        for f in range(5):
            pflux[f, :, 0:256] = flux[f][:, 256:]
        pspeed[:, 0:256] = speed[:, 256:]
        change = [jnp.concatenate([b - a, -b], axis=1) for a, b in zip(one, two)]
        for d, shift, keep in ((1, 16, inner_y), (2, 1, inner_z)):

            def turn(x, amount):
                return pltpu.roll(x, amount % 512, 1) if d == 1 else roll_tiles(x, amount % 128)

            flux, speed = dirflux(u, prims, d)
            ru = [turn(piece, shift) for piece in u]
            rf, rs = dirflux(ru, speeds(ru), d)
            low = face(ru, rf, rs, u, flux, speed)
            low = [piece * keep for piece in low]
            change = [c + (turn(b, -shift) - b) for c, b in zip(change, low)]
        for f in range(5):
            chg[f, :, both] = change[f]
            chg[f, :, plane_lanes(before)] = chg[f, :, plane_lanes(before)] + one[f]
        return 0

    lax.fori_loop(0, BOX // 2, pair, 0)


def fine_edges(fu, edge_y, edge_z):
    tile = lax.broadcasted_iota(jnp.int32, (16, 128), 1)

    @pl.loop(0, 5)
    def _(f):
        for side in range(2):
            for block in range(2):
                cells = None
                for seat in range(8):
                    at = (block * 8 + seat) * 256 + side * 128
                    moved = pltpu.roll(fu[f, :, at : at + 128], (seat + side) * 16 % 128, 1)
                    cells = moved if cells is None else jnp.where(tile >> 4 == seat, moved, cells)
                edge_y[f, :, side * 256 + block * 128 : side * 256 + block * 128 + 128] = cells
            for block in range(2):
                cells = None
                for p in range(BOX):
                    at = p * 256 + block * 128
                    moved = pltpu.roll(fu[f, :, at : at + 128], (p + side * 113) % 128, 1)
                    cells = moved if cells is None else jnp.where(tile & 15 == p, moved, cells)
                edge_z[f, :, side * 256 + block * 128 : side * 256 + block * 128 + 128] = cells


def fine_outer(sub, fu, chg, edge_y, edge_z, ghosts, regs):
    last = (BOX - 1) * 256
    for part in range(3):
        for side in range(2):
            lanes = slice(side * 256, side * 256 + 256)
            if part == 0:
                inside = [fu[f, :, side * last : side * last + 256] for f in range(5)]
            else:
                inside = [(edge_y, edge_z)[part - 1][f, :, lanes] for f in range(5)]
            at = part * 160 + sub * 80
            outside = [ghosts[at + f * 16 : at + f * 16 + 16, lanes] for f in range(5)]
            lower, upper = (outside, inside) if side == 0 else (inside, outside)
            fl, sl = dirflux(lower, speeds(lower), part)
            fh, sh = dirflux(upper, speeds(upper), part)
            through = face(lower, fl, sl, upper, fh, sh)
            for f in range(5):
                line = (part * 5 + f) * 16
                if sub == 0:
                    regs[line : line + 16, lanes] = through[f]
                else:
                    regs[line : line + 16, lanes] = regs[line : line + 16, lanes] + through[f]
                if part == 0:
                    place = slice(side * last, side * last + 256)
                    chg[f, :, place] = chg[f, :, place] + (through[f] if side else -through[f])
                else:
                    (edge_y, edge_z)[part - 1][f, :, lanes] = through[f] if side else -through[f]


def fine_update(courant, fu, chg, edge_y, edge_z):
    tile = lax.broadcasted_iota(jnp.int32, (16, 128), 1)
    y_side = (tile < 16, tile >= 112)
    z_side = (tile & 15 == 0, tile & 15 == 15)

    @pl.loop(0, BOX, unroll=16)
    def _(p):
        seat = lax.rem(p, 8)
        at = pl.multiple_of(p // 8 * 128, 128)
        y_shift = (lax.rem(128 - seat * 16, 128), 112 - seat * 16)
        z_shift = (lax.rem(128 - p, 128), 15 - p)
        for f in range(5):
            for t in range(2):
                place = pl.ds(pl.multiple_of(p * 256 + t * 128, 128), 128)
                change = chg[f, :, place]
                moved = pltpu.roll(edge_y[f, :, pl.ds(t * 256 + at, 128)], y_shift[t], 1)
                change = change + jnp.where(y_side[t], moved, 0.0)
                for side in range(2):
                    piece = edge_z[f, :, side * 256 + t * 128 : side * 256 + t * 128 + 128]
                    change = change + jnp.where(z_side[side], pltpu.roll(piece, z_shift[side], 1), 0.0)
                fu[f, :, place] = fu[f, :, place] - courant * change


def fine_ghosts(courant, g_o, g_c, spread, lhs):
    for part in range(3):
        for f in range(5):
            old = g_o[(f * 3 + part) * 16 : (f * 3 + part) * 16 + 16, :]
            change = g_c[(f * 3 + part) * 16 : (f * 3 + part) * 16 + 16, :]
            put_split(lhs, part * 160 + f * 16, 480, old)
            put_split(lhs, part * 160 + 80 + f * 16, 480, 0.5 * (old + (old - courant * change)))
    return sum_split(dot_nn(lhs[...], spread[...]))


def fine_results(fu, regs, pool, big, stage):
    stage[16 * STAGE_ROWS :, :] = jnp.zeros((STAGE_ROWS, 128), F32)
    left = lax.broadcasted_iota(jnp.int32, (16, 128), 1) < 64
    count = 16 * 70
    for f in range(5):
        for x in range(8):
            at = x * 512
            put_split(big, (f * 8 + x) * 16, count, fu[f, :, at : at + 256] + fu[f, :, at + 256 : at + 512])
    for line in range(15):
        for side in range(2):
            piece = regs[line * 16 : line * 16 + 16, side * 256 : side * 256 + 256]
            put_split(big, (40 + line * 2 + side) * 16, count, piece)
    done = sum_split(dot_nn(big[...], pool[...]))

    def put(line, group):
        tile = jnp.where(left, done[group * 16 : group * 16 + 16], done[group * 16 + 16 : group * 16 + 32])
        for half in range(2):
            stage[pl.ds(half * 8 * STAGE_ROWS + line, 8, stride=STAGE_ROWS), :] = tile[half * 8 : half * 8 + 8]

    for f in range(5):
        for i in range(4):
            put(f * 7 + i, f * 8 + 2 * i)
        for part in range(3):
            put(f * 7 + 4 + part, 40 + (part * 5 + f) * 2)
    for line in range(35, STAGE_ROWS):
        for half in range(2):
            stage[pl.ds(half * 8 * STAGE_ROWS + line, 8, stride=STAGE_ROWS), :] = jnp.zeros((8, 128), F32)


def candidate_keys(owner, keys):
    slots = owner.shape[0]
    lane = lax.broadcasted_iota(jnp.int32, (8, slots * BOX), 1)
    slot = lane >> 4
    spot = lane & 15
    owners = jnp.full(lane.shape, -1, jnp.int32)
    for k in range(slots):
        owners = jnp.where(slot == k, owner[k], owners)
    rank = jnp.zeros(lane.shape, jnp.int32)
    for k in range(slots - 1):
        rank = rank + jnp.where((owners == owner[k]) & (slot > k), 1, 0)
    seat = jnp.where(owners >= 0, rank * 32 + owners, -1)
    on = seat >= 0
    inner = on & (spot >= SHIFT) & (spot < SHIFT + CORE)
    keys[0:1, :] = jnp.where(inner, (spot - SHIFT) * 64 + seat, -1)[0:1]
    outer = jnp.where(spot == SHIFT - 1, seat, jnp.where(spot == SHIFT + CORE, seat + 64, -1))
    keys[1:2, :] = jnp.where(on, outer, -1)[0:1]
    keys[2:8, :] = seat[0:6]


def box_tables(corner, slots, count_z, box_lane, lane_box):
    count = corner.shape[1]
    sources = [corner[0, b] * count_z + lax.div(corner[2, b], slots) for b in range(count)]
    lanes = []
    for b in range(count):
        place = jnp.int32(0)
        for i in range(b):
            place = place + jnp.where(sources[i] == sources[b], 1, 0)
        lanes.append(jnp.minimum(place, 1) * 32 + sources[b])
        box_lane[b] = lanes[b]

    @pl.loop(0, 64)
    def _(lane):
        box = jnp.int32(count)
        for b in range(count):
            box = jnp.where(box_lane[b] == lane, b, box)
        lane_box[lane] = box


def step_kernel(
    owner, corner, coarse, fine,
    base, fine_new, back, gmax, keys,
    fu, chg, chgf, chgl, pflux, pspeed, exy, cxy, cz, rxy, pay_o, pay_c, arr_o, arr_c,
    hy, hz, gx, gy, gz, tops, mine, g_o, g_c, spread, pool, lhs, ghosts, edge_y, edge_z, regs, big, stage,
    ret, by_lane, by_box, box_lane, lane_box,
    in_sem, out_sem, so, ro, sc, rc, sr, rr, hs, hr, ts, tr,
):
    ix, iy, iz = (lax.axis_index(a) for a in ("gx", "gy", "gz"))
    nx, ny, nz = (lax.axis_size(a) for a in ("gx", "gy", "gz"))
    me = ix * nz + iz
    peers = nx * nz
    load_fine = pltpu.make_async_copy(fine, fu, in_sem.at[0])
    load_fine.start()
    barrier = pltpu.get_barrier_semaphore()

    @pl.loop(1, peers)
    def _(s):
        x, z = plane_peer(s, 1)
        pl.semaphore_signal(barrier, inc=1, device_id=(x, iy, z), device_id_type=MESH)

    @pl.loop(1, ny)
    def _(s):
        pl.semaphore_signal(barrier, inc=1, device_id=(ix, lax.rem(iy + s, ny), iz), device_id_type=MESH)

    candidate_keys(owner, keys)
    exy[...] = onehot(keys[0:1, :], 512)
    pack(coarse, keys[1:2, :], exy, pay_o, cxy, cz, rxy)
    pl.semaphore_wait(barrier, peers - 1 + ny - 1)
    old_patch = start_patches(pay_o, arr_o, OUT_BLOCK, 30, so, ro)
    arr_o[block_of(me, OUT_BLOCK, 30), :] = pay_o[block_of(me, OUT_BLOCK, 30), :]

    best = coarse_changes(coarse, keys[2:3, :], chgf, chgl, pflux, pspeed, hy, hz)
    load_fine.wait()

    def fine_plane(p, best):
        u = [fu[f, :, plane_lanes(p)] for f in range(5)]
        return jnp.maximum(best, fastest_of(speeds(u)))

    fine_best = lax.fori_loop(0, BOX, fine_plane, jnp.zeros((16, 256), F32))
    mine[...] = jnp.maximum(best, fold(fine_best))

    def top(s):
        return remote(mine, tops.at[s], ts.at[s], tr.at[s], (ix, lax.rem(iy + s, ny), iz))

    @pl.loop(1, ny)
    def _(s):
        top(s).start()

    pack(chgf, keys[1:2, :], exy, pay_c, cxy, cz, rxy)

    @pl.loop(1, ny)
    def _(s):
        top(s).wait()

    best = mine[...]
    for s in range(1, ny):
        best = jnp.maximum(best, tops[s])
    best = jnp.full((8, 128), jnp.max(best), F32)
    for part in range(4):
        pay_c[pl.ds(part * 8 * OUT_BLOCK + 30, 8, stride=OUT_BLOCK), :] = best
    new_patch = start_patches(pay_c, arr_c, OUT_BLOCK, 31, sc, rc)
    arr_c[block_of(me, OUT_BLOCK, 31), :] = pay_c[block_of(me, OUT_BLOCK, 31), :]
    up_x, down_x = lax.rem(ix + 1, nx), lax.rem(ix + nx - 1, nx)
    up_y, down_y = lax.rem(iy + 1, ny), lax.rem(iy + ny - 1, ny)
    up_z, down_z = lax.rem(iz + 1, nz), lax.rem(iz + nz - 1, nz)
    sides = [
        remote(coarse.at[:, coarse.shape[1] - 1], gx.at[0], hs.at[0], hr.at[0], (up_x, iy, iz)),
        remote(coarse.at[:, 0], gx.at[1], hs.at[1], hr.at[1], (down_x, iy, iz)),
        remote(hy.at[1], gy.at[0], hs.at[2], hr.at[2], (ix, up_y, iz)),
        remote(hy.at[0], gy.at[1], hs.at[3], hr.at[3], (ix, down_y, iz)),
        remote(hz.at[1], gz.at[0], hs.at[4], hr.at[4], (ix, iy, up_z)),
        remote(hz.at[0], gz.at[1], hs.at[5], hr.at[5], (ix, iy, down_z)),
    ]
    for side in sides:
        side.start()

    fine_inner(fu, chg, pflux, pspeed)
    fine_edges(fu, edge_y, edge_z)
    box_tables(corner, owner.shape[0], nz, box_lane, lane_box)
    spread[...] = spread_table()
    pool[...] = pool_table()

    @pl.loop(1, peers)
    def _(s):
        old_patch(s).wait()

    @pl.loop(1, peers)
    def _(s):
        new_patch(s).wait()

    for part in range(4):
        best = jnp.maximum(best, arr_c[pl.ds(part * 8 * OUT_BLOCK + 30, 8, stride=OUT_BLOCK), :])
    gmax[...] = best
    courant = COURANT_NUMBER / jnp.max(best)
    for arr, g in ((arr_o, g_o), (arr_c, g_c)):
        for lane in range(64):
            at = lane % 32 * OUT_BLOCK + lane // 32 * OUT_ROWS
            by_lane[lane] = arr[at : at + OUT_ROWS, :]
        for b in range(16):
            g[pl.ds(b, OUT_ROWS, stride=16), :] = by_lane[box_lane[b]]
    ghosts[...] = fine_ghosts(courant, g_o, g_c, spread, lhs)
    fine_outer(0, fu, chg, edge_y, edge_z, ghosts, regs)
    fine_update(courant, fu, chg, edge_y, edge_z)
    fine_inner(fu, chg, pflux, pspeed)
    fine_edges(fu, edge_y, edge_z)
    fine_outer(1, fu, chg, edge_y, edge_z, ghosts, regs)
    fine_update(courant, fu, chg, edge_y, edge_z)
    fine_results(fu, regs, pool, big, stage)
    for b in range(17):
        by_box[b] = stage[b * STAGE_ROWS : (b + 1) * STAGE_ROWS, :]
    for lane in range(64):
        at = lane % 32 * BACK_BLOCK + lane // 32 * BACK_ROWS
        ret[at : at + BACK_ROWS, :] = by_box[lane_box[lane]][:BACK_ROWS]
    back_patch = start_patches(ret, back, BACK_BLOCK, 70, sr, rr)
    own = pltpu.make_async_copy(
        ret.at[block_of(me, BACK_BLOCK, 70), :], back.at[block_of(me, BACK_BLOCK, 70), :], out_sem.at[0]
    )
    own.start()
    store_fine = pltpu.make_async_copy(fu, fine_new, out_sem.at[1])
    store_fine.start()
    for side in sides:
        side.wait()
    coarse_base(coarse, chgl, courant, gx, gy, gz, hy, hz)
    store_base = pltpu.make_async_copy(chgl, base, out_sem.at[2])
    store_base.start()
    own.wait()
    store_fine.wait()
    store_base.wait()

    @pl.loop(1, peers)
    def _(s):
        back_patch(s).wait()


def apply_kernel(base, keys, arr, gmax, fine, out, fine_out, body, boxes, lxy, lz, dxy, dz, sems):
    nz = base.shape[3]
    load = pltpu.make_async_copy(base, body, sems.at[5])
    load.start()
    load_fine = pltpu.make_async_copy(fine, boxes, sems.at[6])
    load_fine.start()
    courant = COURANT_NUMBER / jnp.max(gmax[...])
    left = lax.broadcasted_iota(jnp.int32, (16, 128), 1) < 64
    left64 = lax.broadcasted_iota(jnp.int32, (64, 128), 1) < 64

    def lanes_of(line):
        return jnp.concatenate(
            [arr[rows_of_lanes(part, BACK_BLOCK, BACK_ROWS, line), :] for part in range(8)], axis=0
        )

    flat = [(f, i) for f in range(5) for i in range(6)]
    for first in range(0, 30, 2):
        pair = flat[first : first + 2]
        turned = jnp.concatenate([lanes_of(f * 7 + i) for f, i in pair], axis=0).T
        for second in range(2):
            pieces = []
            for couple in range(4):
                even = jnp.concatenate(
                    [turned[a * 64 + couple * 16 : a * 64 + couple * 16 + 8] for a in range(2)], axis=0
                )
                odd = jnp.concatenate(
                    [turned[a * 64 + couple * 16 + 8 : a * 64 + couple * 16 + 16] for a in range(2)], axis=0
                )
                if second == 0:
                    pieces.append(jnp.where(left, even, pltpu.roll(odd, 64, 1)))
                else:
                    pieces.append(jnp.where(left, pltpu.roll(even, 64, 1), odd))
            put_split(lxy, (first + second) * 16, 480, jnp.concatenate(pieces, axis=1))
    for f in range(5):
        both = jnp.concatenate([lanes_of(f * 7 + 6), lanes_of(f * 7 + 6)], axis=0).T
        put_split(lz, f * 64, 320, jnp.where(left64, both[:64], both[64:]))
    dxy[...] = sum_split(dot_nn(lxy[...], onehot(keys[0:1, :], 512)))
    dz[...] = sum_split(dot_nn(lz[...], onehot(keys[1:2, :], 128)))
    spot = lax.broadcasted_iota(jnp.int32, (CORE, nz), 1) % BOX
    refined = jnp.broadcast_to(keys[2:3, :], (CORE, nz)) >= 0
    inside = refined & (spot >= SHIFT) & (spot < SHIFT + CORE)
    z_sign = courant * jnp.where(spot == SHIFT - 1, -1.0, jnp.where(spot == SHIFT + CORE, 1.0, 0.0))
    mid = slice(SHIFT, SHIFT + CORE)
    load_fine.wait()
    store_fine = pltpu.make_async_copy(boxes, fine_out, sems.at[7])
    store_fine.start()
    load.wait()
    stores = []
    for f in range(5):
        for side, x, sign in ((0, SHIFT - 1, -1.0), (1, SHIFT + CORE, 1.0)):
            at = (f * 6 + 4) * 16 + side * 8
            body[f, x, mid, :] = body[f, x, mid, :] + (sign * courant) * dxy[at : at + 8, :]
            at = (f * 6 + 5) * 16 + side * 8
            y = x
            for i in range(CORE):
                body[f, SHIFT + i, y : y + 1, :] = (
                    body[f, SHIFT + i, y : y + 1, :] + (sign * courant) * dxy[at + i : at + i + 1, :]
                )
        for i in range(CORE):
            fixed = body[f, SHIFT + i, mid, :] + z_sign * dz[f * 64 + i * 8 : f * 64 + i * 8 + 8, :]
            average = dxy[f * 96 + i * 8 : f * 96 + i * 8 + 8, :]
            body[f, SHIFT + i, mid, :] = jnp.where(inside, average, fixed)
        stores.append(pltpu.make_async_copy(body.at[f], out.at[f], sems.at[f]))
        stores[f].start()
    for store in stores:
        store.wait()
    store_fine.wait()


VMEM = pl.BlockSpec(memory_space=pltpu.VMEM)
SMEM = pl.BlockSpec(memory_space=pltpu.SMEM)
ANY = pl.BlockSpec(memory_space=pl.ANY)


def shape(*dims):
    return jax.ShapeDtypeStruct(dims, F32)


def step_call(owner, corner, coarse, fine):
    peers = lax.axis_size("gx") * lax.axis_size("gz")
    count_y = lax.axis_size("gy")
    _, nx, ny, nz = coarse.shape
    dma = pltpu.SemaphoreType.DMA

    def vmem(*dims, dtype=F32):
        return pltpu.VMEM(dims, dtype)

    return pl.pallas_call(
        step_kernel,
        out_shape=[
            shape(*coarse.shape),
            shape(*fine.shape),
            shape(32 * BACK_BLOCK, 128),
            shape(8, 128),
            jax.ShapeDtypeStruct((8, nz), jnp.int32),
        ],
        in_specs=[SMEM, SMEM, VMEM, ANY],
        out_specs=[ANY, ANY, ANY, VMEM, VMEM],
        scratch_shapes=[
            vmem(*fine.shape),
            vmem(*fine.shape),
            vmem(5, nx, ny, nz),
            vmem(5, nx, ny, nz),
            vmem(5, ny, nz),
            vmem(ny, nz),
            vmem(512, nz, dtype=BF16),
            vmem(480, nz, dtype=BF16),
            vmem(960, nz, dtype=BF16),
            vmem(160, 512),
            *[vmem(32 * OUT_BLOCK, 128)] * 4,
            vmem(2, 5, nx, nz),
            vmem(2, 5, ny, 128),
            vmem(2, 5, ny, nz),
            vmem(2, 5, nx, nz),
            vmem(2, 5, ny, 128),
            vmem(count_y, 8, 128),
            vmem(8, 128),
            vmem(16 * OUT_ROWS, 128),
            vmem(16 * OUT_ROWS, 128),
            vmem(128, 512, dtype=BF16),
            vmem(256, 128, dtype=BF16),
            vmem(1440, 128, dtype=BF16),
            vmem(480, 512),
            vmem(5, 16, 512),
            vmem(5, 16, 512),
            vmem(240, 512),
            vmem(3360, 256, dtype=BF16),
            vmem(17 * STAGE_ROWS, 128),
            vmem(32 * BACK_BLOCK, 128),
            vmem(64, OUT_ROWS, 128),
            vmem(17, STAGE_ROWS, 128),
            pltpu.SMEM((16,), jnp.int32),
            pltpu.SMEM((64,), jnp.int32),
            dma((1,)),
            dma((3,)),
            *[dma((peers,))] * 6,
            dma((6,)),
            dma((6,)),
            dma((count_y,)),
            dma((count_y,)),
        ],
        compiler_params=pltpu.CompilerParams(
            collective_id=0, has_side_effects=True, vmem_limit_bytes=VMEM_LIMIT
        ),
        name="step",
    )(owner, corner, coarse, fine)


def apply_call(base, keys, arr, gmax, fine):
    nz = base.shape[3]
    return pl.pallas_call(
        apply_kernel,
        out_shape=[shape(*base.shape), shape(*fine.shape)],
        in_specs=[ANY, VMEM, VMEM, VMEM, ANY],
        out_specs=[ANY, ANY],
        scratch_shapes=[
            pltpu.VMEM(base.shape, F32),
            pltpu.VMEM(fine.shape, F32),
            pltpu.VMEM((1440, 512), BF16),
            pltpu.VMEM((960, 128), BF16),
            pltpu.VMEM((480, nz), F32),
            pltpu.VMEM((320, nz), F32),
            pltpu.SemaphoreType.DMA((8,)),
        ],
        compiler_params=pltpu.CompilerParams(vmem_limit_bytes=VMEM_LIMIT),
        name="reflux_apply",
    )(base, keys, arr, gmax, fine)


def local(coarse_old, fine_old, slot_owner, box_corner):
    base, fine_new, back, gmax, keys = step_call(
        slot_owner.reshape(-1), box_corner.T, coarse_old, fine_old.transpose(1, 0, 2)
    )
    coarse_new, fine_new = apply_call(base, keys, back, gmax, fine_new)
    return (coarse_new, fine_new.transpose(1, 0, 2))


def solution(mesh):
    in_specs = (
        P(None, "gx", "gy", "gz"),
        P(("gx", "gy", "gz"), None, None),
        P("gx", "gy", "gz"),
        P(("gx", "gy", "gz"), None),
    )
    out_specs = (P(None, "gx", "gy", "gz"), P(("gx", "gy", "gz"), None, None))
    return jax.shard_map(local, mesh=mesh, in_specs=in_specs, out_specs=out_specs, check_vma=False)
```

```python
import jax
import jax.numpy as jnp
from jax import lax
from jax.experimental import pallas as pl
from jax.experimental.pallas import tpu as pltpu
from jax.sharding import PartitionSpec as P

BOX = 16
CORE = 8
SHIFT = 4
HEAT_RATIO = 1.4
COURANT_NUMBER = 0.15
OUT_ROWS = 15
OUT_BLOCK = 32
BACK_ROWS = 35
BACK_BLOCK = 72
STAGE_ROWS = 40
MESH = pl.DeviceIdType.MESH
F32 = jnp.float32
BF16 = jnp.bfloat16
VMEM_LIMIT = 56 * 1024 * 1024


def speeds(u):
    inverse = 1.0 / u[0]
    velocity = [u[1] * inverse, u[2] * inverse, u[3] * inverse]
    kinetic = 0.5 * (u[1] * velocity[0] + u[2] * velocity[1] + u[3] * velocity[2])
    pressure = (HEAT_RATIO - 1.0) * (u[4] - kinetic)
    sound = jnp.sqrt(HEAT_RATIO * pressure * inverse)
    return velocity, pressure, sound


def dirflux(u, prims, d):
    velocity, pressure, sound = prims
    normal = velocity[d]
    flux = [u[1 + d]]
    for m in range(3):
        piece = u[1 + m] * normal
        flux.append(piece + pressure if m == d else piece)
    flux.append((u[4] + pressure) * normal)
    return flux, jnp.abs(normal) + sound


def face(ul, fl, sl, ur, fr, sr):
    half = 0.5 * jnp.maximum(sl, sr)
    return [0.5 * (a + b) - half * (d - c) for a, b, c, d in zip(fl, fr, ul, ur)]


def fastest_of(prims):
    velocity, _, sound = prims
    top = jnp.maximum(jnp.abs(velocity[0]), jnp.abs(velocity[1]))
    return jnp.maximum(top, jnp.abs(velocity[2])) + sound


def fold(top):
    best = None
    for row in range(0, top.shape[0], 8):
        for lane in range(0, top.shape[1], 128):
            tile = top[row : row + 8, lane : lane + 128]
            best = tile if best is None else jnp.maximum(best, tile)
    return best


def split3(x):
    high = x.astype(BF16)
    rest = x - high.astype(F32)
    middle = rest.astype(BF16)
    low = (rest - middle.astype(F32)).astype(BF16)
    return high, middle, low


def put_split(ref, row, count, x):
    for part, piece in enumerate(split3(x)):
        ref[pl.ds(part * count + row, x.shape[0]), :] = piece


def sum_split(product):
    count = product.shape[0] // 3
    return product[:count] + product[count : 2 * count] + product[2 * count :]


def dot_nt(a, b):
    return lax.dot_general(a, b, (((1,), (1,)), ((), ())), preferred_element_type=F32)


def dot_nn(a, b):
    return lax.dot_general(a, b, (((1,), (0,)), ((), ())), preferred_element_type=F32)


def onehot(key_row, rows):
    index = lax.broadcasted_iota(jnp.int32, (rows, key_row.shape[1]), 0)
    return jnp.where(index == key_row, 1.0, 0.0).astype(BF16)


def plane_peer(s, sign):
    count_x, count_z = lax.axis_size("gx"), lax.axis_size("gz")
    x = lax.rem(lax.axis_index("gx") + sign * (s // count_z) + count_x, count_x)
    z = lax.rem(lax.axis_index("gz") + sign * lax.rem(s, count_z) + count_z, count_z)
    return x, z


def remote(src, dst, send, recv, device):
    return pltpu.make_async_remote_copy(
        src_ref=src, dst_ref=dst, send_sem=send, recv_sem=recv, device_id=device, device_id_type=MESH
    )


def rows_of_lanes(part, block, rows, line):
    return pl.ds(part % 4 * 8 * block + part // 4 * rows + line, 8, stride=block)


def block_of(peer, block, rows):
    return pl.ds(pl.multiple_of(peer * block, 8), rows)


def start_patches(pay, arr, block, rows, send, recv):
    iy = lax.axis_index("gy")
    me = lax.axis_index("gx") * lax.axis_size("gz") + lax.axis_index("gz")

    def patch(s):
        x, z = plane_peer(s, 1)
        peer = x * lax.axis_size("gz") + z
        return remote(
            pay.at[block_of(peer, block, rows), :], arr.at[block_of(me, block, rows), :], send.at[s], recv.at[s], (x, iy, z)
        )

    @pl.loop(1, lax.axis_size("gx") * lax.axis_size("gz"))
    def _(s):
        patch(s).start()

    return patch


def pack(fields, keys_z, exy, pay, cxy, cz, rxy):
    outer = (SHIFT - 1, SHIFT + CORE)
    inner = range(SHIFT, SHIFT + CORE)
    for f in range(5):
        on_x = [fields[f, x, SHIFT : SHIFT + CORE, :] for x in outer]
        on_y = [fields[f, x, y : y + 1, :] for y in outer for x in inner]
        put_split(cxy, f * 32, 160, jnp.concatenate(on_x + on_y, axis=0))
        on_z = [fields[f, x, SHIFT : SHIFT + CORE, :] for x in inner]
        put_split(cz, f * 64, 320, jnp.concatenate(on_z, axis=0))
    rxy[...] = sum_split(dot_nt(cxy[...], exy[...]))
    rz = sum_split(dot_nt(cz[...], onehot(keys_z, 128)))
    left = lax.broadcasted_iota(jnp.int32, (8, 128), 1) < 64
    left64 = lax.broadcasted_iota(jnp.int32, (64, 128), 1) < 64

    def put(line, tile):
        for part in range(8):
            pay[rows_of_lanes(part, OUT_BLOCK, OUT_ROWS, line), :] = tile[part * 8 : part * 8 + 8]

    for f in range(5):
        pieces = []
        for side in range(2):
            for j in range(CORE):
                lanes = slice(j // 2 * 128, j // 2 * 128 + 128)
                a = rxy[f * 32 + side * 8 : f * 32 + side * 8 + 8, lanes]
                b = rxy[f * 32 + 16 + side * 8 : f * 32 + 24 + side * 8, lanes]
                if j % 2 == 0:
                    pieces.append(jnp.where(left, a, pltpu.roll(b, 64, 1)))
                else:
                    pieces.append(jnp.where(left, pltpu.roll(a, 64, 1), b))
        turned = jnp.concatenate(pieces, axis=0).T
        put(f * 3, turned[:64])
        put(f * 3 + 1, turned[64:])
        turned = rz[f * 64 : f * 64 + 64]
        turned = jnp.concatenate([turned, turned], axis=0).T
        put(f * 3 + 2, jnp.where(left64, turned[:64], turned[64:]))


def coarse_changes(coarse, refined_row, chgf, chgl, pflux, pspeed, hy, hz):
    nx, ny, nz = coarse.shape[1:]
    row = lax.broadcasted_iota(jnp.int32, (ny, nz), 0)
    lane = lax.broadcasted_iota(jnp.int32, (ny, nz), 1)
    spot = lane % BOX
    refined = jnp.broadcast_to(refined_row, (ny, nz)) >= 0
    row_in = (row >= SHIFT) & (row < SHIFT + CORE)
    lane_in = refined & (spot >= SHIFT) & (spot < SHIFT + CORE)

    def mark(mask):
        return jnp.where(mask, 1.0, 0.0)

    at_x = mark(row_in & lane_in)
    at_y_lo = mark(lane_in & ((row == SHIFT) | (row == SHIFT + CORE)))
    at_y_hi = mark(lane_in & ((row == SHIFT - 1) | (row == SHIFT + CORE - 1)))
    at_z_lo = mark(refined & row_in & ((spot == SHIFT) | (spot == SHIFT + CORE)))
    at_z_hi = mark(refined & row_in & ((spot == SHIFT - 1) | (spot == SHIFT + CORE - 1)))
    keep_row = mark(row > 0)
    keep_lane = mark(lane > 0)
    lane_tile = lax.broadcasted_iota(jnp.int32, (ny, 128), 1)

    def plane(x, best):
        before = jnp.maximum(x - 1, 0)
        u = [coarse[f, x] for f in range(5)]
        prims = speeds(u)
        best = jnp.maximum(best, fastest_of(prims))
        for side, edge in ((0, 0), (1, ny - 1)):
            for f in range(5):
                hy[side, f, pl.ds(x, 1), :] = coarse[f, x, edge : edge + 1, :]
        for side, edge in ((0, 0), (1, nz - 1)):
            for f in range(5):
                column = jnp.broadcast_to(u[f][:, edge : edge + 1], (ny, 128))
                hz[side, f] = jnp.where(lane_tile == x, column, hz[side, f])
        x_inside = jnp.where((x >= SHIFT) & (x < SHIFT + CORE), 1.0, 0.0)
        x_face = jnp.where((x == SHIFT) | (x == SHIFT + CORE), 1.0, 0.0)
        flux, speed = dirflux(u, prims, 0)
        lower = face(
            [coarse[f, before] for f in range(5)], [pflux[f] for f in range(5)], pspeed[...], u, flux, speed
        )
        lower = [jnp.where(x > 0, piece, 0.0) for piece in lower]
        for f in range(5):
            pflux[f] = flux[f]
        pspeed[...] = speed
        keep = 1.0 - x_face * at_x
        lower_l = [piece * keep for piece in lower]
        change = [-piece for piece in lower]
        change_l = [-piece for piece in lower_l]
        for d, axis, size, first, at_lo, at_hi in (
            (1, 0, ny, keep_row, at_y_lo, at_y_hi),
            (2, 1, nz, keep_lane, at_z_lo, at_z_hi),
        ):
            flux, speed = dirflux(u, prims, d)
            ru = [pltpu.roll(piece, 1, axis) for piece in u]
            rf = [ru[1 + d]] + [pltpu.roll(piece, 1, axis) for piece in flux[1:]]
            lo = face(ru, rf, pltpu.roll(speed, 1, axis), u, flux, speed)
            keep_lo = 1.0 - x_inside * at_lo
            keep_hi = 1.0 - x_inside * at_hi
            for f in range(5):
                low = lo[f] * first
                high = pltpu.roll(low, size - 1, axis)
                change[f] = change[f] + (high - low)
                change_l[f] = change_l[f] + (high * keep_hi - low * keep_lo)
        for f in range(5):
            chgf[f, x] = change[f]
            chgl[f, x] = change_l[f]
            chgf[f, before] = chgf[f, before] + lower[f]
            chgl[f, before] = chgl[f, before] + lower_l[f]
        return best

    hz[...] = jnp.zeros_like(hz)
    pflux[...] = jnp.zeros_like(pflux)
    pspeed[...] = jnp.zeros_like(pspeed)
    return fold(lax.fori_loop(0, nx, plane, jnp.zeros((ny, nz), F32)))


def coarse_base(coarse, chgl, courant, gx, gy, gz, hy, hz):
    nx, ny, nz = coarse.shape[1:]

    @pl.loop(0, nx)
    def _(x):
        for f in range(5):
            chgl[f, x] = coarse[f, x] - courant * chgl[f, x]

    def edge(lower, upper, d):
        fl, sl = dirflux(lower, speeds(lower), d)
        fu, su = dirflux(upper, speeds(upper), d)
        return face(lower, fl, sl, upper, fu, su)

    def take(ref, side):
        return [ref[side, f] for f in range(5)]

    low = edge(take(gx, 0), [coarse[f, 0] for f in range(5)], 0)
    high = edge([coarse[f, nx - 1] for f in range(5)], take(gx, 1), 0)
    for f in range(5):
        chgl[f, 0] = chgl[f, 0] + courant * low[f]
        chgl[f, nx - 1] = chgl[f, nx - 1] - courant * high[f]
    low = edge(take(gy, 0), take(hy, 0), 1)
    high = edge(take(hy, 1), take(gy, 1), 1)
    for f in range(5):
        for x in range(nx):
            chgl[f, x, 0:1, :] = chgl[f, x, 0:1, :] + courant * low[f][x : x + 1]
            chgl[f, x, ny - 1 : ny, :] = chgl[f, x, ny - 1 : ny, :] - courant * high[f][x : x + 1]
    tile = lax.broadcasted_iota(jnp.int32, (ny, 128), 1)

    def cells(ref, side):
        return [jnp.where(tile < nx, ref[side, f], 1.0) for f in range(5)]

    low = edge(cells(gz, 0), cells(hz, 0), 2)
    high = edge(cells(hz, 1), cells(gz, 1), 2)
    for f in range(5):
        for x in range(nx):
            add = jnp.broadcast_to(courant * low[f][:, x : x + 1], (ny, 128))
            chgl[f, x, :, 0:128] = chgl[f, x, :, 0:128] + jnp.where(tile == 0, add, 0.0)
            add = jnp.broadcast_to(courant * high[f][:, x : x + 1], (ny, 128))
            chgl[f, x, :, nz - 128 :] = chgl[f, x, :, nz - 128 :] - jnp.where(tile == 127, add, 0.0)


def spread_table():
    cell = lax.broadcasted_iota(jnp.int32, (128, 512), 0)
    lane = lax.broadcasted_iota(jnp.int32, (128, 512), 1)
    wanted = (lane >> 8) * 64 + ((lane & 15) >> 1) * 8 + ((lane >> 5) & 7)
    return jnp.where(cell == wanted, 1.0, 0.0).astype(BF16)


def pool_table():
    lane = lax.broadcasted_iota(jnp.int32, (256, 128), 0)
    cell = lax.broadcasted_iota(jnp.int32, (256, 128), 1) & 63
    wanted = ((lane & 15) >> 1) * 8 + ((lane >> 5) & 7)
    return jnp.where(cell == wanted, 0.125, 0.0).astype(BF16)


def roll_tiles(x, shift):
    return jnp.concatenate([pltpu.roll(x[:, at : at + 128], shift, 1) for at in range(0, x.shape[1], 128)], axis=1)


def plane_lanes(p):
    return pl.ds(pl.multiple_of(p * 256, 256), 256)


def fine_inner(fu, chg, pflux, pspeed):
    lane = lax.broadcasted_iota(jnp.int32, (16, 512), 1)
    inner_y = jnp.where(lane & 255 >= 16, 1.0, 0.0)
    inner_z = jnp.where(lane & 15 != 0, 1.0, 0.0)
    for f in range(5):
        pflux[f, :, 0:256] = jnp.zeros((16, 256), F32)
    pspeed[:, 0:256] = jnp.zeros((16, 256), F32)

    def pair(t, _):
        first = t * 2
        before = jnp.maximum(first - 1, 0)
        both = pl.ds(pl.multiple_of(t * 512, 512), 512)
        u = [fu[f, :, both] for f in range(5)]
        prims = speeds(u)
        flux, speed = dirflux(u, prims, 0)
        lu = [jnp.concatenate([fu[f, :, plane_lanes(before)], u[f][:, :256]], axis=1) for f in range(5)]
        lf = [jnp.concatenate([pflux[f, :, 0:256], flux[f][:, :256]], axis=1) for f in range(5)]
        ls = jnp.concatenate([pspeed[:, 0:256], speed[:, :256]], axis=1)
        lower = face(lu, lf, ls, u, flux, speed)
        one = [jnp.where(t > 0, piece[:, :256], 0.0) for piece in lower]
        two = [piece[:, 256:] for piece in lower]
        for f in range(5):
            pflux[f, :, 0:256] = flux[f][:, 256:]
        pspeed[:, 0:256] = speed[:, 256:]
        change = [jnp.concatenate([b - a, -b], axis=1) for a, b in zip(one, two)]
        for d, shift, keep in ((1, 16, inner_y), (2, 1, inner_z)):

            def turn(x, amount):
                return pltpu.roll(x, amount % 512, 1) if d == 1 else roll_tiles(x, amount % 128)

            flux, speed = dirflux(u, prims, d)
            ru = [turn(piece, shift) for piece in u]
            rf, rs = dirflux(ru, speeds(ru), d)
            low = face(ru, rf, rs, u, flux, speed)
            low = [piece * keep for piece in low]
            change = [c + (turn(b, -shift) - b) for c, b in zip(change, low)]
        for f in range(5):
            chg[f, :, both] = change[f]
            chg[f, :, plane_lanes(before)] = chg[f, :, plane_lanes(before)] + one[f]
        return 0

    lax.fori_loop(0, BOX // 2, pair, 0)


def fine_edges(fu, edge_y, edge_z):
    tile = lax.broadcasted_iota(jnp.int32, (16, 128), 1)

    @pl.loop(0, 5)
    def _(f):
        for side in range(2):
            for block in range(2):
                cells = None
                for seat in range(8):
                    at = (block * 8 + seat) * 256 + side * 128
                    moved = pltpu.roll(fu[f, :, at : at + 128], (seat + side) * 16 % 128, 1)
                    cells = moved if cells is None else jnp.where(tile >> 4 == seat, moved, cells)
                edge_y[f, :, side * 256 + block * 128 : side * 256 + block * 128 + 128] = cells
            for block in range(2):
                cells = None
                for p in range(BOX):
                    at = p * 256 + block * 128
                    moved = pltpu.roll(fu[f, :, at : at + 128], (p + side * 113) % 128, 1)
                    cells = moved if cells is None else jnp.where(tile & 15 == p, moved, cells)
                edge_z[f, :, side * 256 + block * 128 : side * 256 + block * 128 + 128] = cells


def fine_outer(sub, fu, chg, edge_y, edge_z, ghosts, regs):
    last = (BOX - 1) * 256
    for part in range(3):
        for side in range(2):
            lanes = slice(side * 256, side * 256 + 256)
            if part == 0:
                inside = [fu[f, :, side * last : side * last + 256] for f in range(5)]
            else:
                inside = [(edge_y, edge_z)[part - 1][f, :, lanes] for f in range(5)]
            at = part * 80
            outside = [ghosts[at + f * 16 : at + f * 16 + 16, lanes] for f in range(5)]
            lower, upper = (outside, inside) if side == 0 else (inside, outside)
            fl, sl = dirflux(lower, speeds(lower), part)
            fh, sh = dirflux(upper, speeds(upper), part)
            through = face(lower, fl, sl, upper, fh, sh)
            for f in range(5):
                line = (part * 5 + f) * 16
                if sub == 0:
                    regs[line : line + 16, lanes] = through[f]
                else:
                    regs[line : line + 16, lanes] = regs[line : line + 16, lanes] + through[f]
                if part == 0:
                    place = slice(side * last, side * last + 256)
                    chg[f, :, place] = chg[f, :, place] + (through[f] if side else -through[f])
                else:
                    (edge_y, edge_z)[part - 1][f, :, lanes] = through[f] if side else -through[f]


def fine_update(courant, fu, chg, edge_y, edge_z):
    tile = lax.broadcasted_iota(jnp.int32, (16, 128), 1)
    y_side = (tile < 16, tile >= 112)
    z_side = (tile & 15 == 0, tile & 15 == 15)

    @pl.loop(0, BOX, unroll=16)
    def _(p):
        seat = lax.rem(p, 8)
        at = pl.multiple_of(p // 8 * 128, 128)
        y_shift = (lax.rem(128 - seat * 16, 128), 112 - seat * 16)
        z_shift = (lax.rem(128 - p, 128), 15 - p)
        for f in range(5):
            for t in range(2):
                place = pl.ds(pl.multiple_of(p * 256 + t * 128, 128), 128)
                change = chg[f, :, place]
                moved = pltpu.roll(edge_y[f, :, pl.ds(t * 256 + at, 128)], y_shift[t], 1)
                change = change + jnp.where(y_side[t], moved, 0.0)
                for side in range(2):
                    piece = edge_z[f, :, side * 256 + t * 128 : side * 256 + t * 128 + 128]
                    change = change + jnp.where(z_side[side], pltpu.roll(piece, z_shift[side], 1), 0.0)
                fu[f, :, place] = fu[f, :, place] - courant * change


def fine_ghosts(cells, spread, lhs):
    for part in range(3):
        for f in range(5):
            at = (f * 3 + part) * 16
            put_split(lhs, part * 80 + f * 16, 240, cells[at : at + 16, :])
    return sum_split(dot_nn(lhs[...], spread[...]))


def gather_boxes(arr, box_lane, by_lane, g):
    for lane in range(64):
        at = lane % 32 * OUT_BLOCK + lane // 32 * OUT_ROWS
        by_lane[lane] = arr[at : at + OUT_ROWS, :]
    for b in range(16):
        g[pl.ds(b, OUT_ROWS, stride=16), :] = by_lane[box_lane[b]]


def fine_results(fu, regs, pool, big, stage):
    stage[16 * STAGE_ROWS :, :] = jnp.zeros((STAGE_ROWS, 128), F32)
    left = lax.broadcasted_iota(jnp.int32, (16, 128), 1) < 64
    count = 16 * 70
    for f in range(5):
        for x in range(8):
            at = x * 512
            put_split(big, (f * 8 + x) * 16, count, fu[f, :, at : at + 256] + fu[f, :, at + 256 : at + 512])
    for line in range(15):
        for side in range(2):
            piece = regs[line * 16 : line * 16 + 16, side * 256 : side * 256 + 256]
            put_split(big, (40 + line * 2 + side) * 16, count, piece)
    done = sum_split(dot_nn(big[...], pool[...]))

    def put(line, group):
        tile = jnp.where(left, done[group * 16 : group * 16 + 16], done[group * 16 + 16 : group * 16 + 32])
        for half in range(2):
            stage[pl.ds(half * 8 * STAGE_ROWS + line, 8, stride=STAGE_ROWS), :] = tile[half * 8 : half * 8 + 8]

    for f in range(5):
        for i in range(4):
            put(f * 7 + i, f * 8 + 2 * i)
        for part in range(3):
            put(f * 7 + 4 + part, 40 + (part * 5 + f) * 2)
    for line in range(35, STAGE_ROWS):
        for half in range(2):
            stage[pl.ds(half * 8 * STAGE_ROWS + line, 8, stride=STAGE_ROWS), :] = jnp.zeros((8, 128), F32)


def candidate_keys(owner, keys):
    slots = owner.shape[0]
    lane = lax.broadcasted_iota(jnp.int32, (8, slots * BOX), 1)
    slot = lane >> 4
    spot = lane & 15
    owners = jnp.full(lane.shape, -1, jnp.int32)
    for k in range(slots):
        owners = jnp.where(slot == k, owner[k], owners)
    rank = jnp.zeros(lane.shape, jnp.int32)
    for k in range(slots - 1):
        rank = rank + jnp.where((owners == owner[k]) & (slot > k), 1, 0)
    seat = jnp.where(owners >= 0, rank * 32 + owners, -1)
    on = seat >= 0
    inner = on & (spot >= SHIFT) & (spot < SHIFT + CORE)
    keys[0:1, :] = jnp.where(inner, (spot - SHIFT) * 64 + seat, -1)[0:1]
    outer = jnp.where(spot == SHIFT - 1, seat, jnp.where(spot == SHIFT + CORE, seat + 64, -1))
    keys[1:2, :] = jnp.where(on, outer, -1)[0:1]
    keys[2:8, :] = seat[0:6]


def box_tables(corner, slots, count_z, box_lane, lane_box):
    count = corner.shape[1]
    sources = [corner[0, b] * count_z + lax.div(corner[2, b], slots) for b in range(count)]
    lanes = []
    for b in range(count):
        place = jnp.int32(0)
        for i in range(b):
            place = place + jnp.where(sources[i] == sources[b], 1, 0)
        lanes.append(jnp.minimum(place, 1) * 32 + sources[b])
        box_lane[b] = lanes[b]

    @pl.loop(0, 64)
    def _(lane):
        box = jnp.int32(count)
        for b in range(count):
            box = jnp.where(box_lane[b] == lane, b, box)
        lane_box[lane] = box


def step_kernel(
    owner, corner, coarse, fine,
    base, fine_new, back, gmax, keys,
    fu, chg, chgf, chgl, pflux, pspeed, exy, cxy, cz, rxy, pay_o, pay_c, arr_o, arr_c,
    hy, hz, gx, gy, gz, tops, mine, tops_all, mine_all, g_o, g_c, spread, pool, lhs, ghosts, edge_y, edge_z, regs, big, stage,
    ret, by_lane, by_box, box_lane, lane_box,
    in_sem, out_sem, so, ro, sc, rc, sr, rr, us, ur, hs, hr, ts, tr,
):
    ix, iy, iz = (lax.axis_index(a) for a in ("gx", "gy", "gz"))
    nx, ny, nz = (lax.axis_size(a) for a in ("gx", "gy", "gz"))
    me = ix * nz + iz
    peers = nx * nz
    load_fine = pltpu.make_async_copy(fine, fu, in_sem.at[0])
    load_fine.start()
    barrier = pltpu.get_barrier_semaphore()

    @pl.loop(1, peers)
    def _(s):
        x, z = plane_peer(s, 1)
        pl.semaphore_signal(barrier, inc=1, device_id=(x, iy, z), device_id_type=MESH)

    @pl.loop(1, ny)
    def _(s):
        pl.semaphore_signal(barrier, inc=1, device_id=(ix, lax.rem(iy + s, ny), iz), device_id_type=MESH)

    candidate_keys(owner, keys)
    exy[...] = onehot(keys[0:1, :], 512)
    pack(coarse, keys[1:2, :], exy, pay_o, cxy, cz, rxy)
    pl.semaphore_wait(barrier, peers - 1 + ny - 1)
    old_patch = start_patches(pay_o, arr_o, OUT_BLOCK, 30, so, ro)
    arr_o[block_of(me, OUT_BLOCK, 30), :] = pay_o[block_of(me, OUT_BLOCK, 30), :]

    best = coarse_changes(coarse, keys[2:3, :], chgf, chgl, pflux, pspeed, hy, hz)
    load_fine.wait()

    def fine_plane(p, best):
        u = [fu[f, :, plane_lanes(p)] for f in range(5)]
        return jnp.maximum(best, fastest_of(speeds(u)))

    fine_best = lax.fori_loop(0, BOX, fine_plane, jnp.zeros((16, 256), F32))
    mine[...] = jnp.maximum(best, fold(fine_best))

    def top(s):
        return remote(mine, tops.at[s], ts.at[s], tr.at[s], (ix, lax.rem(iy + s, ny), iz))

    @pl.loop(1, ny)
    def _(s):
        top(s).start()

    pack(chgf, keys[1:2, :], exy, pay_c, cxy, cz, rxy)

    @pl.loop(1, ny)
    def _(s):
        top(s).wait()

    best = mine[...]
    for s in range(1, ny):
        best = jnp.maximum(best, tops[s])
    mine_all[...] = jnp.full((1, 128), jnp.max(best), F32)

    def plane_top(s):
        x, z = plane_peer(s, 1)
        return remote(mine_all, tops_all.at[s], us.at[s], ur.at[s], (x, iy, z))

    @pl.loop(1, peers)
    def _(s):
        plane_top(s).start()

    new_patch = start_patches(pay_c, arr_c, OUT_BLOCK, 30, sc, rc)
    arr_c[block_of(me, OUT_BLOCK, 30), :] = pay_c[block_of(me, OUT_BLOCK, 30), :]
    up_x, down_x = lax.rem(ix + 1, nx), lax.rem(ix + nx - 1, nx)
    up_y, down_y = lax.rem(iy + 1, ny), lax.rem(iy + ny - 1, ny)
    up_z, down_z = lax.rem(iz + 1, nz), lax.rem(iz + nz - 1, nz)
    sides = [
        remote(coarse.at[:, coarse.shape[1] - 1], gx.at[0], hs.at[0], hr.at[0], (up_x, iy, iz)),
        remote(coarse.at[:, 0], gx.at[1], hs.at[1], hr.at[1], (down_x, iy, iz)),
        remote(hy.at[1], gy.at[0], hs.at[2], hr.at[2], (ix, up_y, iz)),
        remote(hy.at[0], gy.at[1], hs.at[3], hr.at[3], (ix, down_y, iz)),
        remote(hz.at[1], gz.at[0], hs.at[4], hr.at[4], (ix, iy, up_z)),
        remote(hz.at[0], gz.at[1], hs.at[5], hr.at[5], (ix, iy, down_z)),
    ]
    for side in sides:
        side.start()

    fine_inner(fu, chg, pflux, pspeed)
    fine_edges(fu, edge_y, edge_z)
    box_tables(corner, owner.shape[0], nz, box_lane, lane_box)
    spread[...] = spread_table()
    pool[...] = pool_table()

    @pl.loop(1, peers)
    def _(s):
        old_patch(s).wait()

    gather_boxes(arr_o, box_lane, by_lane, g_o)
    ghosts[...] = fine_ghosts(g_o, spread, lhs)
    fine_outer(0, fu, chg, edge_y, edge_z, ghosts, regs)

    @pl.loop(1, peers)
    def _(s):
        plane_top(s).wait()

    best = mine_all[...]
    for s in range(1, peers):
        best = jnp.maximum(best, tops_all[s])
    fastest = jnp.max(best)
    gmax[...] = jnp.full((8, 128), fastest, F32)
    courant = COURANT_NUMBER / fastest
    fine_update(courant, fu, chg, edge_y, edge_z)
    fine_inner(fu, chg, pflux, pspeed)
    fine_edges(fu, edge_y, edge_z)

    @pl.loop(1, peers)
    def _(s):
        new_patch(s).wait()

    gather_boxes(arr_c, box_lane, by_lane, g_c)
    g_c[...] = 0.5 * (g_o[...] + (g_o[...] - courant * g_c[...]))
    ghosts[...] = fine_ghosts(g_c, spread, lhs)
    fine_outer(1, fu, chg, edge_y, edge_z, ghosts, regs)
    fine_update(courant, fu, chg, edge_y, edge_z)
    fine_results(fu, regs, pool, big, stage)
    for b in range(17):
        by_box[b] = stage[b * STAGE_ROWS : (b + 1) * STAGE_ROWS, :]
    for lane in range(64):
        at = lane % 32 * BACK_BLOCK + lane // 32 * BACK_ROWS
        ret[at : at + BACK_ROWS, :] = by_box[lane_box[lane]][:BACK_ROWS]
    back_patch = start_patches(ret, back, BACK_BLOCK, 70, sr, rr)
    own = pltpu.make_async_copy(
        ret.at[block_of(me, BACK_BLOCK, 70), :], back.at[block_of(me, BACK_BLOCK, 70), :], out_sem.at[0]
    )
    own.start()
    store_fine = pltpu.make_async_copy(fu, fine_new, out_sem.at[1])
    store_fine.start()
    for side in sides:
        side.wait()
    coarse_base(coarse, chgl, courant, gx, gy, gz, hy, hz)
    store_base = pltpu.make_async_copy(chgl, base, out_sem.at[2])
    store_base.start()
    own.wait()
    store_fine.wait()
    store_base.wait()

    @pl.loop(1, peers)
    def _(s):
        back_patch(s).wait()


def apply_kernel(base, keys, arr, gmax, fine, out, fine_out, body, boxes, lxy, lz, dxy, dz, sems):
    nz = base.shape[3]
    load = pltpu.make_async_copy(base, body, sems.at[5])
    load.start()
    load_fine = pltpu.make_async_copy(fine, boxes, sems.at[6])
    load_fine.start()
    courant = COURANT_NUMBER / jnp.max(gmax[...])
    left = lax.broadcasted_iota(jnp.int32, (16, 128), 1) < 64
    left64 = lax.broadcasted_iota(jnp.int32, (64, 128), 1) < 64

    def lanes_of(line):
        return jnp.concatenate(
            [arr[rows_of_lanes(part, BACK_BLOCK, BACK_ROWS, line), :] for part in range(8)], axis=0
        )

    flat = [(f, i) for f in range(5) for i in range(6)]
    for first in range(0, 30, 2):
        pair = flat[first : first + 2]
        turned = jnp.concatenate([lanes_of(f * 7 + i) for f, i in pair], axis=0).T
        for second in range(2):
            pieces = []
            for couple in range(4):
                even = jnp.concatenate(
                    [turned[a * 64 + couple * 16 : a * 64 + couple * 16 + 8] for a in range(2)], axis=0
                )
                odd = jnp.concatenate(
                    [turned[a * 64 + couple * 16 + 8 : a * 64 + couple * 16 + 16] for a in range(2)], axis=0
                )
                if second == 0:
                    pieces.append(jnp.where(left, even, pltpu.roll(odd, 64, 1)))
                else:
                    pieces.append(jnp.where(left, pltpu.roll(even, 64, 1), odd))
            put_split(lxy, (first + second) * 16, 480, jnp.concatenate(pieces, axis=1))
    for f in range(5):
        both = jnp.concatenate([lanes_of(f * 7 + 6), lanes_of(f * 7 + 6)], axis=0).T
        put_split(lz, f * 64, 320, jnp.where(left64, both[:64], both[64:]))
    dxy[...] = sum_split(dot_nn(lxy[...], onehot(keys[0:1, :], 512)))
    dz[...] = sum_split(dot_nn(lz[...], onehot(keys[1:2, :], 128)))
    spot = lax.broadcasted_iota(jnp.int32, (CORE, nz), 1) % BOX
    refined = jnp.broadcast_to(keys[2:3, :], (CORE, nz)) >= 0
    inside = refined & (spot >= SHIFT) & (spot < SHIFT + CORE)
    z_sign = courant * jnp.where(spot == SHIFT - 1, -1.0, jnp.where(spot == SHIFT + CORE, 1.0, 0.0))
    mid = slice(SHIFT, SHIFT + CORE)
    load_fine.wait()
    store_fine = pltpu.make_async_copy(boxes, fine_out, sems.at[7])
    store_fine.start()
    load.wait()
    stores = []
    for f in range(5):
        for side, x, sign in ((0, SHIFT - 1, -1.0), (1, SHIFT + CORE, 1.0)):
            at = (f * 6 + 4) * 16 + side * 8
            body[f, x, mid, :] = body[f, x, mid, :] + (sign * courant) * dxy[at : at + 8, :]
            at = (f * 6 + 5) * 16 + side * 8
            y = x
            for i in range(CORE):
                body[f, SHIFT + i, y : y + 1, :] = (
                    body[f, SHIFT + i, y : y + 1, :] + (sign * courant) * dxy[at + i : at + i + 1, :]
                )
        for i in range(CORE):
            fixed = body[f, SHIFT + i, mid, :] + z_sign * dz[f * 64 + i * 8 : f * 64 + i * 8 + 8, :]
            average = dxy[f * 96 + i * 8 : f * 96 + i * 8 + 8, :]
            body[f, SHIFT + i, mid, :] = jnp.where(inside, average, fixed)
        stores.append(pltpu.make_async_copy(body.at[f], out.at[f], sems.at[f]))
        stores[f].start()
    for store in stores:
        store.wait()
    store_fine.wait()


VMEM = pl.BlockSpec(memory_space=pltpu.VMEM)
SMEM = pl.BlockSpec(memory_space=pltpu.SMEM)
ANY = pl.BlockSpec(memory_space=pl.ANY)


def shape(*dims):
    return jax.ShapeDtypeStruct(dims, F32)


def step_call(owner, corner, coarse, fine):
    peers = lax.axis_size("gx") * lax.axis_size("gz")
    count_y = lax.axis_size("gy")
    _, nx, ny, nz = coarse.shape
    dma = pltpu.SemaphoreType.DMA

    def vmem(*dims, dtype=F32):
        return pltpu.VMEM(dims, dtype)

    return pl.pallas_call(
        step_kernel,
        out_shape=[
            shape(*coarse.shape),
            shape(*fine.shape),
            shape(32 * BACK_BLOCK, 128),
            shape(8, 128),
            jax.ShapeDtypeStruct((8, nz), jnp.int32),
        ],
        in_specs=[SMEM, SMEM, VMEM, ANY],
        out_specs=[ANY, ANY, ANY, VMEM, VMEM],
        scratch_shapes=[
            vmem(*fine.shape),
            vmem(*fine.shape),
            vmem(5, nx, ny, nz),
            vmem(5, nx, ny, nz),
            vmem(5, ny, nz),
            vmem(ny, nz),
            vmem(512, nz, dtype=BF16),
            vmem(480, nz, dtype=BF16),
            vmem(960, nz, dtype=BF16),
            vmem(160, 512),
            *[vmem(32 * OUT_BLOCK, 128)] * 4,
            vmem(2, 5, nx, nz),
            vmem(2, 5, ny, 128),
            vmem(2, 5, ny, nz),
            vmem(2, 5, nx, nz),
            vmem(2, 5, ny, 128),
            vmem(count_y, 8, 128),
            vmem(8, 128),
            vmem(peers, 1, 128),
            vmem(1, 128),
            vmem(16 * OUT_ROWS, 128),
            vmem(16 * OUT_ROWS, 128),
            vmem(128, 512, dtype=BF16),
            vmem(256, 128, dtype=BF16),
            vmem(720, 128, dtype=BF16),
            vmem(240, 512),
            vmem(5, 16, 512),
            vmem(5, 16, 512),
            vmem(240, 512),
            vmem(3360, 256, dtype=BF16),
            vmem(17 * STAGE_ROWS, 128),
            vmem(32 * BACK_BLOCK, 128),
            vmem(64, OUT_ROWS, 128),
            vmem(17, STAGE_ROWS, 128),
            pltpu.SMEM((16,), jnp.int32),
            pltpu.SMEM((64,), jnp.int32),
            dma((1,)),
            dma((3,)),
            *[dma((peers,))] * 8,
            dma((6,)),
            dma((6,)),
            dma((count_y,)),
            dma((count_y,)),
        ],
        compiler_params=pltpu.CompilerParams(
            collective_id=0, has_side_effects=True, vmem_limit_bytes=VMEM_LIMIT
        ),
        name="step",
    )(owner, corner, coarse, fine)


def apply_call(base, keys, arr, gmax, fine):
    nz = base.shape[3]
    return pl.pallas_call(
        apply_kernel,
        out_shape=[shape(*base.shape), shape(*fine.shape)],
        in_specs=[ANY, VMEM, VMEM, VMEM, ANY],
        out_specs=[ANY, ANY],
        scratch_shapes=[
            pltpu.VMEM(base.shape, F32),
            pltpu.VMEM(fine.shape, F32),
            pltpu.VMEM((1440, 512), BF16),
            pltpu.VMEM((960, 128), BF16),
            pltpu.VMEM((480, nz), F32),
            pltpu.VMEM((320, nz), F32),
            pltpu.SemaphoreType.DMA((8,)),
        ],
        compiler_params=pltpu.CompilerParams(vmem_limit_bytes=VMEM_LIMIT),
        name="reflux_apply",
    )(base, keys, arr, gmax, fine)


def local(coarse_old, fine_old, slot_owner, box_corner):
    base, fine_new, back, gmax, keys = step_call(
        slot_owner.reshape(-1), box_corner.T, coarse_old, fine_old.transpose(1, 0, 2)
    )
    coarse_new, fine_new = apply_call(base, keys, back, gmax, fine_new)
    return (coarse_new, fine_new.transpose(1, 0, 2))


def solution(mesh):
    in_specs = (
        P(None, "gx", "gy", "gz"),
        P(("gx", "gy", "gz"), None, None),
        P("gx", "gy", "gz"),
        P(("gx", "gy", "gz"), None),
    )
    out_specs = (P(None, "gx", "gy", "gz"), P(("gx", "gy", "gz"), None, None))
    return jax.shard_map(local, mesh=mesh, in_specs=in_specs, out_specs=out_specs, check_vma=False)
```

```python
import jax
import jax.numpy as jnp
from jax import lax
from jax.experimental import pallas as pl
from jax.experimental.pallas import tpu as pltpu
from jax.sharding import PartitionSpec as P

BOX = 16
CORE = 8
SHIFT = 4
HEAT_RATIO = 1.4
COURANT_NUMBER = 0.15
OUT_ROWS = 15
OUT_BLOCK = 32
BACK_ROWS = 35
BACK_BLOCK = 72
STAGE_ROWS = 40
MESH = pl.DeviceIdType.MESH
F32 = jnp.float32
BF16 = jnp.bfloat16
VMEM_LIMIT = 56 * 1024 * 1024


def speeds(u):
    inverse = 1.0 / u[0]
    velocity = [u[1] * inverse, u[2] * inverse, u[3] * inverse]
    kinetic = 0.5 * (u[1] * velocity[0] + u[2] * velocity[1] + u[3] * velocity[2])
    pressure = (HEAT_RATIO - 1.0) * (u[4] - kinetic)
    sound = jnp.sqrt(HEAT_RATIO * pressure * inverse)
    return velocity, pressure, sound


def dirflux(u, prims, d):
    velocity, pressure, sound = prims
    normal = velocity[d]
    flux = [u[1 + d]]
    for m in range(3):
        piece = u[1 + m] * normal
        flux.append(piece + pressure if m == d else piece)
    flux.append((u[4] + pressure) * normal)
    return flux, jnp.abs(normal) + sound


def face(ul, fl, sl, ur, fr, sr):
    half = 0.5 * jnp.maximum(sl, sr)
    return [0.5 * (a + b) - half * (d - c) for a, b, c, d in zip(fl, fr, ul, ur)]


def fastest_of(prims):
    velocity, _, sound = prims
    top = jnp.maximum(jnp.abs(velocity[0]), jnp.abs(velocity[1]))
    return jnp.maximum(top, jnp.abs(velocity[2])) + sound


def fold(top):
    best = None
    for row in range(0, top.shape[0], 8):
        for lane in range(0, top.shape[1], 128):
            tile = top[row : row + 8, lane : lane + 128]
            best = tile if best is None else jnp.maximum(best, tile)
    return best


def split3(x):
    high = x.astype(BF16)
    rest = x - high.astype(F32)
    middle = rest.astype(BF16)
    low = (rest - middle.astype(F32)).astype(BF16)
    return high, middle, low


def put_split(ref, row, count, x):
    for part, piece in enumerate(split3(x)):
        ref[pl.ds(part * count + row, x.shape[0]), :] = piece


def sum_split(product):
    count = product.shape[0] // 3
    return product[:count] + product[count : 2 * count] + product[2 * count :]


def dot_nt(a, b):
    return lax.dot_general(a, b, (((1,), (1,)), ((), ())), preferred_element_type=F32)


def dot_nn(a, b):
    return lax.dot_general(a, b, (((1,), (0,)), ((), ())), preferred_element_type=F32)


def onehot(key_row, rows):
    index = lax.broadcasted_iota(jnp.int32, (rows, key_row.shape[1]), 0)
    return jnp.where(index == key_row, 1.0, 0.0).astype(BF16)


def plane_peer(s, sign):
    count_x, count_z = lax.axis_size("gx"), lax.axis_size("gz")
    x = lax.rem(lax.axis_index("gx") + sign * (s // count_z) + count_x, count_x)
    z = lax.rem(lax.axis_index("gz") + sign * lax.rem(s, count_z) + count_z, count_z)
    return x, z


def remote(src, dst, send, recv, device):
    return pltpu.make_async_remote_copy(
        src_ref=src, dst_ref=dst, send_sem=send, recv_sem=recv, device_id=device, device_id_type=MESH
    )


def rows_of_lanes(part, block, rows, line):
    return pl.ds(part % 4 * 8 * block + part // 4 * rows + line, 8, stride=block)


def block_of(peer, block, rows):
    return pl.ds(pl.multiple_of(peer * block, 8), rows)


def start_patches(pay, arr, block, rows, send, recv):
    iy = lax.axis_index("gy")
    me = lax.axis_index("gx") * lax.axis_size("gz") + lax.axis_index("gz")

    def patch(s):
        x, z = plane_peer(s, 1)
        peer = x * lax.axis_size("gz") + z
        return remote(
            pay.at[block_of(peer, block, rows), :], arr.at[block_of(me, block, rows), :], send.at[s], recv.at[s], (x, iy, z)
        )

    @pl.loop(1, lax.axis_size("gx") * lax.axis_size("gz"))
    def _(s):
        patch(s).start()

    return patch


def pack(fields, keys_z, exy, pay, cxy, cz, rxy):
    outer = (SHIFT - 1, SHIFT + CORE)
    inner = range(SHIFT, SHIFT + CORE)
    for f in range(5):
        on_x = [fields[f, x, SHIFT : SHIFT + CORE, :] for x in outer]
        on_y = [fields[f, x, y : y + 1, :] for y in outer for x in inner]
        put_split(cxy, f * 32, 160, jnp.concatenate(on_x + on_y, axis=0))
        on_z = [fields[f, x, SHIFT : SHIFT + CORE, :] for x in inner]
        put_split(cz, f * 64, 320, jnp.concatenate(on_z, axis=0))
    rxy[...] = sum_split(dot_nt(cxy[...], exy[...]))
    rz = sum_split(dot_nt(cz[...], onehot(keys_z, 128)))
    left = lax.broadcasted_iota(jnp.int32, (8, 128), 1) < 64
    left64 = lax.broadcasted_iota(jnp.int32, (64, 128), 1) < 64

    def put(line, tile):
        for part in range(8):
            pay[rows_of_lanes(part, OUT_BLOCK, OUT_ROWS, line), :] = tile[part * 8 : part * 8 + 8]

    for f in range(5):
        pieces = []
        for side in range(2):
            for j in range(CORE):
                lanes = slice(j // 2 * 128, j // 2 * 128 + 128)
                a = rxy[f * 32 + side * 8 : f * 32 + side * 8 + 8, lanes]
                b = rxy[f * 32 + 16 + side * 8 : f * 32 + 24 + side * 8, lanes]
                if j % 2 == 0:
                    pieces.append(jnp.where(left, a, pltpu.roll(b, 64, 1)))
                else:
                    pieces.append(jnp.where(left, pltpu.roll(a, 64, 1), b))
        turned = jnp.concatenate(pieces, axis=0).T
        put(f * 3, turned[:64])
        put(f * 3 + 1, turned[64:])
        turned = rz[f * 64 : f * 64 + 64]
        turned = jnp.concatenate([turned, turned], axis=0).T
        put(f * 3 + 2, jnp.where(left64, turned[:64], turned[64:]))


def coarse_changes(coarse, refined_row, chgf, chgl, pflux, pspeed, hy, hz):
    nx, ny, nz = coarse.shape[1:]
    row = lax.broadcasted_iota(jnp.int32, (ny, nz), 0)
    lane = lax.broadcasted_iota(jnp.int32, (ny, nz), 1)
    spot = lane % BOX
    refined = jnp.broadcast_to(refined_row, (ny, nz)) >= 0
    row_in = (row >= SHIFT) & (row < SHIFT + CORE)
    lane_in = refined & (spot >= SHIFT) & (spot < SHIFT + CORE)

    def mark(mask):
        return jnp.where(mask, 1.0, 0.0)

    at_x = mark(row_in & lane_in)
    at_y_lo = mark(lane_in & ((row == SHIFT) | (row == SHIFT + CORE)))
    at_y_hi = mark(lane_in & ((row == SHIFT - 1) | (row == SHIFT + CORE - 1)))
    at_z_lo = mark(refined & row_in & ((spot == SHIFT) | (spot == SHIFT + CORE)))
    at_z_hi = mark(refined & row_in & ((spot == SHIFT - 1) | (spot == SHIFT + CORE - 1)))
    keep_row = mark(row > 0)
    keep_lane = mark(lane > 0)
    lane_tile = lax.broadcasted_iota(jnp.int32, (ny, 128), 1)

    def plane(x, best):
        before = jnp.maximum(x - 1, 0)
        u = [coarse[f, x] for f in range(5)]
        prims = speeds(u)
        best = jnp.maximum(best, fastest_of(prims))
        for side, edge in ((0, 0), (1, ny - 1)):
            for f in range(5):
                hy[side, f, pl.ds(x, 1), :] = coarse[f, x, edge : edge + 1, :]
        for side, edge in ((0, 0), (1, nz - 1)):
            for f in range(5):
                column = jnp.broadcast_to(u[f][:, edge : edge + 1], (ny, 128))
                hz[side, f] = jnp.where(lane_tile == x, column, hz[side, f])
        x_inside = jnp.where((x >= SHIFT) & (x < SHIFT + CORE), 1.0, 0.0)
        x_face = jnp.where((x == SHIFT) | (x == SHIFT + CORE), 1.0, 0.0)
        flux, speed = dirflux(u, prims, 0)
        lower = face(
            [coarse[f, before] for f in range(5)], [pflux[f] for f in range(5)], pspeed[...], u, flux, speed
        )
        lower = [jnp.where(x > 0, piece, 0.0) for piece in lower]
        for f in range(5):
            pflux[f] = flux[f]
        pspeed[...] = speed
        keep = 1.0 - x_face * at_x
        lower_l = [piece * keep for piece in lower]
        change = [-piece for piece in lower]
        change_l = [-piece for piece in lower_l]
        for d, axis, size, first, at_lo, at_hi in (
            (1, 0, ny, keep_row, at_y_lo, at_y_hi),
            (2, 1, nz, keep_lane, at_z_lo, at_z_hi),
        ):
            flux, speed = dirflux(u, prims, d)
            ru = [pltpu.roll(piece, 1, axis) for piece in u]
            rf = [ru[1 + d]] + [pltpu.roll(piece, 1, axis) for piece in flux[1:]]
            lo = face(ru, rf, pltpu.roll(speed, 1, axis), u, flux, speed)
            keep_lo = 1.0 - x_inside * at_lo
            keep_hi = 1.0 - x_inside * at_hi
            for f in range(5):
                low = lo[f] * first
                high = pltpu.roll(low, size - 1, axis)
                change[f] = change[f] + (high - low)
                change_l[f] = change_l[f] + (high * keep_hi - low * keep_lo)
        for f in range(5):
            chgf[f, x] = change[f]
            chgl[f, x] = change_l[f]
            chgf[f, before] = chgf[f, before] + lower[f]
            chgl[f, before] = chgl[f, before] + lower_l[f]
        return best

    hz[...] = jnp.zeros_like(hz)
    pflux[...] = jnp.zeros_like(pflux)
    pspeed[...] = jnp.zeros_like(pspeed)
    return fold(lax.fori_loop(0, nx, plane, jnp.zeros((ny, nz), F32)))


def coarse_base(coarse, chgl, courant, gx, gy, gz, hy, hz):
    nx, ny, nz = coarse.shape[1:]

    @pl.loop(0, nx)
    def _(x):
        for f in range(5):
            chgl[f, x] = coarse[f, x] - courant * chgl[f, x]

    def edge(lower, upper, d):
        fl, sl = dirflux(lower, speeds(lower), d)
        fu, su = dirflux(upper, speeds(upper), d)
        return face(lower, fl, sl, upper, fu, su)

    def take(ref, side):
        return [ref[side, f] for f in range(5)]

    low = edge(take(gx, 0), [coarse[f, 0] for f in range(5)], 0)
    high = edge([coarse[f, nx - 1] for f in range(5)], take(gx, 1), 0)
    for f in range(5):
        chgl[f, 0] = chgl[f, 0] + courant * low[f]
        chgl[f, nx - 1] = chgl[f, nx - 1] - courant * high[f]
    low = edge(take(gy, 0), take(hy, 0), 1)
    high = edge(take(hy, 1), take(gy, 1), 1)
    for f in range(5):
        for x in range(nx):
            chgl[f, x, 0:1, :] = chgl[f, x, 0:1, :] + courant * low[f][x : x + 1]
            chgl[f, x, ny - 1 : ny, :] = chgl[f, x, ny - 1 : ny, :] - courant * high[f][x : x + 1]
    tile = lax.broadcasted_iota(jnp.int32, (ny, 128), 1)

    def cells(ref, side):
        return [jnp.where(tile < nx, ref[side, f], 1.0) for f in range(5)]

    low = edge(cells(gz, 0), cells(hz, 0), 2)
    high = edge(cells(hz, 1), cells(gz, 1), 2)
    for f in range(5):
        for x in range(nx):
            add = jnp.broadcast_to(courant * low[f][:, x : x + 1], (ny, 128))
            chgl[f, x, :, 0:128] = chgl[f, x, :, 0:128] + jnp.where(tile == 0, add, 0.0)
            add = jnp.broadcast_to(courant * high[f][:, x : x + 1], (ny, 128))
            chgl[f, x, :, nz - 128 :] = chgl[f, x, :, nz - 128 :] - jnp.where(tile == 127, add, 0.0)


def spread_table():
    cell = lax.broadcasted_iota(jnp.int32, (128, 512), 0)
    lane = lax.broadcasted_iota(jnp.int32, (128, 512), 1)
    wanted = (lane >> 8) * 64 + ((lane & 15) >> 1) * 8 + ((lane >> 5) & 7)
    return jnp.where(cell == wanted, 1.0, 0.0).astype(BF16)


def pool_table():
    lane = lax.broadcasted_iota(jnp.int32, (256, 128), 0)
    cell = lax.broadcasted_iota(jnp.int32, (256, 128), 1) & 63
    wanted = ((lane & 15) >> 1) * 8 + ((lane >> 5) & 7)
    return jnp.where(cell == wanted, 0.125, 0.0).astype(BF16)


def roll_tiles(x, shift):
    return jnp.concatenate([pltpu.roll(x[:, at : at + 128], shift, 1) for at in range(0, x.shape[1], 128)], axis=1)


def plane_lanes(p):
    return pl.ds(pl.multiple_of(p * 256, 256), 256)


def fine_inner(fu, chg, pflux, pspeed):
    lane = lax.broadcasted_iota(jnp.int32, (16, 512), 1)
    inner_y = jnp.where(lane & 255 >= 16, 1.0, 0.0)
    inner_z = jnp.where(lane & 15 != 0, 1.0, 0.0)
    for f in range(5):
        pflux[f, :, 0:256] = jnp.zeros((16, 256), F32)
    pspeed[:, 0:256] = jnp.zeros((16, 256), F32)

    def pair(t, _):
        first = t * 2
        before = jnp.maximum(first - 1, 0)
        both = pl.ds(pl.multiple_of(t * 512, 512), 512)
        u = [fu[f, :, both] for f in range(5)]
        prims = speeds(u)
        flux, speed = dirflux(u, prims, 0)
        lu = [jnp.concatenate([fu[f, :, plane_lanes(before)], u[f][:, :256]], axis=1) for f in range(5)]
        lf = [jnp.concatenate([pflux[f, :, 0:256], flux[f][:, :256]], axis=1) for f in range(5)]
        ls = jnp.concatenate([pspeed[:, 0:256], speed[:, :256]], axis=1)
        lower = face(lu, lf, ls, u, flux, speed)
        one = [jnp.where(t > 0, piece[:, :256], 0.0) for piece in lower]
        two = [piece[:, 256:] for piece in lower]
        for f in range(5):
            pflux[f, :, 0:256] = flux[f][:, 256:]
        pspeed[:, 0:256] = speed[:, 256:]
        change = [jnp.concatenate([b - a, -b], axis=1) for a, b in zip(one, two)]
        for d, shift, keep in ((1, 16, inner_y), (2, 1, inner_z)):

            def turn(x, amount):
                return pltpu.roll(x, amount % 512, 1) if d == 1 else roll_tiles(x, amount % 128)

            flux, speed = dirflux(u, prims, d)
            ru = [turn(piece, shift) for piece in u]
            rf, rs = dirflux(ru, speeds(ru), d)
            low = face(ru, rf, rs, u, flux, speed)
            low = [piece * keep for piece in low]
            change = [c + (turn(b, -shift) - b) for c, b in zip(change, low)]
        for f in range(5):
            chg[f, :, both] = change[f]
            chg[f, :, plane_lanes(before)] = chg[f, :, plane_lanes(before)] + one[f]
        return 0

    lax.fori_loop(0, BOX // 2, pair, 0)


def fine_edges(fu, edge_y, edge_z):
    tile = lax.broadcasted_iota(jnp.int32, (16, 128), 1)

    @pl.loop(0, 5)
    def _(f):
        for side in range(2):
            for block in range(2):
                cells = None
                for seat in range(8):
                    at = (block * 8 + seat) * 256 + side * 128
                    moved = pltpu.roll(fu[f, :, at : at + 128], (seat + side) * 16 % 128, 1)
                    cells = moved if cells is None else jnp.where(tile >> 4 == seat, moved, cells)
                edge_y[f, :, side * 256 + block * 128 : side * 256 + block * 128 + 128] = cells
            for block in range(2):
                cells = None
                for p in range(BOX):
                    at = p * 256 + block * 128
                    moved = pltpu.roll(fu[f, :, at : at + 128], (p + side * 113) % 128, 1)
                    cells = moved if cells is None else jnp.where(tile & 15 == p, moved, cells)
                edge_z[f, :, side * 256 + block * 128 : side * 256 + block * 128 + 128] = cells


def fine_outer(sub, fu, chg, edge_y, edge_z, ghosts, regs):
    last = (BOX - 1) * 256
    for part in range(3):
        for side in range(2):
            lanes = slice(side * 256, side * 256 + 256)
            if part == 0:
                inside = [fu[f, :, side * last : side * last + 256] for f in range(5)]
            else:
                inside = [(edge_y, edge_z)[part - 1][f, :, lanes] for f in range(5)]
            at = part * 80
            outside = [ghosts[at + f * 16 : at + f * 16 + 16, lanes] for f in range(5)]
            lower, upper = (outside, inside) if side == 0 else (inside, outside)
            fl, sl = dirflux(lower, speeds(lower), part)
            fh, sh = dirflux(upper, speeds(upper), part)
            through = face(lower, fl, sl, upper, fh, sh)
            for f in range(5):
                line = (part * 5 + f) * 16
                if sub == 0:
                    regs[line : line + 16, lanes] = through[f]
                else:
                    regs[line : line + 16, lanes] = regs[line : line + 16, lanes] + through[f]
                if part == 0:
                    place = slice(side * last, side * last + 256)
                    chg[f, :, place] = chg[f, :, place] + (through[f] if side else -through[f])
                else:
                    (edge_y, edge_z)[part - 1][f, :, lanes] = through[f] if side else -through[f]


def fine_update(courant, fu, chg, edge_y, edge_z):
    tile = lax.broadcasted_iota(jnp.int32, (16, 128), 1)
    y_side = (tile < 16, tile >= 112)
    z_side = (tile & 15 == 0, tile & 15 == 15)

    @pl.loop(0, BOX, unroll=16)
    def _(p):
        seat = lax.rem(p, 8)
        at = pl.multiple_of(p // 8 * 128, 128)
        y_shift = (lax.rem(128 - seat * 16, 128), 112 - seat * 16)
        z_shift = (lax.rem(128 - p, 128), 15 - p)
        for f in range(5):
            for t in range(2):
                place = pl.ds(pl.multiple_of(p * 256 + t * 128, 128), 128)
                change = chg[f, :, place]
                moved = pltpu.roll(edge_y[f, :, pl.ds(t * 256 + at, 128)], y_shift[t], 1)
                change = change + jnp.where(y_side[t], moved, 0.0)
                for side in range(2):
                    piece = edge_z[f, :, side * 256 + t * 128 : side * 256 + t * 128 + 128]
                    change = change + jnp.where(z_side[side], pltpu.roll(piece, z_shift[side], 1), 0.0)
                fu[f, :, place] = fu[f, :, place] - courant * change


def fine_ghosts(cells, spread, lhs):
    for part in range(3):
        for f in range(5):
            at = (f * 3 + part) * 16
            put_split(lhs, part * 80 + f * 16, 240, cells[at : at + 16, :])
    return sum_split(dot_nn(lhs[...], spread[...]))


def gather_boxes(arr, box_lane, by_lane, g):
    for lane in range(64):
        at = lane % 32 * OUT_BLOCK + lane // 32 * OUT_ROWS
        by_lane[lane] = arr[at : at + OUT_ROWS, :]
    for b in range(16):
        g[pl.ds(b, OUT_ROWS, stride=16), :] = by_lane[box_lane[b]]


def fine_results(fu, regs, pool, big, stage):
    stage[16 * STAGE_ROWS :, :] = jnp.zeros((STAGE_ROWS, 128), F32)
    left = lax.broadcasted_iota(jnp.int32, (16, 128), 1) < 64
    count = 16 * 70
    for f in range(5):
        for x in range(8):
            at = x * 512
            put_split(big, (f * 8 + x) * 16, count, fu[f, :, at : at + 256] + fu[f, :, at + 256 : at + 512])
    for line in range(15):
        for side in range(2):
            piece = regs[line * 16 : line * 16 + 16, side * 256 : side * 256 + 256]
            put_split(big, (40 + line * 2 + side) * 16, count, piece)
    done = sum_split(dot_nn(big[...], pool[...]))

    def put(line, group):
        tile = jnp.where(left, done[group * 16 : group * 16 + 16], done[group * 16 + 16 : group * 16 + 32])
        for half in range(2):
            stage[pl.ds(half * 8 * STAGE_ROWS + line, 8, stride=STAGE_ROWS), :] = tile[half * 8 : half * 8 + 8]

    for f in range(5):
        for i in range(4):
            put(f * 7 + i, f * 8 + 2 * i)
        for part in range(3):
            put(f * 7 + 4 + part, 40 + (part * 5 + f) * 2)
    for line in range(35, STAGE_ROWS):
        for half in range(2):
            stage[pl.ds(half * 8 * STAGE_ROWS + line, 8, stride=STAGE_ROWS), :] = jnp.zeros((8, 128), F32)


def candidate_keys(owner, keys):
    slots = owner.shape[0]
    lane = lax.broadcasted_iota(jnp.int32, (8, slots * BOX), 1)
    slot = lane >> 4
    spot = lane & 15
    owners = jnp.full(lane.shape, -1, jnp.int32)
    for k in range(slots):
        owners = jnp.where(slot == k, owner[k], owners)
    rank = jnp.zeros(lane.shape, jnp.int32)
    for k in range(slots - 1):
        rank = rank + jnp.where((owners == owner[k]) & (slot > k), 1, 0)
    seat = jnp.where(owners >= 0, rank * 32 + owners, -1)
    on = seat >= 0
    inner = on & (spot >= SHIFT) & (spot < SHIFT + CORE)
    keys[0:1, :] = jnp.where(inner, (spot - SHIFT) * 64 + seat, -1)[0:1]
    outer = jnp.where(spot == SHIFT - 1, seat, jnp.where(spot == SHIFT + CORE, seat + 64, -1))
    keys[1:2, :] = jnp.where(on, outer, -1)[0:1]
    keys[2:8, :] = seat[0:6]


def box_tables(corner, slots, count_z, box_lane, lane_box):
    count = corner.shape[1]
    sources = [corner[0, b] * count_z + lax.div(corner[2, b], slots) for b in range(count)]
    lanes = []
    for b in range(count):
        place = jnp.int32(0)
        for i in range(b):
            place = place + jnp.where(sources[i] == sources[b], 1, 0)
        lanes.append(jnp.minimum(place, 1) * 32 + sources[b])
        box_lane[b] = lanes[b]

    @pl.loop(0, 64)
    def _(lane):
        box = jnp.int32(count)
        for b in range(count):
            box = jnp.where(box_lane[b] == lane, b, box)
        lane_box[lane] = box


def step_kernel(
    owner, corner, coarse, fine,
    base, fine_new, back, gmax, keys,
    fu, chg, chgf, chgl, pflux, pspeed, exy, cxy, cz, rxy, pay_o, pay_c, arr_o, arr_c,
    hy, hz, gx, gy, gz, tops, mine, tops_all, mine_all, g_o, g_c, spread, pool, lhs, ghosts, edge_y, edge_z, regs, big, stage,
    ret, by_lane, by_box, box_lane, lane_box,
    in_sem, out_sem, so, ro, sc, rc, sr, rr, us, ur, hs, hr, ts, tr,
):
    ix, iy, iz = (lax.axis_index(a) for a in ("gx", "gy", "gz"))
    nx, ny, nz = (lax.axis_size(a) for a in ("gx", "gy", "gz"))
    me = ix * nz + iz
    peers = nx * nz
    load_fine = pltpu.make_async_copy(fine, fu, in_sem.at[0])
    load_fine.start()
    barrier = pltpu.get_barrier_semaphore()

    @pl.loop(1, peers)
    def _(s):
        x, z = plane_peer(s, 1)
        pl.semaphore_signal(barrier, inc=1, device_id=(x, iy, z), device_id_type=MESH)

    @pl.loop(1, ny)
    def _(s):
        pl.semaphore_signal(barrier, inc=1, device_id=(ix, lax.rem(iy + s, ny), iz), device_id_type=MESH)

    candidate_keys(owner, keys)
    exy[...] = onehot(keys[0:1, :], 512)
    pack(coarse, keys[1:2, :], exy, pay_o, cxy, cz, rxy)
    pl.semaphore_wait(barrier, peers - 1 + ny - 1)
    old_patch = start_patches(pay_o, arr_o, OUT_BLOCK, 30, so, ro)
    arr_o[block_of(me, OUT_BLOCK, 30), :] = pay_o[block_of(me, OUT_BLOCK, 30), :]

    best = coarse_changes(coarse, keys[2:3, :], chgf, chgl, pflux, pspeed, hy, hz)
    load_fine.wait()

    def fine_plane(p, best):
        u = [fu[f, :, plane_lanes(p)] for f in range(5)]
        return jnp.maximum(best, fastest_of(speeds(u)))

    fine_best = lax.fori_loop(0, BOX, fine_plane, jnp.zeros((16, 256), F32))
    mine[...] = jnp.maximum(best, fold(fine_best))

    def top(s):
        return remote(mine, tops.at[s], ts.at[s], tr.at[s], (ix, lax.rem(iy + s, ny), iz))

    @pl.loop(1, ny)
    def _(s):
        top(s).start()

    pack(chgf, keys[1:2, :], exy, pay_c, cxy, cz, rxy)

    @pl.loop(1, ny)
    def _(s):
        top(s).wait()

    best = mine[...]
    for s in range(1, ny):
        best = jnp.maximum(best, tops[s])
    mine_all[...] = jnp.full((1, 128), jnp.max(best), F32)

    def plane_top(s):
        x, z = plane_peer(s, 1)
        return remote(mine_all, tops_all.at[s], us.at[s], ur.at[s], (x, iy, z))

    @pl.loop(1, peers)
    def _(s):
        plane_top(s).start()

    new_patch = start_patches(pay_c, arr_c, OUT_BLOCK, 30, sc, rc)
    arr_c[block_of(me, OUT_BLOCK, 30), :] = pay_c[block_of(me, OUT_BLOCK, 30), :]
    up_x, down_x = lax.rem(ix + 1, nx), lax.rem(ix + nx - 1, nx)
    up_y, down_y = lax.rem(iy + 1, ny), lax.rem(iy + ny - 1, ny)
    up_z, down_z = lax.rem(iz + 1, nz), lax.rem(iz + nz - 1, nz)
    sides = [
        remote(coarse.at[:, coarse.shape[1] - 1], gx.at[0], hs.at[0], hr.at[0], (up_x, iy, iz)),
        remote(coarse.at[:, 0], gx.at[1], hs.at[1], hr.at[1], (down_x, iy, iz)),
        remote(hy.at[1], gy.at[0], hs.at[2], hr.at[2], (ix, up_y, iz)),
        remote(hy.at[0], gy.at[1], hs.at[3], hr.at[3], (ix, down_y, iz)),
        remote(hz.at[1], gz.at[0], hs.at[4], hr.at[4], (ix, iy, up_z)),
        remote(hz.at[0], gz.at[1], hs.at[5], hr.at[5], (ix, iy, down_z)),
    ]
    for side in sides:
        side.start()

    fine_inner(fu, chg, pflux, pspeed)
    fine_edges(fu, edge_y, edge_z)
    box_tables(corner, owner.shape[0], nz, box_lane, lane_box)
    spread[...] = spread_table()
    pool[...] = pool_table()

    @pl.loop(1, peers)
    def _(s):
        old_patch(s).wait_recv()

    gather_boxes(arr_o, box_lane, by_lane, g_o)
    ghosts[...] = fine_ghosts(g_o, spread, lhs)
    fine_outer(0, fu, chg, edge_y, edge_z, ghosts, regs)

    @pl.loop(1, peers)
    def _(s):
        plane_top(s).wait_recv()

    best = mine_all[...]
    for s in range(1, peers):
        best = jnp.maximum(best, tops_all[s])
    fastest = jnp.max(best)
    gmax[...] = jnp.full((8, 128), fastest, F32)
    courant = COURANT_NUMBER / fastest
    fine_update(courant, fu, chg, edge_y, edge_z)
    fine_inner(fu, chg, pflux, pspeed)
    fine_edges(fu, edge_y, edge_z)

    @pl.loop(1, peers)
    def _(s):
        new_patch(s).wait_recv()

    gather_boxes(arr_c, box_lane, by_lane, g_c)
    used = slice(0, 16 * OUT_ROWS)
    g_c[used, :] = 0.5 * (g_o[used, :] + (g_o[used, :] - courant * g_c[used, :]))
    ghosts[...] = fine_ghosts(g_c, spread, lhs)
    fine_outer(1, fu, chg, edge_y, edge_z, ghosts, regs)
    fine_update(courant, fu, chg, edge_y, edge_z)
    fine_results(fu, regs, pool, big, stage)
    for b in range(17):
        by_box[b] = stage[b * STAGE_ROWS : (b + 1) * STAGE_ROWS, :]
    for lane in range(64):
        at = lane % 32 * BACK_BLOCK + lane // 32 * BACK_ROWS
        ret[at : at + BACK_ROWS, :] = by_box[lane_box[lane]][:BACK_ROWS]
    back_patch = start_patches(ret, back, BACK_BLOCK, 70, sr, rr)
    own = pltpu.make_async_copy(
        ret.at[block_of(me, BACK_BLOCK, 70), :], back.at[block_of(me, BACK_BLOCK, 70), :], out_sem.at[0]
    )
    own.start()
    store_fine = pltpu.make_async_copy(fu, fine_new, out_sem.at[1])
    store_fine.start()
    for side in sides:
        side.wait()
    coarse_base(coarse, chgl, courant, gx, gy, gz, hy, hz)
    store_base = pltpu.make_async_copy(chgl, base, out_sem.at[2])
    store_base.start()
    own.wait()
    store_fine.wait()
    store_base.wait()

    @pl.loop(1, peers)
    def _(s):
        old_patch(s).wait_send()
        plane_top(s).wait_send()
        new_patch(s).wait_send()
        back_patch(s).wait()


def apply_kernel(base, keys, arr, gmax, fine, out, fine_out, body, boxes, lxy, lz, dxy, dz, sems):
    nz = base.shape[3]
    load = pltpu.make_async_copy(base, body, sems.at[5])
    load.start()
    load_fine = pltpu.make_async_copy(fine, boxes, sems.at[6])
    load_fine.start()
    courant = COURANT_NUMBER / jnp.max(gmax[...])
    left = lax.broadcasted_iota(jnp.int32, (16, 128), 1) < 64
    left64 = lax.broadcasted_iota(jnp.int32, (64, 128), 1) < 64

    def lanes_of(line):
        return jnp.concatenate(
            [arr[rows_of_lanes(part, BACK_BLOCK, BACK_ROWS, line), :] for part in range(8)], axis=0
        )

    flat = [(f, i) for f in range(5) for i in range(6)]
    for first in range(0, 30, 2):
        pair = flat[first : first + 2]
        turned = jnp.concatenate([lanes_of(f * 7 + i) for f, i in pair], axis=0).T
        for second in range(2):
            pieces = []
            for couple in range(4):
                even = jnp.concatenate(
                    [turned[a * 64 + couple * 16 : a * 64 + couple * 16 + 8] for a in range(2)], axis=0
                )
                odd = jnp.concatenate(
                    [turned[a * 64 + couple * 16 + 8 : a * 64 + couple * 16 + 16] for a in range(2)], axis=0
                )
                if second == 0:
                    pieces.append(jnp.where(left, even, pltpu.roll(odd, 64, 1)))
                else:
                    pieces.append(jnp.where(left, pltpu.roll(even, 64, 1), odd))
            put_split(lxy, (first + second) * 16, 480, jnp.concatenate(pieces, axis=1))
    for f in range(5):
        both = jnp.concatenate([lanes_of(f * 7 + 6), lanes_of(f * 7 + 6)], axis=0).T
        put_split(lz, f * 64, 320, jnp.where(left64, both[:64], both[64:]))
    dxy[...] = sum_split(dot_nn(lxy[...], onehot(keys[0:1, :], 512)))
    dz[...] = sum_split(dot_nn(lz[...], onehot(keys[1:2, :], 128)))
    spot = lax.broadcasted_iota(jnp.int32, (CORE, nz), 1) % BOX
    refined = jnp.broadcast_to(keys[2:3, :], (CORE, nz)) >= 0
    inside = refined & (spot >= SHIFT) & (spot < SHIFT + CORE)
    z_sign = courant * jnp.where(spot == SHIFT - 1, -1.0, jnp.where(spot == SHIFT + CORE, 1.0, 0.0))
    mid = slice(SHIFT, SHIFT + CORE)
    load_fine.wait()
    store_fine = pltpu.make_async_copy(boxes, fine_out, sems.at[7])
    store_fine.start()
    load.wait()
    stores = []
    for f in range(5):
        for side, x, sign in ((0, SHIFT - 1, -1.0), (1, SHIFT + CORE, 1.0)):
            at = (f * 6 + 4) * 16 + side * 8
            body[f, x, mid, :] = body[f, x, mid, :] + (sign * courant) * dxy[at : at + 8, :]
            at = (f * 6 + 5) * 16 + side * 8
            y = x
            for i in range(CORE):
                body[f, SHIFT + i, y : y + 1, :] = (
                    body[f, SHIFT + i, y : y + 1, :] + (sign * courant) * dxy[at + i : at + i + 1, :]
                )
        for i in range(CORE):
            fixed = body[f, SHIFT + i, mid, :] + z_sign * dz[f * 64 + i * 8 : f * 64 + i * 8 + 8, :]
            average = dxy[f * 96 + i * 8 : f * 96 + i * 8 + 8, :]
            body[f, SHIFT + i, mid, :] = jnp.where(inside, average, fixed)
        stores.append(pltpu.make_async_copy(body.at[f], out.at[f], sems.at[f]))
        stores[f].start()
    for store in stores:
        store.wait()
    store_fine.wait()


VMEM = pl.BlockSpec(memory_space=pltpu.VMEM)
SMEM = pl.BlockSpec(memory_space=pltpu.SMEM)
ANY = pl.BlockSpec(memory_space=pl.ANY)


def shape(*dims):
    return jax.ShapeDtypeStruct(dims, F32)


def step_call(owner, corner, coarse, fine):
    peers = lax.axis_size("gx") * lax.axis_size("gz")
    count_y = lax.axis_size("gy")
    _, nx, ny, nz = coarse.shape
    dma = pltpu.SemaphoreType.DMA

    def vmem(*dims, dtype=F32):
        return pltpu.VMEM(dims, dtype)

    return pl.pallas_call(
        step_kernel,
        out_shape=[
            shape(*coarse.shape),
            shape(*fine.shape),
            shape(33 * BACK_BLOCK, 128),
            shape(8, 128),
            jax.ShapeDtypeStruct((8, nz), jnp.int32),
        ],
        in_specs=[SMEM, SMEM, VMEM, ANY],
        out_specs=[ANY, ANY, ANY, VMEM, VMEM],
        scratch_shapes=[
            vmem(*fine.shape),
            vmem(*fine.shape),
            vmem(5, nx, ny, nz),
            vmem(5, nx, ny, nz),
            vmem(5, ny, nz),
            vmem(ny, nz),
            vmem(512, nz, dtype=BF16),
            vmem(480, nz, dtype=BF16),
            vmem(960, nz, dtype=BF16),
            vmem(160, 512),
            *[vmem(33 * OUT_BLOCK, 128)] * 4,
            vmem(2, 5, nx, nz),
            vmem(2, 5, ny, 128),
            vmem(2, 5, ny, nz),
            vmem(2, 5, nx, nz),
            vmem(2, 5, ny, 128),
            vmem(count_y, 8, 128),
            vmem(8, 128),
            vmem(peers, 1, 128),
            vmem(1, 128),
            vmem(16 * OUT_ROWS + 16, 128),
            vmem(16 * OUT_ROWS + 16, 128),
            vmem(128, 512, dtype=BF16),
            vmem(256, 128, dtype=BF16),
            vmem(720, 128, dtype=BF16),
            vmem(240, 512),
            vmem(5, 16, 512),
            vmem(5, 16, 512),
            vmem(240, 512),
            vmem(3360, 256, dtype=BF16),
            vmem(17 * STAGE_ROWS, 128),
            vmem(32 * BACK_BLOCK, 128),
            vmem(64, OUT_ROWS, 128),
            vmem(17, STAGE_ROWS, 128),
            pltpu.SMEM((16,), jnp.int32),
            pltpu.SMEM((64,), jnp.int32),
            dma((1,)),
            dma((3,)),
            *[dma((peers,))] * 8,
            dma((6,)),
            dma((6,)),
            dma((count_y,)),
            dma((count_y,)),
        ],
        compiler_params=pltpu.CompilerParams(
            collective_id=0, has_side_effects=True, vmem_limit_bytes=VMEM_LIMIT
        ),
        name="step",
    )(owner, corner, coarse, fine)


def apply_call(base, keys, arr, gmax, fine):
    nz = base.shape[3]
    return pl.pallas_call(
        apply_kernel,
        out_shape=[shape(*base.shape), shape(*fine.shape)],
        in_specs=[ANY, VMEM, VMEM, VMEM, ANY],
        out_specs=[ANY, ANY],
        scratch_shapes=[
            pltpu.VMEM(base.shape, F32),
            pltpu.VMEM(fine.shape, F32),
            pltpu.VMEM((1440, 512), BF16),
            pltpu.VMEM((960, 128), BF16),
            pltpu.VMEM((480, nz), F32),
            pltpu.VMEM((320, nz), F32),
            pltpu.SemaphoreType.DMA((8,)),
        ],
        compiler_params=pltpu.CompilerParams(vmem_limit_bytes=VMEM_LIMIT),
        name="reflux_apply",
    )(base, keys, arr, gmax, fine)


def local(coarse_old, fine_old, slot_owner, box_corner):
    base, fine_new, back, gmax, keys = step_call(
        slot_owner.reshape(-1), box_corner.T, coarse_old, fine_old.transpose(1, 0, 2)
    )
    coarse_new, fine_new = apply_call(base, keys, back, gmax, fine_new)
    return (coarse_new, fine_new.transpose(1, 0, 2))


def solution(mesh):
    in_specs = (
        P(None, "gx", "gy", "gz"),
        P(("gx", "gy", "gz"), None, None),
        P("gx", "gy", "gz"),
        P(("gx", "gy", "gz"), None),
    )
    out_specs = (P(None, "gx", "gy", "gz"), P(("gx", "gy", "gz"), None, None))
    return jax.shard_map(local, mesh=mesh, in_specs=in_specs, out_specs=out_specs, check_vma=False)
```
